32 devices in a mesh: seq: 4 (over y, x), ctx: 8 (over z, core).
Axes of the slice: x: 2, y: 2, z: 4, core: 2. Of those that a mesh axis runs over, the one named last changes fastest.
Arguments:
- tokens: bfloat16 [4096, 2304], P(('seq', 'ctx')), may hold values from -6 to 6
- w_query: bfloat16 [2304, 2048], P(('seq', 'ctx')), may hold values from -0.125 to 0.125
- w_key: bfloat16 [2304, 1024], P(('seq', 'ctx')), may hold values from -0.125 to 0.125
- w_value: bfloat16 [2304, 1024], P(('seq', 'ctx')), may hold values from -0.125 to 0.125
- w_output: bfloat16 [2048, 2304], P(('seq', 'ctx')), may hold values from -0.125 to 0.125
- w_gate: bfloat16 [2304, 9216], P('seq', 'ctx'), may hold values from -0.125 to 0.125
- w_up: bfloat16 [2304, 9216], P('seq', 'ctx'), may hold values from -0.125 to 0.125
- w_down: bfloat16 [9216, 2304], P('ctx', 'seq'), may hold values from -0.0625 to 0.0625
- first_gain: bfloat16 [2304], P(('seq', 'ctx')), may hold values from 0.25 to 1.75
- second_gain: bfloat16 [2304], P(('seq', 'ctx')), may hold values from 0.25 to 1.75
- third_gain: bfloat16 [2304], P(('seq', 'ctx')), may hold values from 0.25 to 1.75
- fourth_gain: bfloat16 [2304], P(('seq', 'ctx')), may hold values from 0.25 to 1.75
- block_pairs: int32 [8, 2], replicated, may hold values from 0 to 15, as said below
- cotangent: bfloat16 [4096, 2304], P(('seq', 'ctx')), may hold values from -6 to 6
Outputs:
- layer_out: bfloat16 [4096, 2304], P(('seq', 'ctx'))
- grad_tokens: bfloat16 [4096, 2304], P(('seq', 'ctx'))
- grad_query: float32 [2304, 2048], P(('seq', 'ctx'))
- grad_key: float32 [2304, 1024], P(('seq', 'ctx'))
- grad_value: float32 [2304, 1024], P(('seq', 'ctx'))
- grad_output: float32 [2048, 2304], P(('seq', 'ctx'))
- grad_gate: float32 [2304, 9216], P('seq', 'ctx')
- grad_up: float32 [2304, 9216], P('seq', 'ctx')
- grad_down: float32 [9216, 2304], P('ctx', 'seq')
- grad_first: float32 [2304], P(('seq', 'ctx'))
- grad_second: float32 [2304], P(('seq', 'ctx'))
- grad_third: float32 [2304], P(('seq', 'ctx'))
- grad_fourth: float32 [2304], P(('seq', 'ctx'))
The draws below stay inside these ranges and needn't reach their ends.
Inputs may be any that keep to these rules, and one draw needn't show every extreme that they name: `block_pairs`: row c holds a front block number below 8 and the back block number 2 * 8 - 1 minus it; every block number appears once in the array.
All inputs are finite; a program needn't handle non-finite values.
Results may differ from the reference program's by a relative error of at most 0.023.
Values may be sent and summed in bfloat16 or wider, within the bound.
No kernel may reach another device: no remote copies, remote signals or barrier semaphores. Data moves between devices by JAX's collectives and lax.ppermute only.
A program may use at most 320 MiB of HBM per device.

```python
import jax
import jax.numpy as jnp
from jax import lax

D = 2304
QUERY_HEAD_COUNT = 8
KV_HEADS = 4
HEAD_FEATURES = 256
FF = 9216
BLK = 64
SEQ_LEN = 1024
TOKENS = 4096
N_SEQ = 4
N_CTX = 8


def draw_block_pairs(key, part):
    order = jax.random.permutation(key, N_CTX).astype(jnp.int32)
    return jnp.stack([order, 2 * N_CTX - 1 - order], axis=1).astype(jnp.int32)


def steps_of(own_key, extent, pieces, low, largest):
    def one(position, blocks):
        steps = jax.random.uniform(jax.random.fold_in(jax.random.fold_in(own_key, 6), position), (blocks,), jnp.float32, low / len(pieces), largest / len(pieces))
        return jnp.repeat(jnp.exp(steps), extent[position] // blocks).reshape((-1,) + (1,) * (len(extent) - position - 1))

    factor_of = one(*pieces[0])
    for cut in pieces[1:]:
        factor_of = factor_of * one(*cut)
    return factor_of


def gaussian(key, extent, scale, limit, cuts=(), kind=jnp.bfloat16):
    drawn = scale * jax.random.normal(key, extent, jnp.float32)
    if cuts:
        drawn = drawn * steps_of(key, extent, cuts, -0.22, 0.18)
    return jnp.clip(drawn, -limit, limit).astype(kind)


def setup_inputs(seed: int = 0) -> dict:
    key_of = jax.random.split(jax.random.key(seed), 15)
    return {
        "tokens": gaussian(key_of[0], (TOKENS, D), 1.0, 6.0, ((0, 32),)),
        "w_query": gaussian(key_of[1], (D, QUERY_HEAD_COUNT * HEAD_FEATURES), D ** -0.5, 0.125, ((0, 32),)),
        "w_key": gaussian(key_of[2], (D, KV_HEADS * HEAD_FEATURES), D ** -0.5, 0.125, ((0, 32),)),
        "w_value": gaussian(key_of[3], (D, KV_HEADS * HEAD_FEATURES), D ** -0.5, 0.125, ((0, 32),)),
        "w_output": gaussian(key_of[4], (QUERY_HEAD_COUNT * HEAD_FEATURES, D), (QUERY_HEAD_COUNT * HEAD_FEATURES) ** -0.5, 0.125, ((0, 32),)),
        "w_gate": gaussian(key_of[5], (D, FF), D ** -0.5, 0.125, ((0, 4), (1, 8))),
        "w_up": gaussian(key_of[6], (D, FF), D ** -0.5, 0.125, ((0, 4), (1, 8))),
        "w_down": gaussian(key_of[7], (FF, D), FF ** -0.5, 0.0625, ((0, 8), (1, 4))),
        "first_gain": jnp.clip(1.0 + 0.15 * jax.random.normal(key_of[8], (D,), jnp.float32), 0.25, 1.75).astype(jnp.bfloat16),
        "second_gain": jnp.clip(1.0 + 0.15 * jax.random.normal(key_of[9], (D,), jnp.float32), 0.25, 1.75).astype(jnp.bfloat16),
        "third_gain": jnp.clip(1.0 + 0.15 * jax.random.normal(key_of[10], (D,), jnp.float32), 0.25, 1.75).astype(jnp.bfloat16),
        "fourth_gain": jnp.clip(1.0 + 0.15 * jax.random.normal(key_of[11], (D,), jnp.float32), 0.25, 1.75).astype(jnp.bfloat16),
        "block_pairs": draw_block_pairs(jax.random.fold_in(key_of[14], 71), 0),
        "cotangent": gaussian(key_of[13], (TOKENS, D), 1.0, 6.0, ((0, 32),)),
    }


epsilon = 1e-06
softcap = 50.0
theta = 10000.0
floor_value = -1e+30

@jax.custom_vjp
def low(v):
    return lax.optimization_barrier(v.astype(jnp.bfloat16)).astype(jnp.float32)

@jax.custom_vjp
def low_back(v):
    return v

def low_keep(v):
    return (low(v), None)

def low_pass(kept, grad):
    return (grad,)

def back_keep(v):
    return (v, None)

def back_low(kept, grad):
    return (low(grad),)
low.defvjp(low_keep, low_pass)
low_back.defvjp(back_keep, back_low)

def matmul(left, right):
    return jnp.dot(left, right, precision=lax.Precision.HIGHEST)

def rms_scale(signal, weight):
    return signal * lax.rsqrt(lax.optimization_barrier(jnp.mean(signal * signal, axis=-1, keepdims=True)) + epsilon) * weight

def rotate(signal, positions, head_width):
    row_count = signal.shape[0]
    head_count = signal.shape[1] // head_width
    half_width = head_width // 2
    frequency = theta ** (-2.0 * jnp.arange(half_width, dtype=jnp.float32) / head_width)
    angles = positions.astype(jnp.float32)[:, None] * frequency[None, :]
    cosine = jnp.cos(angles)[:, None, :]
    sine_wave = jnp.sin(angles)[:, None, :]
    shaped = signal.reshape(row_count, head_count, head_width)
    first_half = shaped[:, :, :half_width]
    second = shaped[:, :, half_width:]
    turned = jnp.concatenate([first_half * cosine - second * sine_wave, second * cosine + first_half * sine_wave], axis=2)
    return turned.reshape(row_count, head_count * head_width)

def block_forward(seq_rows, w_query, w_key, w_value, w_output, w_gate, w_up, w_down, first_gain, second_gain, third_gain, fourth_gain, positions):
    length_total = seq_rows.shape[0]
    group_size = QUERY_HEAD_COUNT // KV_HEADS
    normed = low(rms_scale(seq_rows, first_gain))
    query_proj = low_back(matmul(normed, w_query))
    key_proj = low_back(matmul(normed, w_key))
    value_proj = low_back(matmul(normed, w_value))
    rotary_queries = low(rotate(query_proj, positions, HEAD_FEATURES)).reshape(length_total, KV_HEADS, group_size, HEAD_FEATURES)
    rotary_keys = low(rotate(key_proj, positions, HEAD_FEATURES)).reshape(length_total, KV_HEADS, HEAD_FEATURES)
    lowered_values = low(value_proj).reshape(length_total, KV_HEADS, HEAD_FEATURES)
    unscaled_score = low_back(jnp.einsum('fwvi,hwi->wvfh', rotary_queries, rotary_keys, precision=lax.Precision.HIGHEST) * HEAD_FEATURES ** (-0.5))
    capped = softcap * jnp.tanh(unscaled_score / softcap)
    allowed = positions[None, :] <= positions[:, None]
    capped = jnp.where(allowed, capped, floor_value)
    lowered_probs = low(jax.nn.softmax(capped, axis=-1))
    full_mixture = jnp.einsum('xmbe,exk->bxmk', lowered_probs, lowered_values, precision=lax.Precision.HIGHEST).reshape(length_total, QUERY_HEAD_COUNT * HEAD_FEATURES)
    mixed_low = low(low_back(full_mixture))
    branch = low_back(matmul(mixed_low, w_output))
    residual = seq_rows + rms_scale(branch, second_gain)
    feed_input = low(rms_scale(residual, third_gain))
    gate_pre = low_back(matmul(feed_input, w_gate))
    up_pre = low_back(matmul(feed_input, w_up))
    hidden = low(jax.nn.gelu(gate_pre, approximate=True) * up_pre)
    feed_out = low_back(matmul(hidden, w_down))
    return residual + rms_scale(feed_out, fourth_gain)

def reference(tokens, w_query, w_key, w_value, w_output, w_gate, w_up, w_down, first_gain, second_gain, third_gain, fourth_gain, block_pairs, cotangent):
    offsets = jnp.arange(BLK, dtype=jnp.int32)
    positions = (block_pairs[:, :, None] * BLK + offsets[None, None, :]).reshape(SEQ_LEN).astype(jnp.int32)
    floats = tuple((entry.astype(jnp.float32) for entry in (tokens, w_query, w_key, w_value, w_output, w_gate, w_up, w_down, first_gain, second_gain, third_gain, fourth_gain)))

    def forward(token_rows, query_w, key_w, value_w, output_w, gate_w, up_w, down_w, gain_one, gain_two, gain_three, gain_four):

        def one_sequence(seq_rows):
            return block_forward(seq_rows, query_w, key_w, value_w, output_w, gate_w, up_w, down_w, gain_one, gain_two, gain_three, gain_four, positions)
        stacked = token_rows.reshape(N_SEQ, SEQ_LEN, D)
        return lax.map(jax.checkpoint(one_sequence), stacked).reshape(TOKENS, D)
    outcome, pullback = jax.vjp(forward, *floats)
    gradients = pullback(cotangent.astype(jnp.float32))
    return (outcome.astype(jnp.bfloat16), gradients[0].astype(jnp.bfloat16), gradients[1], gradients[2], gradients[3], gradients[4], gradients[5], gradients[6], gradients[7], gradients[8], gradients[9], gradients[10], gradients[11])
```

```python
from functools import partial

import jax
import jax.numpy as jnp
from jax import lax
from jax.sharding import PartitionSpec as P

QUERY_HEAD_COUNT = 8
KV_HEADS = 4
HEAD_FEATURES = 256


epsilon = 1e-06
softcap = 50.0
theta = 10000.0
floor_value = -1e30


def rms_scale(signal, weight):
    return signal * lax.rsqrt(jnp.mean(signal * signal, axis=-1, keepdims=True) + epsilon) * weight


def norm_back(signal, weight, upstream):
    outcome, pullback = jax.vjp(rms_scale, signal, weight)
    return pullback(upstream)


def gate_mix(gate_pre, up_pre):
    return jax.nn.gelu(gate_pre, approximate=True) * up_pre


def rotate(signal, positions, head_width):
    row_count = signal.shape[0]
    head_count = signal.shape[1] // head_width
    half_width = head_width // 2
    frequency = theta ** (-2.0 * jnp.arange(half_width, dtype=jnp.float32) / head_width)
    angles = positions.astype(jnp.float32)[:, None] * frequency[None, :]
    cosine = jnp.cos(angles)[:, None, :]
    sine_wave = jnp.sin(angles)[:, None, :]
    shaped = signal.reshape(row_count, head_count, head_width)
    first_half = shaped[:, :, :half_width]
    second = shaped[:, :, half_width:]
    turned = jnp.concatenate(
        [first_half * cosine - second * sine_wave, second * cosine + first_half * sine_wave], axis=2
    )
    return turned.reshape(row_count, head_count * head_width)


def block_scores(head_queries, key_all, key_pos, query_pos, block_rows, score_scale):
    block_keys = key_all.reshape(block_rows, KV_HEADS, HEAD_FEATURES)
    allowed = key_pos[None, :] <= query_pos[:, None]
    unscaled_score = (
        jnp.einsum("fwvi,hwi->wvfh", head_queries, block_keys, preferred_element_type=jnp.float32)
        * score_scale
    )
    bent_score = jnp.tanh(unscaled_score / softcap)
    capped = jnp.where(allowed, softcap * bent_score, floor_value)
    return (block_keys, allowed, bent_score, capped)


def attend(head_queries, key_all, value_all, query_pos, key_pos, score_scale):
    length_total = key_all.shape[0]
    block_count = max(1, length_total // 2048)
    block_rows = length_total // block_count
    row_count = head_queries.shape[0]
    group_size = head_queries.shape[2]

    def total_step(block_index, carried):
        running_max, running_sum = carried
        block_keys, allowed, bent_score, capped = block_scores(
            head_queries, key_all, key_pos, query_pos, block_rows, score_scale
        )
        new_max = jnp.maximum(running_max, jnp.max(capped, axis=-1))
        added = jnp.sum(jnp.where(allowed, jnp.exp(capped - new_max[..., None]), 0.0), axis=-1)
        return (new_max, running_sum * jnp.exp(running_max - new_max) + added)

    start_max = jnp.full((KV_HEADS, group_size, row_count), floor_value, jnp.float32)
    start_sum = jnp.zeros((KV_HEADS, group_size, row_count), jnp.float32)
    running_max, running_sum = lax.fori_loop(0, block_count, total_step, (start_max, start_sum))
    log_total = running_max + jnp.log(running_sum)

    def mix_step(block_index, carried):
        accum, rest_acc = carried
        block_keys, allowed, bent_score, capped = block_scores(
            head_queries, key_all, key_pos, query_pos, block_rows, score_scale
        )
        block_values = value_all.reshape(block_rows, KV_HEADS, HEAD_FEATURES)
        prob_full = jnp.where(allowed, jnp.exp(capped - log_total[..., None]), 0.0)
        lowered_probs = prob_full.astype(jnp.bfloat16)
        remaining_probs = (prob_full - lowered_probs.astype(jnp.float32)).astype(jnp.bfloat16)
        accum = accum + jnp.einsum(
            "xmbe,exk->bxmk", lowered_probs, block_values, preferred_element_type=jnp.float32
        )
        rest_acc = rest_acc + jnp.einsum(
            "xmbe,exk->bxmk", remaining_probs, block_values, preferred_element_type=jnp.float32
        )
        return (accum, rest_acc)

    start_mix = jnp.zeros((row_count, KV_HEADS, group_size, HEAD_FEATURES), jnp.float32)
    full_mixture, rest_acc = lax.fori_loop(0, block_count, mix_step, (start_mix, start_mix))
    exact_mixture = full_mixture + rest_acc
    return (
        log_total,
        full_mixture.reshape(row_count, QUERY_HEAD_COUNT * HEAD_FEATURES),
        exact_mixture,
    )


def attend_back(
    head_queries,
    key_all,
    value_all,
    query_pos,
    key_pos,
    score_scale,
    log_total,
    exact_mixture,
    mixed_grad,
):
    length_total = key_all.shape[0]
    block_count = max(1, length_total // 2048)
    block_rows = length_total // block_count
    row_count = head_queries.shape[0]
    group_size = head_queries.shape[2]
    head_gradient = mixed_grad.reshape(row_count, KV_HEADS, group_size, HEAD_FEATURES)
    row_difference = jnp.einsum("ozlq,ozlq->zlo", head_gradient.astype(jnp.float32), exact_mixture)

    def grad_step(block_index, carried):
        query_acc, key_acc, value_acc = carried
        block_keys, allowed, bent_score, capped = block_scores(
            head_queries, key_all, key_pos, query_pos, block_rows, score_scale
        )
        block_values = value_all.reshape(block_rows, KV_HEADS, HEAD_FEATURES)
        prob_full = jnp.where(allowed, jnp.exp(capped - log_total[..., None]), 0.0)
        lowered_probs = prob_full.astype(jnp.bfloat16)
        value_part = jnp.einsum(
            "zwcv,czwy->vzy", lowered_probs, head_gradient, preferred_element_type=jnp.float32
        )
        prob_grad = jnp.einsum(
            "fwvi,hwi->wvfh", head_gradient, block_values, preferred_element_type=jnp.float32
        )
        lowered_logits = (
            prob_full * (prob_grad - row_difference[..., None]) * (1.0 - bent_score * bent_score)
        ).astype(jnp.bfloat16)
        query_acc = (
            query_acc
            + jnp.einsum(
                "xmbe,exk->bxmk", lowered_logits, block_keys, preferred_element_type=jnp.float32
            )
            * score_scale
        )
        key_part = (
            jnp.einsum(
                "zwcv,czwy->vzy", lowered_logits, head_queries, preferred_element_type=jnp.float32
            )
            * score_scale
        )
        key_acc = key_part.reshape(block_rows, KV_HEADS * HEAD_FEATURES)
        value_acc = value_part.reshape(block_rows, KV_HEADS * HEAD_FEATURES)
        return (query_acc, key_acc, value_acc)

    start = (
        jnp.zeros((row_count, KV_HEADS, group_size, HEAD_FEATURES), jnp.float32),
        jnp.zeros((length_total, KV_HEADS * HEAD_FEATURES), jnp.float32),
        jnp.zeros((length_total, KV_HEADS * HEAD_FEATURES), jnp.float32),
    )
    query_acc, key_acc, value_acc = lax.fori_loop(0, block_count, grad_step, start)
    return (query_acc.reshape(row_count, QUERY_HEAD_COUNT * HEAD_FEATURES), key_acc, value_acc)


def context_body(
    tokens,
    w_query,
    w_key,
    w_value,
    w_output,
    w_gate,
    w_up,
    w_down,
    first_gain,
    second_gain,
    third_gain,
    fourth_gain,
    block_pairs,
    cotangent,
):
    query_full, key_full, value_full, output_full, gain_one, gain_two, gain_three, gain_four = (
        lax.all_gather(w_query, ("seq", "ctx"), axis=0, tiled=True),
        lax.all_gather(w_key, ("seq", "ctx"), axis=0, tiled=True),
        lax.all_gather(w_value, ("seq", "ctx"), axis=0, tiled=True),
        lax.all_gather(w_output, ("seq", "ctx"), axis=0, tiled=True),
        lax.all_gather(first_gain, ("seq", "ctx"), axis=0, tiled=True),
        lax.all_gather(second_gain, ("seq", "ctx"), axis=0, tiled=True),
        lax.all_gather(third_gain, ("seq", "ctx"), axis=0, tiled=True),
        lax.all_gather(fourth_gain, ("seq", "ctx"), axis=0, tiled=True),
    )
    gain_one = gain_one.astype(jnp.float32)
    gain_two = gain_two.astype(jnp.float32)
    gain_three = gain_three.astype(jnp.float32)
    gain_four = gain_four.astype(jnp.float32)
    row_count = tokens.shape[0]
    block_size = row_count // 2
    group_size = QUERY_HEAD_COUNT // KV_HEADS
    score_scale = HEAD_FEATURES ** (-0.5)
    own_pair = lax.dynamic_index_in_dim(block_pairs, lax.axis_index("ctx"), 0, keepdims=False)
    offsets = jnp.arange(block_size, dtype=jnp.int32)
    query_pos = jnp.concatenate(
        [own_pair[0] * block_size + offsets, own_pair[1] * block_size + offsets]
    )
    key_pos = (block_pairs[:, :, None] * block_size + offsets[None, None, :]).reshape(-1)
    residual_in = tokens.astype(jnp.float32)
    normed = rms_scale(residual_in, gain_one).astype(jnp.bfloat16)
    query_proj = jnp.dot(normed, query_full, preferred_element_type=jnp.float32)
    key_proj = jnp.dot(normed, key_full, preferred_element_type=jnp.float32)
    value_proj = jnp.dot(normed, value_full, preferred_element_type=jnp.float32)
    query_low = rotate(query_proj, query_pos, HEAD_FEATURES).astype(jnp.bfloat16)
    key_low = rotate(key_proj, query_pos, HEAD_FEATURES).astype(jnp.bfloat16)
    lowered_values = value_proj.astype(jnp.bfloat16)
    key_all, value_all = (
        lax.all_gather(key_low, "ctx", axis=0, tiled=True),
        lax.all_gather(lowered_values, "ctx", axis=0, tiled=True),
    )
    head_queries = query_low.reshape(row_count, KV_HEADS, group_size, HEAD_FEATURES)
    log_total, full_mixture, exact_mixture = attend(
        head_queries, key_all, value_all, query_pos, key_pos, score_scale
    )
    mixed_low = full_mixture.astype(jnp.bfloat16)
    branch = jnp.dot(mixed_low, output_full, preferred_element_type=jnp.float32)
    residual = residual_in + rms_scale(branch, gain_two)
    feed_input = rms_scale(residual, gain_three).astype(jnp.bfloat16)
    part_gate, part_up, part_down = (
        lax.all_gather(w_gate, "seq", axis=0, tiled=True),
        lax.all_gather(w_up, "seq", axis=0, tiled=True),
        lax.all_gather(w_down, "seq", axis=1, tiled=True),
    )
    feed_all = lax.all_gather(feed_input, "ctx", axis=0, tiled=True)
    gate_pre = jnp.dot(feed_all, part_gate, preferred_element_type=jnp.float32)
    up_pre = jnp.dot(feed_all, part_up, preferred_element_type=jnp.float32)
    hidden = gate_mix(gate_pre, up_pre).astype(jnp.bfloat16)
    feed_out = lax.psum_scatter(
        jnp.dot(hidden, part_down, preferred_element_type=jnp.float32).astype(jnp.bfloat16),
        "ctx",
        scatter_dimension=0,
        tiled=True,
    ).astype(jnp.float32)
    layer_out = (residual + rms_scale(feed_out, gain_four)).astype(jnp.bfloat16)
    upstream = cotangent.astype(jnp.float32)
    feed_grad, fourth_term = norm_back(feed_out, gain_four, upstream)
    feed_low = feed_grad.astype(jnp.bfloat16)
    cotangent_all = lax.all_gather(feed_low, "ctx", axis=0, tiled=True)
    hidden_grad = jnp.einsum(
        "td,fd->tf", cotangent_all, part_down, preferred_element_type=jnp.float32
    )
    outcome, mix_pull = jax.vjp(gate_mix, gate_pre, up_pre)
    gate_grad, up_grad = mix_pull(hidden_grad)
    gate_low = gate_grad.astype(jnp.bfloat16)
    up_low = up_grad.astype(jnp.bfloat16)
    input_part = jnp.einsum(
        "tf,df->td", gate_low, part_gate, preferred_element_type=jnp.float32
    ) + jnp.einsum("tf,df->td", up_low, part_up, preferred_element_type=jnp.float32)
    feed_input_grad = lax.psum_scatter(
        input_part.astype(jnp.bfloat16), "ctx", scatter_dimension=0, tiled=True
    ).astype(jnp.float32)
    gate_term = jnp.einsum("tf,td->fd", gate_low, feed_all, preferred_element_type=jnp.float32)
    up_term = jnp.einsum("tf,td->fd", up_low, feed_all, preferred_element_type=jnp.float32)
    down_term = jnp.einsum("tf,td->fd", hidden, cotangent_all, preferred_element_type=jnp.float32)
    gate_sum, up_sum, down_sum = (
        lax.psum_scatter(
            gate_term.astype(jnp.bfloat16), "seq", scatter_dimension=1, tiled=True
        ).astype(jnp.float32),
        lax.psum_scatter(
            up_term.astype(jnp.bfloat16), "seq", scatter_dimension=1, tiled=True
        ).astype(jnp.float32),
        lax.psum_scatter(
            down_term.astype(jnp.bfloat16), "seq", scatter_dimension=1, tiled=True
        ).astype(jnp.float32),
    )
    middle_grad, third_term = norm_back(residual, gain_three, feed_input_grad)
    residual_grad = upstream + middle_grad
    branch_grad, second_term = norm_back(branch, gain_two, residual_grad)
    branch_low = branch_grad.astype(jnp.bfloat16)
    output_term = jnp.einsum("th,td->hd", mixed_low, branch_low, preferred_element_type=jnp.float32)
    mixed_grad = jnp.einsum(
        "td,hd->th", branch_low, output_full, preferred_element_type=jnp.float32
    ).astype(jnp.bfloat16)
    query_sum, key_acc, value_acc = attend_back(
        head_queries,
        key_all,
        value_all,
        query_pos,
        key_pos,
        score_scale,
        log_total,
        exact_mixture,
        mixed_grad,
    )
    key_own, value_own = (
        lax.psum_scatter(
            key_acc.astype(jnp.bfloat16), "ctx", scatter_dimension=0, tiled=True
        ).astype(jnp.float32),
        lax.psum_scatter(
            value_acc.astype(jnp.bfloat16), "ctx", scatter_dimension=0, tiled=True
        ).astype(jnp.float32),
    )
    query_grad = rotate(query_sum, -query_pos, HEAD_FEATURES).astype(jnp.bfloat16)
    key_grad = rotate(key_own, -query_pos, HEAD_FEATURES).astype(jnp.bfloat16)
    value_grad = value_own.astype(jnp.bfloat16)
    normed_grad = jnp.einsum(
        "th,dh->td", query_grad, query_full, preferred_element_type=jnp.float32
    )
    normed_grad = normed_grad + jnp.einsum(
        "th,dh->td", key_grad, key_full, preferred_element_type=jnp.float32
    )
    normed_grad = normed_grad + jnp.einsum(
        "th,dh->td", value_grad, value_full, preferred_element_type=jnp.float32
    )
    query_term = jnp.einsum("td,th->dh", normed, query_grad, preferred_element_type=jnp.float32)
    key_term = jnp.einsum("td,th->dh", normed, key_grad, preferred_element_type=jnp.float32)
    value_term = jnp.einsum("td,th->dh", normed, value_grad, preferred_element_type=jnp.float32)
    input_grad, first_term = norm_back(residual_in, gain_one, normed_grad)
    grad_tokens = (residual_grad + input_grad).astype(jnp.bfloat16)
    grad_sums = (
        lax.psum_scatter(query_term, ("seq", "ctx"), scatter_dimension=0, tiled=True),
        lax.psum_scatter(key_term, ("seq", "ctx"), scatter_dimension=0, tiled=True),
        lax.psum_scatter(value_term, ("seq", "ctx"), scatter_dimension=0, tiled=True),
        lax.psum_scatter(output_term, ("seq", "ctx"), scatter_dimension=0, tiled=True),
        lax.psum_scatter(first_term, ("seq", "ctx"), scatter_dimension=0, tiled=True),
        lax.psum_scatter(second_term, ("seq", "ctx"), scatter_dimension=0, tiled=True),
        lax.psum_scatter(third_term, ("seq", "ctx"), scatter_dimension=0, tiled=True),
        lax.psum_scatter(fourth_term, ("seq", "ctx"), scatter_dimension=0, tiled=True),
    )
    return (
        layer_out,
        grad_tokens,
        grad_sums[0],
        grad_sums[1],
        grad_sums[2],
        grad_sums[3],
        gate_sum.T,
        up_sum.T,
        down_sum,
        grad_sums[4],
        grad_sums[5],
        grad_sums[6],
        grad_sums[7],
    )


CORES = 2
GELU_IN = 0.7978845608
GELU_CUBE = 0.044715


def rms_parts(signal):
    scale = lax.rsqrt(jnp.mean(signal * signal, axis=-1, keepdims=True) + epsilon)
    return scale, signal * scale


def rms_back(scale, unit, weight, upstream):
    weighted = upstream * weight
    mean = jnp.mean(weighted * unit, axis=-1, keepdims=True)
    return scale * (weighted - unit * mean), jnp.sum(upstream * unit, axis=0)


def dot_nn(left, right):
    return jnp.dot(left, right, preferred_element_type=jnp.float32)


def dot_nt(left, right):
    return jnp.einsum("ab,cb->ac", left, right, preferred_element_type=jnp.float32)


def dot_tn(left, right):
    return jnp.einsum("ab,ac->bc", left, right, preferred_element_type=jnp.float32)


class Moves:
    def __init__(self, n_seq, n_ctx):
        self.n_seq, self.n_ctx = n_seq, n_ctx
        self.line = n_ctx // CORES
        self.seq = lax.axis_index("seq")
        ctx = lax.axis_index("ctx")
        self.plane = ctx // CORES
        self.core = ctx % CORES

    def _send(self, value, move):
        pairs = []
        for s in range(self.n_seq):
            for c in range(self.n_ctx):
                t = move(s, c // CORES, c % CORES)
                pairs.append((s * self.n_ctx + c, t[0] * self.n_ctx + t[1] * CORES + t[2]))
        return lax.ppermute(value, ("seq", "ctx"), pairs)

    def across(self, value, mask):
        return self._send(value, lambda s, z, k: (s ^ mask, z, k))

    def along(self, value, step):
        return self._send(value, lambda s, z, k: (s, (z + step) % self.line, k))

    def swap(self, value):
        return self._send(value, lambda s, z, k: (s, z, k ^ 1))

    def gather_seq(self, block):
        half = block.shape[0] // 2
        by_x = self.across(block, 1)
        by_y = self.across(block, 2)
        far_low = self.across(by_x[:half], 2)
        far_high = self.across(by_y[half:], 1)
        out = jnp.zeros((self.n_seq,) + block.shape, block.dtype)
        out = lax.dynamic_update_index_in_dim(out, block, self.seq, 0)
        out = lax.dynamic_update_index_in_dim(out, by_x, self.seq ^ 1, 0)
        out = lax.dynamic_update_index_in_dim(out, by_y, self.seq ^ 2, 0)
        far = jnp.concatenate([far_low, far_high], axis=0)
        return lax.dynamic_update_index_in_dim(out, far, self.seq ^ 3, 0)

    def scatter_seq(self, parts):
        half = parts.shape[1] // 2
        take = lambda mask, low: lax.dynamic_index_in_dim(parts, self.seq ^ mask, 0, False)[
            slice(0, half) if low else slice(half, None)
        ]
        low_in = self.across(jnp.stack([take(1, True), take(3, True)]), 1)
        high_in = self.across(jnp.stack([take(2, False), take(3, False)]), 2)
        wide = lambda v: v.astype(jnp.float32)
        low_on = (wide(take(2, True)) + wide(low_in[1])).astype(jnp.bfloat16)
        high_on = (wide(take(1, False)) + wide(high_in[1])).astype(jnp.bfloat16)
        low_far = self.across(low_on, 2)
        high_far = self.across(high_on, 1)
        low = wide(take(0, True)) + wide(low_in[0]) + wide(low_far)
        high = wide(take(0, False)) + wide(high_in[0]) + wide(high_far)
        return jnp.concatenate([low, high], axis=0)

    def exchange_line(self, blocks):
        out = jnp.zeros_like(blocks)
        own = lax.dynamic_index_in_dim(blocks, self.plane, 0, False)
        out = lax.dynamic_update_index_in_dim(out, own, self.plane, 0)
        for step in range(1, self.line):
            sent = lax.dynamic_index_in_dim(blocks, (self.plane + step) % self.line, 0, False)
            got = self.along(sent, step)
            out = lax.dynamic_update_index_in_dim(out, got, (self.plane - step) % self.line, 0)
        return out

    def exchange_cores(self, blocks):
        own = lax.dynamic_index_in_dim(blocks, self.core, 0, False)
        got = self.swap(lax.dynamic_index_in_dim(blocks, 1 - self.core, 0, False))
        first = self.core == 0
        return jnp.stack([jnp.where(first, own, got), jnp.where(first, got, own)])


def head_body(
    tokens,
    w_query,
    w_key,
    w_value,
    w_output,
    w_gate,
    w_up,
    w_down,
    first_gain,
    second_gain,
    third_gain,
    fourth_gain,
    block_pairs,
    cotangent,
    n_seq,
    n_ctx,
):
    moves = Moves(n_seq, n_ctx)
    line = moves.line
    core_zero = moves.core == 0
    width = tokens.shape[1]
    row_count = tokens.shape[0]
    length_total = row_count * n_ctx
    feat_rows = w_query.shape[0]
    out_rows = w_output.shape[0]
    feats = HEAD_FEATURES
    score_scale = feats ** (-0.5)
    pad = 128
    block_size = row_count // 2
    offsets = jnp.arange(block_size, dtype=jnp.int32)
    pos = (block_pairs[:, :, None] * block_size + offsets[None, None, :]).reshape(-1)

    tokens_all = lax.all_gather(tokens, "ctx", axis=0, tiled=True)
    gains_in = jnp.stack([first_gain, second_gain, third_gain, fourth_gain], axis=1)
    gains_in = jnp.pad(gains_in, ((0, 0), (0, pad - 4)))
    by_head = jnp.concatenate(
        [
            w_query.reshape(feat_rows, line, CORES, feats),
            jnp.stack(
                [
                    w_key.reshape(feat_rows, line, feats),
                    w_value.reshape(feat_rows, line, feats),
                ],
                axis=2,
            ),
            jnp.broadcast_to(gains_in[:, None, None, :], (feat_rows, line, CORES, pad)),
        ],
        axis=3,
    ).transpose(2, 1, 0, 3)
    by_plane = moves.exchange_cores(by_head).transpose(1, 0, 2, 3)
    own_columns = moves.exchange_line(by_plane).reshape(n_ctx * feat_rows, 2 * feats + pad)
    columns = moves.gather_seq(own_columns).reshape(width, 2 * feats + pad)
    w_qkv = columns[:, : 2 * feats]
    gains = columns[:, 2 * feats : 2 * feats + 8].astype(jnp.float32).T
    gain_one, gain_two, gain_three, gain_four = gains[0], gains[1], gains[2], gains[3]

    out_seq = jnp.zeros((n_seq,) + w_output.shape, w_output.dtype)
    out_seq = lax.dynamic_update_index_in_dim(out_seq, w_output, moves.seq, 0)
    for mask in (1, 2, 3):
        out_seq = lax.dynamic_update_index_in_dim(
            out_seq, moves.across(w_output, mask), moves.seq ^ mask, 0
        )
    out_line = moves.exchange_line(out_seq).reshape(CORES, CORES, out_rows, width)
    w_out = moves.exchange_cores(out_line).transpose(1, 0, 2, 3).reshape(feats, width)

    gate_w = moves.gather_seq(w_gate).reshape(width, -1)
    up_w = moves.gather_seq(w_up).reshape(width, -1)
    down_w = moves.gather_seq(w_down.T).reshape(width, -1)

    wide_all = tokens_all.astype(jnp.float32)
    normed = (rms_parts(wide_all)[1] * gain_one).astype(jnp.bfloat16)
    qkv = dot_nn(normed, w_qkv)
    query_low = rotate(qkv[:, :feats], pos, feats).astype(jnp.bfloat16)
    pair = qkv[:, feats:]
    pair_low = jnp.where(core_zero, rotate(pair, pos, feats), pair).astype(jnp.bfloat16)
    pair_other = moves.swap(pair_low)
    key_low = jnp.where(core_zero, pair_low, pair_other)
    value_low = jnp.where(core_zero, pair_other, pair_low)
    allowed = pos[None, :] <= pos[:, None]
    bent = jnp.tanh(dot_nt(query_low, key_low) * (score_scale / softcap))
    weight = jnp.where(allowed, jnp.exp(softcap * bent), 0.0)
    probs = weight / jnp.sum(weight, axis=-1, keepdims=True)
    prob_low = probs.astype(jnp.bfloat16)
    mixed_low = dot_nn(prob_low, value_low).astype(jnp.bfloat16)
    branch = lax.psum_scatter(
        dot_nn(mixed_low, w_out).astype(jnp.bfloat16), "ctx", scatter_dimension=0, tiled=True
    ).astype(jnp.float32)

    residual_in = tokens.astype(jnp.float32)
    scale_two, unit_two = rms_parts(branch)
    residual = residual_in + unit_two * gain_two
    scale_three, unit_three = rms_parts(residual)
    feed_input = (unit_three * gain_three).astype(jnp.bfloat16)
    feed_all = lax.all_gather(feed_input, "ctx", axis=0, tiled=True)
    gate_pre = dot_nn(feed_all, gate_w)
    up_pre = dot_nn(feed_all, up_w)
    bend = jnp.tanh(GELU_IN * (gate_pre + GELU_CUBE * gate_pre * gate_pre * gate_pre))
    gelu = 0.5 * gate_pre * (1.0 + bend)
    hidden = (gelu * up_pre).astype(jnp.bfloat16)
    feed_out = lax.psum_scatter(
        dot_nt(hidden, down_w).astype(jnp.bfloat16), "ctx", scatter_dimension=0, tiled=True
    ).astype(jnp.float32)
    scale_four, unit_four = rms_parts(feed_out)
    layer_out = (residual + unit_four * gain_four).astype(jnp.bfloat16)

    upstream = cotangent.astype(jnp.float32)
    feed_grad, fourth_term = rms_back(scale_four, unit_four, gain_four, upstream)
    feed_low = feed_grad.astype(jnp.bfloat16)
    grad_all = lax.all_gather(feed_low, "ctx", axis=0, tiled=True)
    hidden_grad = dot_nn(grad_all, down_w)
    slope = 0.5 * (1.0 + bend) + 0.5 * gate_pre * (1.0 - bend * bend) * GELU_IN * (
        1.0 + 3.0 * GELU_CUBE * gate_pre * gate_pre
    )
    gate_low = (hidden_grad * up_pre * slope).astype(jnp.bfloat16)
    up_low = (hidden_grad * gelu).astype(jnp.bfloat16)
    input_part = dot_nt(gate_low, gate_w) + dot_nt(up_low, up_w)
    feed_input_grad = lax.psum_scatter(
        input_part.astype(jnp.bfloat16), "ctx", scatter_dimension=0, tiled=True
    ).astype(jnp.float32)
    shape = (n_seq, width // n_seq, gate_low.shape[1])
    down_sum = moves.scatter_seq(dot_tn(grad_all, hidden).astype(jnp.bfloat16).reshape(shape)).T
    gate_sum = moves.scatter_seq(dot_tn(feed_all, gate_low).astype(jnp.bfloat16).reshape(shape))
    up_sum = moves.scatter_seq(dot_tn(feed_all, up_low).astype(jnp.bfloat16).reshape(shape))

    middle_grad, third_term = rms_back(scale_three, unit_three, gain_three, feed_input_grad)
    residual_grad = upstream + middle_grad
    branch_grad, second_term = rms_back(scale_two, unit_two, gain_two, residual_grad)
    branch_low = branch_grad.astype(jnp.bfloat16)

    branch_all = lax.all_gather(branch_low, "ctx", axis=0, tiled=True)
    output_term = dot_tn(mixed_low, branch_all).astype(jnp.bfloat16)
    mixed_grad = dot_nt(branch_all, w_out).astype(jnp.bfloat16)
    value_part = dot_tn(prob_low, mixed_grad)
    prob_grad = dot_nt(mixed_grad, value_low)
    delta = jnp.sum(probs * prob_grad, axis=-1, keepdims=True)
    raw_low = (probs * (prob_grad - delta) * (1.0 - bent * bent)).astype(jnp.bfloat16)
    query_sum = dot_nn(raw_low, key_low) * score_scale
    key_part = dot_tn(raw_low, query_low) * score_scale
    pair_sum = jnp.where(core_zero, key_part, value_part) + moves.swap(
        jnp.where(core_zero, value_part, key_part)
    )
    query_grad = rotate(query_sum, -pos, feats)
    pair_grad = jnp.where(core_zero, rotate(pair_sum, -pos, feats), pair_sum)
    qkv_grad = jnp.concatenate([query_grad, pair_grad], axis=1).astype(jnp.bfloat16)
    normed_grad = lax.psum_scatter(
        dot_nt(qkv_grad, w_qkv).astype(jnp.bfloat16), "ctx", scatter_dimension=0, tiled=True
    ).astype(jnp.float32)
    scale_one, unit_one = rms_parts(residual_in)
    input_grad, _ = rms_back(scale_one, unit_one, gain_one, normed_grad)
    grad_tokens = (residual_grad + input_grad).astype(jnp.bfloat16)

    terms = jnp.stack([second_term, third_term, fourth_term])
    terms = jnp.pad(terms, ((0, pad - 3), (0, 0))).T
    qkv_term = jnp.concatenate([dot_tn(normed, qkv_grad), terms], axis=1).astype(jnp.bfloat16)
    own_term = moves.scatter_seq(qkv_term.reshape(n_seq, width // n_seq, -1)).astype(jnp.bfloat16)
    own_term = own_term.reshape(line, CORES, feat_rows, 2 * feats + pad)
    own_term = moves.exchange_line(own_term).transpose(1, 0, 2, 3)
    own_term = moves.exchange_cores(own_term).transpose(2, 1, 0, 3).astype(jnp.float32)
    grad_query = own_term[..., :feats].reshape(feat_rows, -1)
    grad_key = own_term[:, :, 0, feats : 2 * feats].reshape(feat_rows, -1)
    grad_value = own_term[:, :, 1, feats : 2 * feats].reshape(feat_rows, -1)
    grad_gains = jnp.sum(own_term[..., 2 * feats : 2 * feats + 3], axis=(1, 2))
    grad_first = (
        jnp.sum(w_query.astype(jnp.float32) * grad_query, axis=1)
        + jnp.sum(w_key.astype(jnp.float32) * grad_key, axis=1)
        + jnp.sum(w_value.astype(jnp.float32) * grad_value, axis=1)
    ) / first_gain.astype(jnp.float32)

    out_term = output_term.reshape(CORES, CORES, out_rows, width).transpose(1, 0, 2, 3)
    out_term = moves.exchange_cores(out_term).reshape(line, out_rows, width)
    out_term = moves.exchange_line(out_term)
    grad_output = moves.scatter_seq(out_term)
    return (
        layer_out,
        grad_tokens,
        grad_query,
        grad_key,
        grad_value,
        grad_output,
        gate_sum,
        up_sum,
        down_sum,
        grad_first,
        grad_gains[:, 0],
        grad_gains[:, 1],
        grad_gains[:, 2],
    )


def solution(mesh):
    placed = (
        P(("seq", "ctx"), None),
        P(("seq", "ctx"), None),
        P(("seq", "ctx"), None),
        P(("seq", "ctx"), None),
        P(("seq", "ctx"), None),
        P("seq", "ctx"),
        P("seq", "ctx"),
        P("ctx", "seq"),
        P(("seq", "ctx")),
        P(("seq", "ctx")),
        P(("seq", "ctx")),
        P(("seq", "ctx")),
        P(),
        P(("seq", "ctx"), None),
    )
    n_seq, n_ctx = mesh.shape["seq"], mesh.shape["ctx"]
    if n_ctx == QUERY_HEAD_COUNT and n_seq == 4:
        body = partial(head_body, n_seq=n_seq, n_ctx=n_ctx)
    else:
        body = context_body
    return jax.shard_map(
        body,
        mesh=mesh,
        in_specs=placed,
        out_specs=(
            P(("seq", "ctx"), None),
            P(("seq", "ctx"), None),
            P(("seq", "ctx"), None),
            P(("seq", "ctx"), None),
            P(("seq", "ctx"), None),
            P(("seq", "ctx"), None),
            P("seq", "ctx"),
            P("seq", "ctx"),
            P("ctx", "seq"),
            P(("seq", "ctx")),
            P(("seq", "ctx")),
            P(("seq", "ctx")),
            P(("seq", "ctx")),
        ),
        check_vma=False,
    )
```

```python
from functools import partial

import jax
import jax.numpy as jnp
from jax import lax
from jax.experimental import pallas as pl
from jax.experimental.pallas import tpu as pltpu
from jax.sharding import PartitionSpec as P

QUERY_HEAD_COUNT = 8
KV_HEADS = 4
HEAD_FEATURES = 256


epsilon = 1e-06
softcap = 50.0
theta = 10000.0
floor_value = -1e30


def rms_scale(signal, weight):
    return signal * lax.rsqrt(jnp.mean(signal * signal, axis=-1, keepdims=True) + epsilon) * weight


def norm_back(signal, weight, upstream):
    outcome, pullback = jax.vjp(rms_scale, signal, weight)
    return pullback(upstream)


def gate_mix(gate_pre, up_pre):
    return jax.nn.gelu(gate_pre, approximate=True) * up_pre


def rotate(signal, positions, head_width):
    row_count = signal.shape[0]
    head_count = signal.shape[1] // head_width
    half_width = head_width // 2
    frequency = theta ** (-2.0 * jnp.arange(half_width, dtype=jnp.float32) / head_width)
    angles = positions.astype(jnp.float32)[:, None] * frequency[None, :]
    cosine = jnp.cos(angles)[:, None, :]
    sine_wave = jnp.sin(angles)[:, None, :]
    shaped = signal.reshape(row_count, head_count, head_width)
    first_half = shaped[:, :, :half_width]
    second = shaped[:, :, half_width:]
    turned = jnp.concatenate(
        [first_half * cosine - second * sine_wave, second * cosine + first_half * sine_wave], axis=2
    )
    return turned.reshape(row_count, head_count * head_width)


def block_scores(head_queries, key_all, key_pos, query_pos, block_rows, score_scale):
    block_keys = key_all.reshape(block_rows, KV_HEADS, HEAD_FEATURES)
    allowed = key_pos[None, :] <= query_pos[:, None]
    unscaled_score = (
        jnp.einsum("fwvi,hwi->wvfh", head_queries, block_keys, preferred_element_type=jnp.float32)
        * score_scale
    )
    bent_score = jnp.tanh(unscaled_score / softcap)
    capped = jnp.where(allowed, softcap * bent_score, floor_value)
    return (block_keys, allowed, bent_score, capped)


def attend(head_queries, key_all, value_all, query_pos, key_pos, score_scale):
    length_total = key_all.shape[0]
    block_count = max(1, length_total // 2048)
    block_rows = length_total // block_count
    row_count = head_queries.shape[0]
    group_size = head_queries.shape[2]

    def total_step(block_index, carried):
        running_max, running_sum = carried
        block_keys, allowed, bent_score, capped = block_scores(
            head_queries, key_all, key_pos, query_pos, block_rows, score_scale
        )
        new_max = jnp.maximum(running_max, jnp.max(capped, axis=-1))
        added = jnp.sum(jnp.where(allowed, jnp.exp(capped - new_max[..., None]), 0.0), axis=-1)
        return (new_max, running_sum * jnp.exp(running_max - new_max) + added)

    start_max = jnp.full((KV_HEADS, group_size, row_count), floor_value, jnp.float32)
    start_sum = jnp.zeros((KV_HEADS, group_size, row_count), jnp.float32)
    running_max, running_sum = lax.fori_loop(0, block_count, total_step, (start_max, start_sum))
    log_total = running_max + jnp.log(running_sum)

    def mix_step(block_index, carried):
        accum, rest_acc = carried
        block_keys, allowed, bent_score, capped = block_scores(
            head_queries, key_all, key_pos, query_pos, block_rows, score_scale
        )
        block_values = value_all.reshape(block_rows, KV_HEADS, HEAD_FEATURES)
        prob_full = jnp.where(allowed, jnp.exp(capped - log_total[..., None]), 0.0)
        lowered_probs = prob_full.astype(jnp.bfloat16)
        remaining_probs = (prob_full - lowered_probs.astype(jnp.float32)).astype(jnp.bfloat16)
        accum = accum + jnp.einsum(
            "xmbe,exk->bxmk", lowered_probs, block_values, preferred_element_type=jnp.float32
        )
        rest_acc = rest_acc + jnp.einsum(
            "xmbe,exk->bxmk", remaining_probs, block_values, preferred_element_type=jnp.float32
        )
        return (accum, rest_acc)

    start_mix = jnp.zeros((row_count, KV_HEADS, group_size, HEAD_FEATURES), jnp.float32)
    full_mixture, rest_acc = lax.fori_loop(0, block_count, mix_step, (start_mix, start_mix))
    exact_mixture = full_mixture + rest_acc
    return (
        log_total,
        full_mixture.reshape(row_count, QUERY_HEAD_COUNT * HEAD_FEATURES),
        exact_mixture,
    )


def attend_back(
    head_queries,
    key_all,
    value_all,
    query_pos,
    key_pos,
    score_scale,
    log_total,
    exact_mixture,
    mixed_grad,
):
    length_total = key_all.shape[0]
    block_count = max(1, length_total // 2048)
    block_rows = length_total // block_count
    row_count = head_queries.shape[0]
    group_size = head_queries.shape[2]
    head_gradient = mixed_grad.reshape(row_count, KV_HEADS, group_size, HEAD_FEATURES)
    row_difference = jnp.einsum("ozlq,ozlq->zlo", head_gradient.astype(jnp.float32), exact_mixture)

    def grad_step(block_index, carried):
        query_acc, key_acc, value_acc = carried
        block_keys, allowed, bent_score, capped = block_scores(
            head_queries, key_all, key_pos, query_pos, block_rows, score_scale
        )
        block_values = value_all.reshape(block_rows, KV_HEADS, HEAD_FEATURES)
        prob_full = jnp.where(allowed, jnp.exp(capped - log_total[..., None]), 0.0)
        lowered_probs = prob_full.astype(jnp.bfloat16)
        value_part = jnp.einsum(
            "zwcv,czwy->vzy", lowered_probs, head_gradient, preferred_element_type=jnp.float32
        )
        prob_grad = jnp.einsum(
            "fwvi,hwi->wvfh", head_gradient, block_values, preferred_element_type=jnp.float32
        )
        lowered_logits = (
            prob_full * (prob_grad - row_difference[..., None]) * (1.0 - bent_score * bent_score)
        ).astype(jnp.bfloat16)
        query_acc = (
            query_acc
            + jnp.einsum(
                "xmbe,exk->bxmk", lowered_logits, block_keys, preferred_element_type=jnp.float32
            )
            * score_scale
        )
        key_part = (
            jnp.einsum(
                "zwcv,czwy->vzy", lowered_logits, head_queries, preferred_element_type=jnp.float32
            )
            * score_scale
        )
        key_acc = key_part.reshape(block_rows, KV_HEADS * HEAD_FEATURES)
        value_acc = value_part.reshape(block_rows, KV_HEADS * HEAD_FEATURES)
        return (query_acc, key_acc, value_acc)

    start = (
        jnp.zeros((row_count, KV_HEADS, group_size, HEAD_FEATURES), jnp.float32),
        jnp.zeros((length_total, KV_HEADS * HEAD_FEATURES), jnp.float32),
        jnp.zeros((length_total, KV_HEADS * HEAD_FEATURES), jnp.float32),
    )
    query_acc, key_acc, value_acc = lax.fori_loop(0, block_count, grad_step, start)
    return (query_acc.reshape(row_count, QUERY_HEAD_COUNT * HEAD_FEATURES), key_acc, value_acc)


def context_body(
    tokens,
    w_query,
    w_key,
    w_value,
    w_output,
    w_gate,
    w_up,
    w_down,
    first_gain,
    second_gain,
    third_gain,
    fourth_gain,
    block_pairs,
    cotangent,
):
    query_full, key_full, value_full, output_full, gain_one, gain_two, gain_three, gain_four = (
        lax.all_gather(w_query, ("seq", "ctx"), axis=0, tiled=True),
        lax.all_gather(w_key, ("seq", "ctx"), axis=0, tiled=True),
        lax.all_gather(w_value, ("seq", "ctx"), axis=0, tiled=True),
        lax.all_gather(w_output, ("seq", "ctx"), axis=0, tiled=True),
        lax.all_gather(first_gain, ("seq", "ctx"), axis=0, tiled=True),
        lax.all_gather(second_gain, ("seq", "ctx"), axis=0, tiled=True),
        lax.all_gather(third_gain, ("seq", "ctx"), axis=0, tiled=True),
        lax.all_gather(fourth_gain, ("seq", "ctx"), axis=0, tiled=True),
    )
    gain_one = gain_one.astype(jnp.float32)
    gain_two = gain_two.astype(jnp.float32)
    gain_three = gain_three.astype(jnp.float32)
    gain_four = gain_four.astype(jnp.float32)
    row_count = tokens.shape[0]
    block_size = row_count // 2
    group_size = QUERY_HEAD_COUNT // KV_HEADS
    score_scale = HEAD_FEATURES ** (-0.5)
    own_pair = lax.dynamic_index_in_dim(block_pairs, lax.axis_index("ctx"), 0, keepdims=False)
    offsets = jnp.arange(block_size, dtype=jnp.int32)
    query_pos = jnp.concatenate(
        [own_pair[0] * block_size + offsets, own_pair[1] * block_size + offsets]
    )
    key_pos = (block_pairs[:, :, None] * block_size + offsets[None, None, :]).reshape(-1)
    residual_in = tokens.astype(jnp.float32)
    normed = rms_scale(residual_in, gain_one).astype(jnp.bfloat16)
    query_proj = jnp.dot(normed, query_full, preferred_element_type=jnp.float32)
    key_proj = jnp.dot(normed, key_full, preferred_element_type=jnp.float32)
    value_proj = jnp.dot(normed, value_full, preferred_element_type=jnp.float32)
    query_low = rotate(query_proj, query_pos, HEAD_FEATURES).astype(jnp.bfloat16)
    key_low = rotate(key_proj, query_pos, HEAD_FEATURES).astype(jnp.bfloat16)
    lowered_values = value_proj.astype(jnp.bfloat16)
    key_all, value_all = (
        lax.all_gather(key_low, "ctx", axis=0, tiled=True),
        lax.all_gather(lowered_values, "ctx", axis=0, tiled=True),
    )
    head_queries = query_low.reshape(row_count, KV_HEADS, group_size, HEAD_FEATURES)
    log_total, full_mixture, exact_mixture = attend(
        head_queries, key_all, value_all, query_pos, key_pos, score_scale
    )
    mixed_low = full_mixture.astype(jnp.bfloat16)
    branch = jnp.dot(mixed_low, output_full, preferred_element_type=jnp.float32)
    residual = residual_in + rms_scale(branch, gain_two)
    feed_input = rms_scale(residual, gain_three).astype(jnp.bfloat16)
    part_gate, part_up, part_down = (
        lax.all_gather(w_gate, "seq", axis=0, tiled=True),
        lax.all_gather(w_up, "seq", axis=0, tiled=True),
        lax.all_gather(w_down, "seq", axis=1, tiled=True),
    )
    feed_all = lax.all_gather(feed_input, "ctx", axis=0, tiled=True)
    gate_pre = jnp.dot(feed_all, part_gate, preferred_element_type=jnp.float32)
    up_pre = jnp.dot(feed_all, part_up, preferred_element_type=jnp.float32)
    hidden = gate_mix(gate_pre, up_pre).astype(jnp.bfloat16)
    feed_out = lax.psum_scatter(
        jnp.dot(hidden, part_down, preferred_element_type=jnp.float32).astype(jnp.bfloat16),
        "ctx",
        scatter_dimension=0,
        tiled=True,
    ).astype(jnp.float32)
    layer_out = (residual + rms_scale(feed_out, gain_four)).astype(jnp.bfloat16)
    upstream = cotangent.astype(jnp.float32)
    feed_grad, fourth_term = norm_back(feed_out, gain_four, upstream)
    feed_low = feed_grad.astype(jnp.bfloat16)
    cotangent_all = lax.all_gather(feed_low, "ctx", axis=0, tiled=True)
    hidden_grad = jnp.einsum(
        "td,fd->tf", cotangent_all, part_down, preferred_element_type=jnp.float32
    )
    outcome, mix_pull = jax.vjp(gate_mix, gate_pre, up_pre)
    gate_grad, up_grad = mix_pull(hidden_grad)
    gate_low = gate_grad.astype(jnp.bfloat16)
    up_low = up_grad.astype(jnp.bfloat16)
    input_part = jnp.einsum(
        "tf,df->td", gate_low, part_gate, preferred_element_type=jnp.float32
    ) + jnp.einsum("tf,df->td", up_low, part_up, preferred_element_type=jnp.float32)
    feed_input_grad = lax.psum_scatter(
        input_part.astype(jnp.bfloat16), "ctx", scatter_dimension=0, tiled=True
    ).astype(jnp.float32)
    gate_term = jnp.einsum("tf,td->fd", gate_low, feed_all, preferred_element_type=jnp.float32)
    up_term = jnp.einsum("tf,td->fd", up_low, feed_all, preferred_element_type=jnp.float32)
    down_term = jnp.einsum("tf,td->fd", hidden, cotangent_all, preferred_element_type=jnp.float32)
    gate_sum, up_sum, down_sum = (
        lax.psum_scatter(
            gate_term.astype(jnp.bfloat16), "seq", scatter_dimension=1, tiled=True
        ).astype(jnp.float32),
        lax.psum_scatter(
            up_term.astype(jnp.bfloat16), "seq", scatter_dimension=1, tiled=True
        ).astype(jnp.float32),
        lax.psum_scatter(
            down_term.astype(jnp.bfloat16), "seq", scatter_dimension=1, tiled=True
        ).astype(jnp.float32),
    )
    middle_grad, third_term = norm_back(residual, gain_three, feed_input_grad)
    residual_grad = upstream + middle_grad
    branch_grad, second_term = norm_back(branch, gain_two, residual_grad)
    branch_low = branch_grad.astype(jnp.bfloat16)
    output_term = jnp.einsum("th,td->hd", mixed_low, branch_low, preferred_element_type=jnp.float32)
    mixed_grad = jnp.einsum(
        "td,hd->th", branch_low, output_full, preferred_element_type=jnp.float32
    ).astype(jnp.bfloat16)
    query_sum, key_acc, value_acc = attend_back(
        head_queries,
        key_all,
        value_all,
        query_pos,
        key_pos,
        score_scale,
        log_total,
        exact_mixture,
        mixed_grad,
    )
    key_own, value_own = (
        lax.psum_scatter(
            key_acc.astype(jnp.bfloat16), "ctx", scatter_dimension=0, tiled=True
        ).astype(jnp.float32),
        lax.psum_scatter(
            value_acc.astype(jnp.bfloat16), "ctx", scatter_dimension=0, tiled=True
        ).astype(jnp.float32),
    )
    query_grad = rotate(query_sum, -query_pos, HEAD_FEATURES).astype(jnp.bfloat16)
    key_grad = rotate(key_own, -query_pos, HEAD_FEATURES).astype(jnp.bfloat16)
    value_grad = value_own.astype(jnp.bfloat16)
    normed_grad = jnp.einsum(
        "th,dh->td", query_grad, query_full, preferred_element_type=jnp.float32
    )
    normed_grad = normed_grad + jnp.einsum(
        "th,dh->td", key_grad, key_full, preferred_element_type=jnp.float32
    )
    normed_grad = normed_grad + jnp.einsum(
        "th,dh->td", value_grad, value_full, preferred_element_type=jnp.float32
    )
    query_term = jnp.einsum("td,th->dh", normed, query_grad, preferred_element_type=jnp.float32)
    key_term = jnp.einsum("td,th->dh", normed, key_grad, preferred_element_type=jnp.float32)
    value_term = jnp.einsum("td,th->dh", normed, value_grad, preferred_element_type=jnp.float32)
    input_grad, first_term = norm_back(residual_in, gain_one, normed_grad)
    grad_tokens = (residual_grad + input_grad).astype(jnp.bfloat16)
    grad_sums = (
        lax.psum_scatter(query_term, ("seq", "ctx"), scatter_dimension=0, tiled=True),
        lax.psum_scatter(key_term, ("seq", "ctx"), scatter_dimension=0, tiled=True),
        lax.psum_scatter(value_term, ("seq", "ctx"), scatter_dimension=0, tiled=True),
        lax.psum_scatter(output_term, ("seq", "ctx"), scatter_dimension=0, tiled=True),
        lax.psum_scatter(first_term, ("seq", "ctx"), scatter_dimension=0, tiled=True),
        lax.psum_scatter(second_term, ("seq", "ctx"), scatter_dimension=0, tiled=True),
        lax.psum_scatter(third_term, ("seq", "ctx"), scatter_dimension=0, tiled=True),
        lax.psum_scatter(fourth_term, ("seq", "ctx"), scatter_dimension=0, tiled=True),
    )
    return (
        layer_out,
        grad_tokens,
        grad_sums[0],
        grad_sums[1],
        grad_sums[2],
        grad_sums[3],
        gate_sum.T,
        up_sum.T,
        down_sum,
        grad_sums[4],
        grad_sums[5],
        grad_sums[6],
        grad_sums[7],
    )


CORES = 2
GELU_IN = 0.7978845608
GELU_CUBE = 0.044715
VMEM_LIMIT = 56 * 2**20


def wide(value):
    return value.astype(jnp.float32)


def narrow(value):
    return value.astype(jnp.bfloat16)


def rms_parts(signal):
    scale = lax.rsqrt(jnp.mean(signal * signal, axis=-1, keepdims=True) + epsilon)
    return scale, signal * scale


def rms_back(scale, unit, weight, upstream):
    weighted = upstream * weight
    mean = jnp.mean(weighted * unit, axis=-1, keepdims=True)
    return scale * (weighted - unit * mean), jnp.sum(upstream * unit, axis=0)


def dot_nn(left, right):
    return jnp.dot(left, right, preferred_element_type=jnp.float32)


def dot_nt(left, right):
    return jnp.einsum("ab,cb->ac", left, right, preferred_element_type=jnp.float32)


def dot_tn(left, right):
    return jnp.einsum("ab,ac->bc", left, right, preferred_element_type=jnp.float32)


def after(value, *others):
    anywhere = pl.BlockSpec(memory_space=pl.ANY)
    return pl.pallas_call(
        lambda *refs: None,
        in_specs=[anywhere] * (1 + len(others)),
        out_specs=anywhere,
        out_shape=jax.ShapeDtypeStruct(value.shape, value.dtype),
        input_output_aliases={0: 0},
    )(value, *others)


def fresh(shape, dtype, *others):
    anywhere = pl.BlockSpec(memory_space=pl.ANY)
    return pl.pallas_call(
        lambda *refs: None,
        in_specs=[anywhere] * len(others),
        out_specs=anywhere,
        out_shape=jax.ShapeDtypeStruct(shape, dtype),
    )(*others)


def lull(*others):
    anywhere = pl.BlockSpec(memory_space=pl.ANY)
    return pl.pallas_call(
        lambda *refs: None,
        in_specs=[anywhere] * len(others),
        out_specs=anywhere,
        out_shape=jax.ShapeDtypeStruct((8, 128), jnp.float32),
        cost_estimate=pl.CostEstimate(flops=10**12, bytes_accessed=0, transcendentals=0),
    )(*others)


class Order:
    def __init__(self):
        self.last = ()

    def pin(self, value, sent=None):
        extra = () if sent is None else (lull(sent),)
        value = after(value, *self.last, *extra)
        self.last = (value,)
        return value

    def mark(self, value):
        self.last = (value,)

    def hold(self, value):
        return after(value, *self.last)


class Moves:
    def __init__(self, n_seq, n_ctx):
        self.n_seq, self.n_ctx = n_seq, n_ctx
        self.line = n_ctx // CORES
        self.seq = lax.axis_index("seq")
        self.ctx = lax.axis_index("ctx")
        self.plane = self.ctx // CORES
        self.core = self.ctx % CORES

    def _send(self, value, move):
        pairs = []
        for s in range(self.n_seq):
            for c in range(self.n_ctx):
                t = move(s, c // CORES, c % CORES)
                pairs.append((s * self.n_ctx + c, t[0] * self.n_ctx + t[1] * CORES + t[2]))
        return lax.ppermute(value, ("seq", "ctx"), pairs)

    def across(self, value, mask):
        return self._send(value, lambda s, z, k: (s ^ mask, z, k))

    def along(self, value, step):
        return self._send(value, lambda s, z, k: (s, (z + step) % self.line, k))

    def plane_swap(self, value, mask):
        return self._send(value, lambda s, z, k: (s, z ^ mask, k))

    def swap(self, value):
        return self._send(value, lambda s, z, k: (s, z, k ^ 1))

    def gather_halves(self, block, gate):
        half = block.shape[0] // 2
        low, high = block[:half], block[half:]
        low_near = self.across(low, 2)
        high_near = self.across(high, 1)
        yield None
        low_near, high_near = gate(low_near, block), gate(high_near)
        low_two, high_two = jnp.stack([low, low_near]), jnp.stack([high, high_near])
        low_far = self.across(low_two, 1)
        high_far = self.across(high_two, 2)
        yield None
        yield block, low_near, high_near, gate(low_far, low_two), gate(high_far)

    def place_halves(self, pieces):
        block, low_near, high_near, low_far, high_far = pieces
        half = block.shape[0] // 2
        out = fresh((self.n_seq,) + block.shape, block.dtype, low_near)
        put = lambda out, piece, mask, at: lax.dynamic_update_slice(
            out, piece[None], (self.seq ^ mask, at) + (0,) * (block.ndim - 1)
        )
        out = lax.dynamic_update_index_in_dim(out, block, self.seq, 0)
        out = put(out, low_near, 2, 0)
        out = put(out, high_near, 1, half)
        out = put(out, low_far[0], 1, 0)
        out = put(out, low_far[1], 3, 0)
        out = put(out, high_far[0], 2, half)
        return put(out, high_far[1], 3, half).reshape((-1,) + block.shape[1:])

    def scatter_whole(self, terms, mask, gate):
        other = 3 - mask
        pick = lambda m: lax.dynamic_index_in_dim(terms, self.seq ^ m, 0, False)
        sent = jnp.stack([pick(mask), pick(3)])
        near = self.across(sent, mask)
        yield None
        near = gate(near, sent)
        onward = narrow(wide(pick(other)) + wide(near[1]))
        far = self.across(onward, other)
        yield None
        yield wide(pick(0)) + wide(near[0]) + wide(gate(far, onward))

    def scatter_halves(self, terms, gate):
        half = terms.shape[1] // 2
        low = self.scatter_whole(terms[:, :half], 1, gate)
        high = self.scatter_whole(terms[:, half:], 2, gate)
        for _ in range(2):
            next(low), next(high)
            yield None
        yield jnp.concatenate([next(low), next(high)], axis=0)

    def exchange_line(self, blocks):
        out = fresh(blocks.shape, blocks.dtype, blocks)
        own = lax.dynamic_index_in_dim(blocks, self.plane, 0, False)
        out = lax.dynamic_update_index_in_dim(out, own, self.plane, 0)
        for step in range(1, self.line):
            sent = lax.dynamic_index_in_dim(blocks, (self.plane + step) % self.line, 0, False)
            got = self.along(sent, step)
            out = lax.dynamic_update_index_in_dim(out, got, (self.plane - step) % self.line, 0)
        return out

    def exchange_planes(self, blocks, pin):
        pick = lambda mask: lax.dynamic_index_in_dim(blocks, self.plane ^ mask, 0, False)
        sent = jnp.stack([pick(2), pick(3)])
        near = self.plane_swap(sent, 2)
        yield None
        near = pin(near, sent)
        sent = jnp.stack([pick(1), near[1]])
        far = self.plane_swap(sent, 1)
        yield None
        far = pin(far, sent)
        out = fresh(blocks.shape, blocks.dtype, far)
        for mask, block in ((0, pick(0)), (2, near[0]), (1, far[0]), (3, far[1])):
            out = lax.dynamic_update_index_in_dim(out, block, self.plane ^ mask, 0)
        yield out

    def exchange_cores(self, blocks):
        own = lax.dynamic_index_in_dim(blocks, self.core, 0, False)
        got = self.swap(lax.dynamic_index_in_dim(blocks, 1 - self.core, 0, False))
        first = self.core == 0
        return jnp.stack([jnp.where(first, own, got), jnp.where(first, got, own)])


ANYWHERE = pl.BlockSpec(memory_space=pl.ANY)


def tile(rows, columns):
    return pl.BlockSpec((rows, columns), lambda i: (i, 0))


def whole(*shape):
    return pl.BlockSpec(shape, lambda i: (0,) * len(shape))


def call(kernel, steps, in_specs, out_specs, out_shape, flops, args, scratch=(), others=()):
    count = len(args)

    def body(*refs):
        kernel(*refs[:count], *refs[count + len(others) :])

    return pl.pallas_call(
        body,
        grid=(steps,),
        in_specs=in_specs + [ANYWHERE] * len(others),
        out_specs=out_specs,
        out_shape=out_shape,
        scratch_shapes=list(scratch),
        compiler_params=pltpu.CompilerParams(vmem_limit_bytes=VMEM_LIMIT),
        cost_estimate=pl.CostEstimate(flops=flops, bytes_accessed=0, transcendentals=0),
    )(*args, *others)


def array(dtype, *shape):
    return jax.ShapeDtypeStruct(shape, dtype)


def mul_nt(left, right):
    return lax.dot_general(
        left, right, (((1,), (1,)), ((), ())), preferred_element_type=jnp.float32
    )


def mul_tn(left, right):
    return lax.dot_general(
        left, right, (((0,), (0,)), ((), ())), preferred_element_type=jnp.float32
    )


def turn_pair(value, cosine, sine):
    half = value.shape[1] // 2
    first, second = value[:, :half], value[:, half:]
    return jnp.concatenate(
        [first * cosine - second * sine, second * cosine + first * sine], axis=1
    )


BF16, F32 = jnp.bfloat16, jnp.float32
TILE = 256


def load(copies, sems):
    started = [pltpu.make_async_copy(a, b, sems.at[i]) for i, (a, b) in enumerate(copies)]
    for copy in started:
        copy.start()
    return started


def whole_copies(seq, pieces, target):
    mask, own, near, far = pieces
    rows = own.shape[0]
    at = lambda m: target.at[pl.ds(pl.multiple_of((seq ^ m) * rows, 64), rows)]
    other = 3 - mask
    first, second = far.at[pl.ds(0, rows)], far.at[pl.ds(rows, rows)]
    return [(own, at(0)), (near, at(mask)), (first, at(other)), (second, at(3))]


def half_copies(seq, pieces, target):
    own, low_near, high_near, low_far, high_far = pieces
    rows = own.shape[0]
    half = rows // 2
    at = lambda m, h: target.at[pl.ds(pl.multiple_of((seq ^ m) * rows + h * half, 32), half)]
    return [
        (own, target.at[pl.ds(pl.multiple_of(seq * rows, 64), rows)]),
        (low_near, at(2, 0)),
        (high_near, at(1, 1)),
        (low_far.at[0], at(1, 0)),
        (low_far.at[1], at(3, 0)),
        (high_far.at[0], at(2, 1)),
        (high_far.at[1], at(3, 1)),
    ]


SCALARS = pl.BlockSpec(memory_space=pltpu.SMEM)


def project_rows(place, tokens, pieces, feats, tables):
    rows, width = tokens.shape
    wide_columns = pieces[0].shape[1]

    def kernel(place_ref, x_ref, own, near_a, near_b, far_a, far_b, cq, sq, cp, sp, *refs):
        normed_ref, query_ref, pair_ref, gains_ref, w_ref, sems = refs

        @pl.when(pl.program_id(0) == 0)
        def _():
            copies = half_copies(place_ref[2], (own, near_a, near_b, far_a, far_b), w_ref)
            for copy in load(copies, sems):
                copy.wait()
            gains_ref[...] = w_ref[:, 2 * feats :].astype(F32).T[:8]

        x = x_ref[...].astype(F32)
        scale = lax.rsqrt(jnp.mean(x * x, axis=-1, keepdims=True) + epsilon)
        normed = (x * scale * gains_ref[0:1]).astype(BF16)
        normed_ref[...] = normed
        both = dot_nn(normed, w_ref[:, : 2 * feats])
        query_ref[...] = turn_pair(both[:, :feats], cq[...], sq[...]).astype(BF16)
        pair_ref[...] = turn_pair(both[:, feats:], cp[...], sp[...]).astype(BF16)

    half = feats // 2
    return call(
        kernel,
        rows // TILE,
        [SCALARS, tile(TILE, width)] + [ANYWHERE] * 5 + [tile(TILE, half)] * 4,
        [tile(TILE, width), tile(TILE, feats), tile(TILE, feats), whole(8, width)],
        [
            array(BF16, rows, width),
            array(BF16, rows, feats),
            array(BF16, rows, feats),
            array(F32, 8, width),
        ],
        4 * rows * width * feats,
        (place, tokens) + pieces + tables,
        [pltpu.VMEM((width, wide_columns), BF16), pltpu.SemaphoreType.DMA((7,))],
    )


def soft_rows(query, keys, place, places):
    bent = jnp.tanh(mul_nt(query, keys) * (HEAD_FEATURES ** (-0.5) / softcap))
    weight = jnp.where(places <= place, jnp.exp(softcap * bent), 0.0)
    return bent, weight / jnp.sum(weight, axis=-1, keepdims=True)


def attend_head(query, key, value, place, places, others):
    rows, feats = query.shape

    def kernel(q_ref, k_ref, v_ref, place_ref, places_ref, out_ref):
        _, probs = soft_rows(q_ref[...], k_ref[...], place_ref[...], places_ref[...])
        out_ref[...] = dot_nn(probs.astype(BF16), v_ref[...]).astype(BF16)

    return call(
        kernel,
        rows // TILE,
        [tile(TILE, feats), whole(rows, feats), whole(rows, feats), tile(TILE, 1), whole(1, rows)],
        [tile(TILE, feats)],
        [array(BF16, rows, feats)],
        4 * rows * rows * feats,
        (query, key, value, place, places),
        (),
        others,
    )[0]


def attend_head_back(place, query, key, value, mixed_grad, spot, spots, cosine, sine, others):
    rows, feats = query.shape
    score_scale = HEAD_FEATURES ** (-0.5)
    steps = rows // TILE

    def kernel(place_ref, q_ref, k_ref, v_ref, g_ref, spot_ref, spots_ref, c_ref, s_ref, *refs):
        dq, own_ref, send_ref, dk, dv = refs
        step = pl.program_id(0)

        @pl.when(step == 0)
        def _():
            dk[...] = jnp.zeros_like(dk)
            dv[...] = jnp.zeros_like(dv)

        query, keys, grad = q_ref[...], k_ref[...], g_ref[...]
        bent, probs = soft_rows(query, keys, spot_ref[...], spots_ref[...])
        prob_grad = mul_nt(grad, v_ref[...])
        delta = jnp.sum(probs * prob_grad, axis=-1, keepdims=True)
        raw = (probs * (prob_grad - delta) * (1.0 - bent * bent)).astype(BF16)
        total = dot_nn(raw, keys) * score_scale
        dq[...] = turn_pair(total, c_ref[...], -s_ref[...]).astype(BF16)
        dk[...] += mul_tn(raw, query) * score_scale
        dv[...] += mul_tn(probs.astype(BF16), grad)

        @pl.when(step == steps - 1)
        def _():
            first = place_ref[1] == 0
            own_ref[...] = jnp.where(first, dk[...], dv[...])
            send_ref[...] = jnp.where(first, dv[...], dk[...])

    return call(
        kernel,
        steps,
        [SCALARS, tile(TILE, feats), whole(rows, feats), whole(rows, feats), tile(TILE, feats)]
        + [tile(TILE, 1), whole(1, rows)]
        + [tile(TILE, feats // 2), tile(TILE, feats // 2)],
        [tile(TILE, feats), whole(rows, feats), whole(rows, feats)],
        [array(BF16, rows, feats), array(F32, rows, feats), array(F32, rows, feats)],
        10 * rows * rows * feats,
        (place, query, key, value, mixed_grad, spot, spots, cosine, sine),
        [pltpu.VMEM((rows, feats), F32)] * 2,
        others,
    )


def branch_rows(place, mixed, own, other, tokens, gain_two, gain_three):
    heads, rows, feats = mixed.shape
    blocks, out_rows, width = own.shape
    per_head = feats // (CORES * out_rows)
    own_rows = TILE // CORES

    def kernel(
        place_ref, m_ref, own_ref, other_ref, x_ref, two_ref, three_ref, out_ref, mine_ref, w_ref, sems
    ):
        step = pl.program_id(0)
        core = place_ref[1]

        @pl.when(step == 0)
        def _():
            copies = [(own_ref, w_ref.at[:, core]), (other_ref, w_ref.at[:, 1 - core])]
            for copy in load(copies, sems):
                copy.wait()

        branch = 0.0
        for h in range(heads):
            head = w_ref[h * per_head : (h + 1) * per_head].reshape(feats, width)
            branch += dot_nn(m_ref[h], head)

        @pl.when(step == place_ref[0])
        def _():
            mine_ref[...] = jnp.where(core == 0, branch[:own_rows], branch[own_rows:])

        scale = lax.rsqrt(jnp.mean(branch * branch, axis=-1, keepdims=True) + epsilon)
        residual = x_ref[...].astype(F32) + branch * scale * two_ref[...]
        scale = lax.rsqrt(jnp.mean(residual * residual, axis=-1, keepdims=True) + epsilon)
        out_ref[...] = (residual * scale * three_ref[...]).astype(BF16)

    return call(
        kernel,
        rows // TILE,
        [
            pl.BlockSpec(memory_space=pltpu.SMEM),
            pl.BlockSpec((heads, TILE, feats), lambda i: (0, i, 0)),
            ANYWHERE,
            ANYWHERE,
            tile(TILE, width),
            whole(1, width),
            whole(1, width),
        ],
        [tile(TILE, width), whole(own_rows, width)],
        [array(BF16, rows, width), array(F32, own_rows, width)],
        2 * heads * rows * feats * width,
        (place, mixed, own, other, tokens, gain_two, gain_three),
        [
            pltpu.VMEM((blocks, CORES, out_rows, width), BF16),
            pltpu.SemaphoreType.DMA((2,)),
        ],
    )


def feed_open(place, feed, gate_pieces, up_pieces):
    rows, width = feed.shape
    units = gate_pieces[0].shape[1]

    def kernel(place_ref, x_ref, *refs):
        gates, ups = refs[:3], refs[3:6]
        hidden_ref, gate_ref, up_ref, gw_ref, uw_ref, gate_sems, up_sems = refs[6:]
        seq = place_ref[2]
        gate_copies = whole_copies(seq, (1,) + gates, gw_ref)
        up_copies = whole_copies(seq, (2,) + ups, uw_ref)
        first = pl.program_id(0) == 0

        @pl.when(first)
        def _():
            started = load(gate_copies, gate_sems)
            load(up_copies, up_sems)
            for copy in started:
                copy.wait()

        x = x_ref[...]
        gate = dot_nn(x, gw_ref[...])

        @pl.when(first)
        def _():
            for i, (a, b) in enumerate(up_copies):
                pltpu.make_async_copy(a, b, up_sems.at[i]).wait()

        up = dot_nn(x, uw_ref[...])
        square = gate * gate
        bend = jnp.tanh(GELU_IN * (gate + GELU_CUBE * square * gate))
        half = 0.5 * (1.0 + bend)
        gelu = half * gate
        slope = half + 0.5 * gate * (1.0 - bend * bend) * (
            GELU_IN + 3.0 * GELU_IN * GELU_CUBE * square
        )
        hidden_ref[...] = (gelu * up).astype(BF16)
        gate_ref[...] = (up * slope).astype(BF16)
        up_ref[...] = gelu.astype(BF16)

    return call(
        kernel,
        rows // TILE,
        [SCALARS, tile(TILE, width)] + [ANYWHERE] * 6,
        [tile(TILE, units)] * 3,
        [array(BF16, rows, units)] * 3,
        4 * rows * width * units,
        (place, feed) + gate_pieces + up_pieces,
        [pltpu.VMEM((width, units), BF16)] * 2 + [pltpu.SemaphoreType.DMA((4,))] * 2,
    )


def feed_close(place, hidden, down_pieces):
    rows, units = hidden.shape
    width = down_pieces[0].shape[0] * 4

    def kernel(place_ref, x_ref, *refs):
        out_ref, dw_ref, sems = refs[5:]

        @pl.when(pl.program_id(0) == 0)
        def _():
            for copy in load(half_copies(place_ref[2], refs[:5], dw_ref), sems):
                copy.wait()

        out_ref[...] = mul_nt(x_ref[...], dw_ref[...]).astype(BF16)

    return call(
        kernel,
        rows // TILE,
        [SCALARS, tile(TILE, units)] + [ANYWHERE] * 5,
        [tile(TILE, width)],
        [array(BF16, rows, width)],
        2 * rows * width * units,
        (place, hidden) + down_pieces,
        [pltpu.VMEM((width, units), BF16), pltpu.SemaphoreType.DMA((7,))],
    )[0]


def mixed_back(place, branch, own, other):
    rows, width = branch.shape
    blocks, out_rows, _ = own.shape
    heads = QUERY_HEAD_COUNT
    per_head = blocks // heads
    feats = per_head * CORES * out_rows

    def kernel(place_ref, b_ref, own_ref, other_ref, out_ref, w_ref):
        core = place_ref[1]
        w_ref[:, pl.ds(core, 1)] = own_ref[...][:, None]
        w_ref[:, pl.ds(1 - core, 1)] = other_ref[...][:, None]
        out_ref[0] = mul_nt(b_ref[...], w_ref[...].reshape(feats, width)).astype(BF16)

    blocks_of = pl.BlockSpec((per_head, out_rows, width), lambda i: (i, 0, 0))
    return call(
        kernel,
        heads,
        [SCALARS, whole(rows, width), blocks_of, blocks_of],
        [pl.BlockSpec((1, rows, feats), lambda i: (i, 0, 0))],
        [array(BF16, heads, rows, feats)],
        2 * rows * width * heads * feats,
        (place, branch, own, other),
        [pltpu.VMEM((per_head, CORES, out_rows, width), BF16)],
    )[0]


def feed_back(place, grad, gate_factor, up_factor, gate_pieces, up_pieces, down_pieces):
    rows, width = grad.shape
    units = gate_factor.shape[1]

    def kernel(place_ref, g_ref, gf_ref, uf_ref, *refs):
        gates, ups, downs = refs[:3], refs[3:6], refs[6:11]
        gate_ref, up_ref, out_ref, gw_ref, uw_ref, dw_ref, gate_sems, up_sems, down_sems = refs[11:]
        seq = place_ref[2]
        gate_copies = whole_copies(seq, (1,) + gates, gw_ref)
        up_copies = whole_copies(seq, (2,) + ups, uw_ref)
        first = pl.program_id(0) == 0

        @pl.when(first)
        def _():
            started = load(half_copies(seq, downs, dw_ref), down_sems)
            load(gate_copies, gate_sems)
            load(up_copies, up_sems)
            for copy in started:
                copy.wait()

        hidden_grad = dot_nn(g_ref[...], dw_ref[...])
        gate_low = (hidden_grad * gf_ref[...].astype(F32)).astype(BF16)
        up_low = (hidden_grad * uf_ref[...].astype(F32)).astype(BF16)
        gate_ref[...] = gate_low
        up_ref[...] = up_low

        @pl.when(first)
        def _():
            for copies, sems in ((gate_copies, gate_sems), (up_copies, up_sems)):
                for i, (a, b) in enumerate(copies):
                    pltpu.make_async_copy(a, b, sems.at[i]).wait()

        out_ref[...] = (mul_nt(gate_low, gw_ref[...]) + mul_nt(up_low, uw_ref[...])).astype(BF16)

    return call(
        kernel,
        rows // TILE,
        [SCALARS, tile(TILE, width), tile(TILE, units), tile(TILE, units)] + [ANYWHERE] * 11,
        [tile(TILE, units), tile(TILE, units), tile(TILE, width)],
        [array(BF16, rows, units), array(BF16, rows, units), array(BF16, rows, width)],
        6 * rows * width * units,
        (place, grad, gate_factor, up_factor) + gate_pieces + up_pieces + down_pieces,
        [pltpu.VMEM((width, units), BF16)] * 3
        + [pltpu.SemaphoreType.DMA((4,))] * 2
        + [pltpu.SemaphoreType.DMA((7,))],
    )


def normed_back(place, query_grad, own, other, cosine, sine, pieces):
    rows, feats = query_grad.shape
    width, wide_columns = pieces[0].shape[0] * 4, pieces[0].shape[1]

    def kernel(place_ref, q_ref, own_ref, other_ref, c_ref, s_ref, *refs):
        both_ref, out_ref, w_ref, sems = refs[5:]

        @pl.when(pl.program_id(0) == 0)
        def _():
            for copy in load(half_copies(place_ref[2], refs[:5], w_ref), sems):
                copy.wait()

        pair = turn_pair(own_ref[...] + other_ref[...], c_ref[...], -s_ref[...]).astype(BF16)
        both_ref[:, :feats] = q_ref[...]
        both_ref[:, feats:] = pair
        out_ref[...] = mul_nt(both_ref[...], w_ref[:, : 2 * feats]).astype(BF16)

    return call(
        kernel,
        rows // TILE,
        [SCALARS] + [tile(TILE, feats)] * 3 + [tile(TILE, feats // 2)] * 2 + [ANYWHERE] * 5,
        [tile(TILE, 2 * feats), tile(TILE, width)],
        [array(BF16, rows, 2 * feats), array(BF16, rows, width)],
        4 * rows * feats * width,
        (place, query_grad, own, other, cosine, sine) + pieces,
        [pltpu.VMEM((width, wide_columns), BF16), pltpu.SemaphoreType.DMA((7,))],
    )


def weight_grad(left, right, block, others, more=None):
    rows, width = left.shape
    columns = right.shape[1]
    total = columns + (0 if more is None else more.shape[1])

    def kernel(left_ref, right_ref, *refs):
        refs[-1][:, :columns] = mul_tn(left_ref[...], right_ref[...]).astype(BF16)
        if more is not None:
            refs[-1][:, columns:] = refs[0][...]

    extra = () if more is None else (more,)
    return call(
        kernel,
        width // block,
        [pl.BlockSpec((rows, block), lambda i: (0, i)), whole(rows, columns)]
        + [tile(block, v.shape[1]) for v in extra],
        [tile(block, total)],
        [array(BF16, width, total)],
        2 * rows * width * columns,
        (left, right) + extra,
        (),
        others,
    )[0]


def head_body(
    tokens,
    w_query,
    w_key,
    w_value,
    w_output,
    w_gate,
    w_up,
    w_down,
    first_gain,
    second_gain,
    third_gain,
    fourth_gain,
    block_pairs,
    cotangent,
    n_seq,
    n_ctx,
):
    moves = Moves(n_seq, n_ctx)
    order = Order()
    pin, hold = order.pin, order.hold
    free = lambda v: v
    line = moves.line
    core_zero = moves.core == 0
    rows, width = tokens.shape
    feat_rows = w_query.shape[0]
    out_rows = w_output.shape[0]
    feats = HEAD_FEATURES
    pad = 128
    gather = lambda v: lax.all_gather(v, "ctx", axis=0, tiled=True)
    scatter = lambda v: lax.psum_scatter(v, "ctx", scatter_dimension=0, tiled=True)

    place = jnp.stack([moves.plane, moves.core, moves.seq]).astype(jnp.int32)
    block = w_gate.shape[0]
    half = block // 2

    gate_near = moves.across(w_gate, 1)
    up_near = moves.across(w_up, 2)
    gains_in = jnp.stack([first_gain, second_gain, third_gain, fourth_gain], axis=1)
    gains_in = jnp.pad(gains_in, ((0, 0), (0, pad - 4)))
    by_head = jnp.concatenate(
        [
            w_query.reshape(feat_rows, line, CORES, feats),
            jnp.stack(
                [
                    w_key.reshape(feat_rows, line, feats),
                    w_value.reshape(feat_rows, line, feats),
                ],
                axis=2,
            ),
            jnp.broadcast_to(gains_in[:, None, None, :], (feat_rows, line, CORES, pad)),
        ],
        axis=3,
    ).transpose(2, 1, 0, 3)
    by_plane = moves.exchange_cores(by_head).transpose(1, 0, 2, 3)
    own_columns = moves.exchange_line(by_plane).reshape(n_ctx * feat_rows, 2 * feats + pad)
    own_columns = pin(own_columns, by_plane)
    tokens_in = hold(tokens)
    tokens_all = gather(tokens_in)
    columns_move = moves.gather_halves(own_columns, pin)
    next(columns_move)
    gate_near, up_near = pin(gate_near), pin(up_near)
    over_y = pin(jnp.stack([w_gate, gate_near]))
    over_x = pin(jnp.stack([w_up, up_near]))
    next(columns_move)

    block_size = rows // 2
    offsets = jnp.arange(block_size, dtype=jnp.int32)
    pos = (hold(block_pairs)[:, :, None] * block_size + offsets[None, None, :]).reshape(-1)
    spot, spots = pos[:, None], pos[None, :]
    frequency = theta ** (-2.0 * jnp.arange(feats // 2, dtype=jnp.float32) / feats)
    angles = wide(pos)[:, None] * frequency[None, :]
    cosine, sine = pin(jnp.cos(angles)), pin(jnp.sin(angles))
    pair_cosine = pin(jnp.where(core_zero, cosine, 1.0))
    pair_sine = pin(jnp.where(core_zero, sine, 0.0))
    tables = (cosine, sine, pair_cosine, pair_sine)

    columns = next(columns_move)
    over_y = moves.across(hold(over_y), 2)
    over_x = moves.across(hold(over_x), 1)
    down_own = pin(hold(w_down).T)
    tokens_all = pin(tokens_all, tokens_in)
    out_near = moves.plane_swap(hold(w_output), 2)

    normed, query, pair, gains = project_rows(place, tokens_all, columns, feats, tables)
    gain_one, gain_two, gain_three, gain_four = (gains[i : i + 1] for i in range(4))
    pair_other = moves.swap(pair)
    order.mark(pair)
    out_near = pin(out_near)
    out_two = pin(jnp.stack([w_output, out_near]))
    out_far = moves.plane_swap(out_two, 1)
    pair_other = pin(pair_other, pair)
    key = jnp.where(core_zero, pair, pair_other)
    value = jnp.where(core_zero, pair_other, pair)
    mixed = pin(attend_head(query, key, value, spot, spots, order.last))
    mixed_all = lax.all_gather(mixed, "ctx", axis=0)

    out_far = pin(out_far, out_two)
    out_line = fresh((line,) + w_output.shape, w_output.dtype, out_far)
    for mask, piece in ((0, w_output), (2, out_near), (1, out_far[0]), (3, out_far[1])):
        out_line = lax.dynamic_update_index_in_dim(out_line, piece, moves.plane ^ mask, 0)
    out_move = moves.gather_halves(pin(out_line), pin)
    next(out_move), next(out_move)
    down_move = moves.gather_halves(hold(down_own), pin)
    next(down_move)
    out_own = pin(moves.place_halves(next(out_move)))
    out_other = moves.swap(out_own)
    next(down_move)
    out_other = pin(out_other, out_own)
    mixed_all = pin(mixed_all, mixed)
    feed_all, branch = branch_rows(
        place, mixed_all, out_own, out_other, tokens_all, gain_two, gain_three
    )
    order.mark(branch)
    over_x, over_y = pin(over_x), pin(over_y)
    gate_pieces = (w_gate, gate_near, over_y.reshape(-1, over_y.shape[2]))
    up_pieces = (w_up, up_near, over_x.reshape(-1, over_x.shape[2]))
    hidden, gate_factor, up_factor = feed_open(place, feed_all, gate_pieces, up_pieces)
    order.mark(hidden)
    down_pieces = next(down_move)
    feed_part = feed_close(place, hidden, down_pieces)
    order.mark(feed_part)
    feed_out = scatter(feed_part)

    scale_two, unit_two = rms_parts(hold(branch))
    residual = wide(tokens) + unit_two * gain_two
    scale_three, unit_three = rms_parts(residual)
    unit_two, unit_three, residual = pin(unit_two), pin(unit_three), pin(residual)

    upstream = wide(cotangent)
    feed_out = pin(feed_out, feed_part)
    scale_four, unit_four = rms_parts(wide(feed_out))
    layer_out = narrow(residual + unit_four * gain_four)
    feed_grad, fourth_term = rms_back(scale_four, unit_four, gain_four, upstream)
    feed_low = pin(narrow(feed_grad))
    grad_all = pin(gather(feed_low), feed_low)
    gate_low, up_low, input_part = feed_back(
        place, grad_all, gate_factor, up_factor, gate_pieces, up_pieces, down_pieces
    )
    order.mark(input_part)
    feed_input_grad = scatter(input_part)
    shape = (n_seq, block, gate_low.shape[1])
    down_term = weight_grad(grad_all, hidden, 384, order.last).reshape(shape)
    order.mark(down_term)
    down_move = moves.scatter_halves(down_term, pin)
    next(down_move)
    gate_term = weight_grad(feed_all, gate_low, 384, order.last).reshape(shape)
    order.mark(gate_term)
    gate_move = moves.scatter_whole(gate_term, 1, pin)
    next(gate_move)
    up_term = weight_grad(feed_all, up_low, 384, order.last).reshape(shape)
    order.mark(up_term)
    up_move = moves.scatter_whole(up_term, 2, pin)
    next(up_move)
    next(down_move)
    feed_input_grad = wide(pin(feed_input_grad, input_part))
    middle_grad, third_term = rms_back(scale_three, unit_three, gain_three, feed_input_grad)
    residual_grad = upstream + middle_grad
    branch_grad, second_term = rms_back(scale_two, unit_two, gain_two, residual_grad)
    branch_low = pin(narrow(branch_grad))
    branch_all = gather(branch_low)

    mixed_own = pin(mixed_back(place, branch_low, out_own, out_other))
    mixed_grad = lax.all_to_all(mixed_own, "ctx", split_axis=0, concat_axis=0, tiled=True)
    mixed_grad = pin(mixed_grad.reshape(-1, feats), mixed_own)
    query_grad, pair_own, pair_send = attend_head_back(
        place, query, key, value, mixed_grad, spot, spots, cosine, sine, order.last
    )
    order.mark(query_grad)
    pair_other = moves.swap(pair_send)
    down_sum = pin(next(down_move)).T
    pair_other = pin(pair_other, pair_send)
    qkv_grad, normed_part = normed_back(
        place, query_grad, pair_own, pair_other, pair_cosine, pair_sine, columns
    )
    order.mark(normed_part)
    normed_grad = scatter(normed_part)

    next(gate_move), next(up_move)
    branch_all = pin(branch_all)
    output_term = weight_grad(mixed, branch_all, feats, order.last)
    order.mark(output_term)
    out_term = output_term.reshape(CORES, CORES, out_rows, width).transpose(1, 0, 2, 3)
    out_term = moves.exchange_cores(out_term).reshape(line, out_rows, width)
    terms = jnp.stack([second_term, third_term, fourth_term])
    terms = narrow(jnp.pad(terms, ((0, pad - 3), (0, 0))).T)
    qkv_term = weight_grad(normed, qkv_grad, 384, order.last, terms)
    order.mark(qkv_term)
    qkv_move = moves.scatter_halves(qkv_term.reshape(n_seq, width // n_seq, -1), pin)
    next(qkv_move)
    out_move = moves.exchange_planes(pin(out_term), pin)
    next(out_move)
    next(qkv_move)
    next(out_move)
    gate_sum, up_sum = next(gate_move), next(up_move)
    own_term = pin(narrow(next(qkv_move))).reshape(line, CORES, feat_rows, 2 * feats + pad)
    own_term = moves.exchange_line(own_term).transpose(1, 0, 2, 3)
    out_term = next(out_move)
    out_move = moves.scatter_whole(out_term, 1, pin)
    next(out_move)
    next(out_move)
    own_term = wide(pin(moves.exchange_cores(own_term)).transpose(2, 1, 0, 3))
    grad_query = own_term[..., :feats].reshape(feat_rows, -1)
    grad_key = own_term[:, :, 0, feats : 2 * feats].reshape(feat_rows, -1)
    grad_value = own_term[:, :, 1, feats : 2 * feats].reshape(feat_rows, -1)
    grad_gains = jnp.sum(own_term[..., 2 * feats : 2 * feats + 3], axis=(1, 2))
    grad_first = (
        jnp.sum(wide(w_query) * grad_query, axis=1)
        + jnp.sum(wide(w_key) * grad_key, axis=1)
        + jnp.sum(wide(w_value) * grad_value, axis=1)
    ) / wide(first_gain)
    grad_output = next(out_move)

    scale_one, unit_one = rms_parts(wide(tokens))
    input_grad, _ = rms_back(scale_one, unit_one, gain_one, wide(normed_grad))
    grad_tokens = narrow(residual_grad + input_grad)
    return (
        layer_out,
        grad_tokens,
        grad_query,
        grad_key,
        grad_value,
        grad_output,
        gate_sum,
        up_sum,
        down_sum,
        grad_first,
        grad_gains[:, 0],
        grad_gains[:, 1],
        grad_gains[:, 2],
    )


def solution(mesh):
    placed = (
        P(("seq", "ctx"), None),
        P(("seq", "ctx"), None),
        P(("seq", "ctx"), None),
        P(("seq", "ctx"), None),
        P(("seq", "ctx"), None),
        P("seq", "ctx"),
        P("seq", "ctx"),
        P("ctx", "seq"),
        P(("seq", "ctx")),
        P(("seq", "ctx")),
        P(("seq", "ctx")),
        P(("seq", "ctx")),
        P(),
        P(("seq", "ctx"), None),
    )
    n_seq, n_ctx = mesh.shape["seq"], mesh.shape["ctx"]
    if n_ctx == QUERY_HEAD_COUNT and n_seq == 4:
        body = partial(head_body, n_seq=n_seq, n_ctx=n_ctx)
    else:
        body = context_body
    return jax.shard_map(
        body,
        mesh=mesh,
        in_specs=placed,
        out_specs=(
            P(("seq", "ctx"), None),
            P(("seq", "ctx"), None),
            P(("seq", "ctx"), None),
            P(("seq", "ctx"), None),
            P(("seq", "ctx"), None),
            P(("seq", "ctx"), None),
            P("seq", "ctx"),
            P("seq", "ctx"),
            P("ctx", "seq"),
            P(("seq", "ctx")),
            P(("seq", "ctx")),
            P(("seq", "ctx")),
            P(("seq", "ctx")),
        ),
        check_vma=False,
    )
```

```python
from functools import partial

import jax
import jax.numpy as jnp
from jax import lax
from jax.experimental import pallas as pl
from jax.experimental.pallas import tpu as pltpu
from jax.sharding import PartitionSpec as P

QUERY_HEAD_COUNT = 8
KV_HEADS = 4
HEAD_FEATURES = 256


epsilon = 1e-06
softcap = 50.0
theta = 10000.0
floor_value = -1e30


def rms_scale(signal, weight):
    return signal * lax.rsqrt(jnp.mean(signal * signal, axis=-1, keepdims=True) + epsilon) * weight


def norm_back(signal, weight, upstream):
    outcome, pullback = jax.vjp(rms_scale, signal, weight)
    return pullback(upstream)


def gate_mix(gate_pre, up_pre):
    return jax.nn.gelu(gate_pre, approximate=True) * up_pre


def rotate(signal, positions, head_width):
    row_count = signal.shape[0]
    head_count = signal.shape[1] // head_width
    half_width = head_width // 2
    frequency = theta ** (-2.0 * jnp.arange(half_width, dtype=jnp.float32) / head_width)
    angles = positions.astype(jnp.float32)[:, None] * frequency[None, :]
    cosine = jnp.cos(angles)[:, None, :]
    sine_wave = jnp.sin(angles)[:, None, :]
    shaped = signal.reshape(row_count, head_count, head_width)
    first_half = shaped[:, :, :half_width]
    second = shaped[:, :, half_width:]
    turned = jnp.concatenate(
        [first_half * cosine - second * sine_wave, second * cosine + first_half * sine_wave], axis=2
    )
    return turned.reshape(row_count, head_count * head_width)


def block_scores(head_queries, key_all, key_pos, query_pos, block_rows, score_scale):
    block_keys = key_all.reshape(block_rows, KV_HEADS, HEAD_FEATURES)
    allowed = key_pos[None, :] <= query_pos[:, None]
    unscaled_score = (
        jnp.einsum("fwvi,hwi->wvfh", head_queries, block_keys, preferred_element_type=jnp.float32)
        * score_scale
    )
    bent_score = jnp.tanh(unscaled_score / softcap)
    capped = jnp.where(allowed, softcap * bent_score, floor_value)
    return (block_keys, allowed, bent_score, capped)


def attend(head_queries, key_all, value_all, query_pos, key_pos, score_scale):
    length_total = key_all.shape[0]
    block_count = max(1, length_total // 2048)
    block_rows = length_total // block_count
    row_count = head_queries.shape[0]
    group_size = head_queries.shape[2]

    def total_step(block_index, carried):
        running_max, running_sum = carried
        block_keys, allowed, bent_score, capped = block_scores(
            head_queries, key_all, key_pos, query_pos, block_rows, score_scale
        )
        new_max = jnp.maximum(running_max, jnp.max(capped, axis=-1))
        added = jnp.sum(jnp.where(allowed, jnp.exp(capped - new_max[..., None]), 0.0), axis=-1)
        return (new_max, running_sum * jnp.exp(running_max - new_max) + added)

    start_max = jnp.full((KV_HEADS, group_size, row_count), floor_value, jnp.float32)
    start_sum = jnp.zeros((KV_HEADS, group_size, row_count), jnp.float32)
    running_max, running_sum = lax.fori_loop(0, block_count, total_step, (start_max, start_sum))
    log_total = running_max + jnp.log(running_sum)

    def mix_step(block_index, carried):
        accum, rest_acc = carried
        block_keys, allowed, bent_score, capped = block_scores(
            head_queries, key_all, key_pos, query_pos, block_rows, score_scale
        )
        block_values = value_all.reshape(block_rows, KV_HEADS, HEAD_FEATURES)
        prob_full = jnp.where(allowed, jnp.exp(capped - log_total[..., None]), 0.0)
        lowered_probs = prob_full.astype(jnp.bfloat16)
        remaining_probs = (prob_full - lowered_probs.astype(jnp.float32)).astype(jnp.bfloat16)
        accum = accum + jnp.einsum(
            "xmbe,exk->bxmk", lowered_probs, block_values, preferred_element_type=jnp.float32
        )
        rest_acc = rest_acc + jnp.einsum(
            "xmbe,exk->bxmk", remaining_probs, block_values, preferred_element_type=jnp.float32
        )
        return (accum, rest_acc)

    start_mix = jnp.zeros((row_count, KV_HEADS, group_size, HEAD_FEATURES), jnp.float32)
    full_mixture, rest_acc = lax.fori_loop(0, block_count, mix_step, (start_mix, start_mix))
    exact_mixture = full_mixture + rest_acc
    return (
        log_total,
        full_mixture.reshape(row_count, QUERY_HEAD_COUNT * HEAD_FEATURES),
        exact_mixture,
    )


def attend_back(
    head_queries,
    key_all,
    value_all,
    query_pos,
    key_pos,
    score_scale,
    log_total,
    exact_mixture,
    mixed_grad,
):
    length_total = key_all.shape[0]
    block_count = max(1, length_total // 2048)
    block_rows = length_total // block_count
    row_count = head_queries.shape[0]
    group_size = head_queries.shape[2]
    head_gradient = mixed_grad.reshape(row_count, KV_HEADS, group_size, HEAD_FEATURES)
    row_difference = jnp.einsum("ozlq,ozlq->zlo", head_gradient.astype(jnp.float32), exact_mixture)

    def grad_step(block_index, carried):
        query_acc, key_acc, value_acc = carried
        block_keys, allowed, bent_score, capped = block_scores(
            head_queries, key_all, key_pos, query_pos, block_rows, score_scale
        )
        block_values = value_all.reshape(block_rows, KV_HEADS, HEAD_FEATURES)
        prob_full = jnp.where(allowed, jnp.exp(capped - log_total[..., None]), 0.0)
        lowered_probs = prob_full.astype(jnp.bfloat16)
        value_part = jnp.einsum(
            "zwcv,czwy->vzy", lowered_probs, head_gradient, preferred_element_type=jnp.float32
        )
        prob_grad = jnp.einsum(
            "fwvi,hwi->wvfh", head_gradient, block_values, preferred_element_type=jnp.float32
        )
        lowered_logits = (
            prob_full * (prob_grad - row_difference[..., None]) * (1.0 - bent_score * bent_score)
        ).astype(jnp.bfloat16)
        query_acc = (
            query_acc
            + jnp.einsum(
                "xmbe,exk->bxmk", lowered_logits, block_keys, preferred_element_type=jnp.float32
            )
            * score_scale
        )
        key_part = (
            jnp.einsum(
                "zwcv,czwy->vzy", lowered_logits, head_queries, preferred_element_type=jnp.float32
            )
            * score_scale
        )
        key_acc = key_part.reshape(block_rows, KV_HEADS * HEAD_FEATURES)
        value_acc = value_part.reshape(block_rows, KV_HEADS * HEAD_FEATURES)
        return (query_acc, key_acc, value_acc)

    start = (
        jnp.zeros((row_count, KV_HEADS, group_size, HEAD_FEATURES), jnp.float32),
        jnp.zeros((length_total, KV_HEADS * HEAD_FEATURES), jnp.float32),
        jnp.zeros((length_total, KV_HEADS * HEAD_FEATURES), jnp.float32),
    )
    query_acc, key_acc, value_acc = lax.fori_loop(0, block_count, grad_step, start)
    return (query_acc.reshape(row_count, QUERY_HEAD_COUNT * HEAD_FEATURES), key_acc, value_acc)


def context_body(
    tokens,
    w_query,
    w_key,
    w_value,
    w_output,
    w_gate,
    w_up,
    w_down,
    first_gain,
    second_gain,
    third_gain,
    fourth_gain,
    block_pairs,
    cotangent,
):
    query_full, key_full, value_full, output_full, gain_one, gain_two, gain_three, gain_four = (
        lax.all_gather(w_query, ("seq", "ctx"), axis=0, tiled=True),
        lax.all_gather(w_key, ("seq", "ctx"), axis=0, tiled=True),
        lax.all_gather(w_value, ("seq", "ctx"), axis=0, tiled=True),
        lax.all_gather(w_output, ("seq", "ctx"), axis=0, tiled=True),
        lax.all_gather(first_gain, ("seq", "ctx"), axis=0, tiled=True),
        lax.all_gather(second_gain, ("seq", "ctx"), axis=0, tiled=True),
        lax.all_gather(third_gain, ("seq", "ctx"), axis=0, tiled=True),
        lax.all_gather(fourth_gain, ("seq", "ctx"), axis=0, tiled=True),
    )
    gain_one = gain_one.astype(jnp.float32)
    gain_two = gain_two.astype(jnp.float32)
    gain_three = gain_three.astype(jnp.float32)
    gain_four = gain_four.astype(jnp.float32)
    row_count = tokens.shape[0]
    block_size = row_count // 2
    group_size = QUERY_HEAD_COUNT // KV_HEADS
    score_scale = HEAD_FEATURES ** (-0.5)
    own_pair = lax.dynamic_index_in_dim(block_pairs, lax.axis_index("ctx"), 0, keepdims=False)
    offsets = jnp.arange(block_size, dtype=jnp.int32)
    query_pos = jnp.concatenate(
        [own_pair[0] * block_size + offsets, own_pair[1] * block_size + offsets]
    )
    key_pos = (block_pairs[:, :, None] * block_size + offsets[None, None, :]).reshape(-1)
    residual_in = tokens.astype(jnp.float32)
    normed = rms_scale(residual_in, gain_one).astype(jnp.bfloat16)
    query_proj = jnp.dot(normed, query_full, preferred_element_type=jnp.float32)
    key_proj = jnp.dot(normed, key_full, preferred_element_type=jnp.float32)
    value_proj = jnp.dot(normed, value_full, preferred_element_type=jnp.float32)
    query_low = rotate(query_proj, query_pos, HEAD_FEATURES).astype(jnp.bfloat16)
    key_low = rotate(key_proj, query_pos, HEAD_FEATURES).astype(jnp.bfloat16)
    lowered_values = value_proj.astype(jnp.bfloat16)
    key_all, value_all = (
        lax.all_gather(key_low, "ctx", axis=0, tiled=True),
        lax.all_gather(lowered_values, "ctx", axis=0, tiled=True),
    )
    head_queries = query_low.reshape(row_count, KV_HEADS, group_size, HEAD_FEATURES)
    log_total, full_mixture, exact_mixture = attend(
        head_queries, key_all, value_all, query_pos, key_pos, score_scale
    )
    mixed_low = full_mixture.astype(jnp.bfloat16)
    branch = jnp.dot(mixed_low, output_full, preferred_element_type=jnp.float32)
    residual = residual_in + rms_scale(branch, gain_two)
    feed_input = rms_scale(residual, gain_three).astype(jnp.bfloat16)
    part_gate, part_up, part_down = (
        lax.all_gather(w_gate, "seq", axis=0, tiled=True),
        lax.all_gather(w_up, "seq", axis=0, tiled=True),
        lax.all_gather(w_down, "seq", axis=1, tiled=True),
    )
    feed_all = lax.all_gather(feed_input, "ctx", axis=0, tiled=True)
    gate_pre = jnp.dot(feed_all, part_gate, preferred_element_type=jnp.float32)
    up_pre = jnp.dot(feed_all, part_up, preferred_element_type=jnp.float32)
    hidden = gate_mix(gate_pre, up_pre).astype(jnp.bfloat16)
    feed_out = lax.psum_scatter(
        jnp.dot(hidden, part_down, preferred_element_type=jnp.float32).astype(jnp.bfloat16),
        "ctx",
        scatter_dimension=0,
        tiled=True,
    ).astype(jnp.float32)
    layer_out = (residual + rms_scale(feed_out, gain_four)).astype(jnp.bfloat16)
    upstream = cotangent.astype(jnp.float32)
    feed_grad, fourth_term = norm_back(feed_out, gain_four, upstream)
    feed_low = feed_grad.astype(jnp.bfloat16)
    cotangent_all = lax.all_gather(feed_low, "ctx", axis=0, tiled=True)
    hidden_grad = jnp.einsum(
        "td,fd->tf", cotangent_all, part_down, preferred_element_type=jnp.float32
    )
    outcome, mix_pull = jax.vjp(gate_mix, gate_pre, up_pre)
    gate_grad, up_grad = mix_pull(hidden_grad)
    gate_low = gate_grad.astype(jnp.bfloat16)
    up_low = up_grad.astype(jnp.bfloat16)
    input_part = jnp.einsum(
        "tf,df->td", gate_low, part_gate, preferred_element_type=jnp.float32
    ) + jnp.einsum("tf,df->td", up_low, part_up, preferred_element_type=jnp.float32)
    feed_input_grad = lax.psum_scatter(
        input_part.astype(jnp.bfloat16), "ctx", scatter_dimension=0, tiled=True
    ).astype(jnp.float32)
    gate_term = jnp.einsum("tf,td->fd", gate_low, feed_all, preferred_element_type=jnp.float32)
    up_term = jnp.einsum("tf,td->fd", up_low, feed_all, preferred_element_type=jnp.float32)
    down_term = jnp.einsum("tf,td->fd", hidden, cotangent_all, preferred_element_type=jnp.float32)
    gate_sum, up_sum, down_sum = (
        lax.psum_scatter(
            gate_term.astype(jnp.bfloat16), "seq", scatter_dimension=1, tiled=True
        ).astype(jnp.float32),
        lax.psum_scatter(
            up_term.astype(jnp.bfloat16), "seq", scatter_dimension=1, tiled=True
        ).astype(jnp.float32),
        lax.psum_scatter(
            down_term.astype(jnp.bfloat16), "seq", scatter_dimension=1, tiled=True
        ).astype(jnp.float32),
    )
    middle_grad, third_term = norm_back(residual, gain_three, feed_input_grad)
    residual_grad = upstream + middle_grad
    branch_grad, second_term = norm_back(branch, gain_two, residual_grad)
    branch_low = branch_grad.astype(jnp.bfloat16)
    output_term = jnp.einsum("th,td->hd", mixed_low, branch_low, preferred_element_type=jnp.float32)
    mixed_grad = jnp.einsum(
        "td,hd->th", branch_low, output_full, preferred_element_type=jnp.float32
    ).astype(jnp.bfloat16)
    query_sum, key_acc, value_acc = attend_back(
        head_queries,
        key_all,
        value_all,
        query_pos,
        key_pos,
        score_scale,
        log_total,
        exact_mixture,
        mixed_grad,
    )
    key_own, value_own = (
        lax.psum_scatter(
            key_acc.astype(jnp.bfloat16), "ctx", scatter_dimension=0, tiled=True
        ).astype(jnp.float32),
        lax.psum_scatter(
            value_acc.astype(jnp.bfloat16), "ctx", scatter_dimension=0, tiled=True
        ).astype(jnp.float32),
    )
    query_grad = rotate(query_sum, -query_pos, HEAD_FEATURES).astype(jnp.bfloat16)
    key_grad = rotate(key_own, -query_pos, HEAD_FEATURES).astype(jnp.bfloat16)
    value_grad = value_own.astype(jnp.bfloat16)
    normed_grad = jnp.einsum(
        "th,dh->td", query_grad, query_full, preferred_element_type=jnp.float32
    )
    normed_grad = normed_grad + jnp.einsum(
        "th,dh->td", key_grad, key_full, preferred_element_type=jnp.float32
    )
    normed_grad = normed_grad + jnp.einsum(
        "th,dh->td", value_grad, value_full, preferred_element_type=jnp.float32
    )
    query_term = jnp.einsum("td,th->dh", normed, query_grad, preferred_element_type=jnp.float32)
    key_term = jnp.einsum("td,th->dh", normed, key_grad, preferred_element_type=jnp.float32)
    value_term = jnp.einsum("td,th->dh", normed, value_grad, preferred_element_type=jnp.float32)
    input_grad, first_term = norm_back(residual_in, gain_one, normed_grad)
    grad_tokens = (residual_grad + input_grad).astype(jnp.bfloat16)
    grad_sums = (
        lax.psum_scatter(query_term, ("seq", "ctx"), scatter_dimension=0, tiled=True),
        lax.psum_scatter(key_term, ("seq", "ctx"), scatter_dimension=0, tiled=True),
        lax.psum_scatter(value_term, ("seq", "ctx"), scatter_dimension=0, tiled=True),
        lax.psum_scatter(output_term, ("seq", "ctx"), scatter_dimension=0, tiled=True),
        lax.psum_scatter(first_term, ("seq", "ctx"), scatter_dimension=0, tiled=True),
        lax.psum_scatter(second_term, ("seq", "ctx"), scatter_dimension=0, tiled=True),
        lax.psum_scatter(third_term, ("seq", "ctx"), scatter_dimension=0, tiled=True),
        lax.psum_scatter(fourth_term, ("seq", "ctx"), scatter_dimension=0, tiled=True),
    )
    return (
        layer_out,
        grad_tokens,
        grad_sums[0],
        grad_sums[1],
        grad_sums[2],
        grad_sums[3],
        gate_sum.T,
        up_sum.T,
        down_sum,
        grad_sums[4],
        grad_sums[5],
        grad_sums[6],
        grad_sums[7],
    )


CORES = 2
GELU_IN = 0.7978845608
GELU_CUBE = 0.044715
VMEM_LIMIT = 56 * 2**20


def wide(value):
    return value.astype(jnp.float32)


def narrow(value):
    return value.astype(jnp.bfloat16)


def rms_parts(signal):
    scale = lax.rsqrt(jnp.mean(signal * signal, axis=-1, keepdims=True) + epsilon)
    return scale, signal * scale


def rms_back(scale, unit, weight, upstream):
    weighted = upstream * weight
    mean = jnp.mean(weighted * unit, axis=-1, keepdims=True)
    return scale * (weighted - unit * mean), jnp.sum(upstream * unit, axis=0)


def dot_nn(left, right):
    return jnp.dot(left, right, preferred_element_type=jnp.float32)


def dot_nt(left, right):
    return jnp.einsum("ab,cb->ac", left, right, preferred_element_type=jnp.float32)


def dot_tn(left, right):
    return jnp.einsum("ab,ac->bc", left, right, preferred_element_type=jnp.float32)


def after(value, *others):
    anywhere = pl.BlockSpec(memory_space=pl.ANY)
    return pl.pallas_call(
        lambda *refs: None,
        in_specs=[anywhere] * (1 + len(others)),
        out_specs=anywhere,
        out_shape=jax.ShapeDtypeStruct(value.shape, value.dtype),
        input_output_aliases={0: 0},
    )(value, *others)


def fresh(shape, dtype, *others):
    anywhere = pl.BlockSpec(memory_space=pl.ANY)
    return pl.pallas_call(
        lambda *refs: None,
        in_specs=[anywhere] * len(others),
        out_specs=anywhere,
        out_shape=jax.ShapeDtypeStruct(shape, dtype),
    )(*others)


def lull(*others):
    anywhere = pl.BlockSpec(memory_space=pl.ANY)
    return pl.pallas_call(
        lambda *refs: None,
        in_specs=[anywhere] * len(others),
        out_specs=anywhere,
        out_shape=jax.ShapeDtypeStruct((8, 128), jnp.float32),
        cost_estimate=pl.CostEstimate(flops=10**12, bytes_accessed=0, transcendentals=0),
    )(*others)


class Order:
    def __init__(self):
        self.last = ()

    def pin(self, value, sent=None):
        extra = () if sent is None else (lull(sent),)
        value = after(value, *self.last, *extra)
        self.last = (value,)
        return value

    def mark(self, value):
        self.last = (value,)

    def hold(self, value):
        return after(value, *self.last)


class Moves:
    def __init__(self, n_seq, n_ctx):
        self.n_seq, self.n_ctx = n_seq, n_ctx
        self.line = n_ctx // CORES
        self.seq = lax.axis_index("seq")
        self.ctx = lax.axis_index("ctx")
        self.plane = self.ctx // CORES
        self.core = self.ctx % CORES

    def _send(self, value, move):
        pairs = []
        for s in range(self.n_seq):
            for c in range(self.n_ctx):
                t = move(s, c // CORES, c % CORES)
                pairs.append((s * self.n_ctx + c, t[0] * self.n_ctx + t[1] * CORES + t[2]))
        return lax.ppermute(value, ("seq", "ctx"), pairs)

    def across(self, value, mask):
        return self._send(value, lambda s, z, k: (s ^ mask, z, k))

    def along(self, value, step):
        return self._send(value, lambda s, z, k: (s, (z + step) % self.line, k))

    def plane_swap(self, value, mask):
        return self._send(value, lambda s, z, k: (s, z ^ mask, k))

    def swap(self, value):
        return self._send(value, lambda s, z, k: (s, z, k ^ 1))

    def gather_halves(self, low, high, gate):
        low_near = self.across(low, 2)
        high_near = self.across(high, 1)
        yield None
        low_near, high_near = gate(low_near, low), gate(high_near)
        low_two, high_two = jnp.stack([low, low_near]), jnp.stack([high, high_near])
        low_far = self.across(low_two, 1)
        high_far = self.across(high_two, 2)
        yield None
        yield low_near, high_near, gate(low_far, low_two), gate(high_far)

    def scatter_whole(self, terms, mask, gate):
        other = 3 - mask
        pick = lambda m: lax.dynamic_index_in_dim(terms, self.seq ^ m, 0, False)
        sent = jnp.stack([pick(mask), pick(3)])
        near = self.across(sent, mask)
        yield None
        near = gate(near, sent)
        onward = narrow(wide(pick(other)) + wide(near[1]))
        far = self.across(onward, other)
        yield None
        yield wide(pick(0)) + wide(near[0]) + wide(gate(far, onward))

    def scatter_halves(self, terms, gate):
        half = terms.shape[1] // 2
        low = self.scatter_whole(terms[:, :half], 1, gate)
        high = self.scatter_whole(terms[:, half:], 2, gate)
        for _ in range(2):
            next(low), next(high)
            yield None
        yield jnp.concatenate([next(low), next(high)], axis=0)

    def exchange_line(self, blocks):
        out = fresh(blocks.shape, blocks.dtype, blocks)
        own = lax.dynamic_index_in_dim(blocks, self.plane, 0, False)
        out = lax.dynamic_update_index_in_dim(out, own, self.plane, 0)
        for step in range(1, self.line):
            sent = lax.dynamic_index_in_dim(blocks, (self.plane + step) % self.line, 0, False)
            got = self.along(sent, step)
            out = lax.dynamic_update_index_in_dim(out, got, (self.plane - step) % self.line, 0)
        return out

    def exchange_steps(self, blocks):
        pick = lambda step: lax.dynamic_index_in_dim(blocks, (self.plane + step) % self.line, 0, False)
        return jnp.stack([pick(0)] + [self.along(pick(step), step) for step in range(1, self.line)])

    def transpose_chips(self, value):
        return self._send(value, lambda s, z, k: (z, s, k))

    def exchange_cores(self, blocks):
        own = lax.dynamic_index_in_dim(blocks, self.core, 0, False)
        got = self.swap(lax.dynamic_index_in_dim(blocks, 1 - self.core, 0, False))
        first = self.core == 0
        return jnp.stack([jnp.where(first, own, got), jnp.where(first, got, own)])


ANYWHERE = pl.BlockSpec(memory_space=pl.ANY)


def tile(rows, columns):
    return pl.BlockSpec((rows, columns), lambda i: (i, 0))


def whole(*shape):
    return pl.BlockSpec(shape, lambda i: (0,) * len(shape))


def call(kernel, steps, in_specs, out_specs, out_shape, flops, args, scratch=(), others=()):
    count = len(args)

    def body(*refs):
        kernel(*refs[:count], *refs[count + len(others) :])

    return pl.pallas_call(
        body,
        grid=(steps,),
        in_specs=in_specs + [ANYWHERE] * len(others),
        out_specs=out_specs,
        out_shape=out_shape,
        scratch_shapes=list(scratch),
        compiler_params=pltpu.CompilerParams(vmem_limit_bytes=VMEM_LIMIT),
        cost_estimate=pl.CostEstimate(flops=flops, bytes_accessed=0, transcendentals=0),
    )(*args, *others)


def array(dtype, *shape):
    return jax.ShapeDtypeStruct(shape, dtype)


def mul_nt(left, right):
    return lax.dot_general(
        left, right, (((1,), (1,)), ((), ())), preferred_element_type=jnp.float32
    )


def mul_tn(left, right):
    return lax.dot_general(
        left, right, (((0,), (0,)), ((), ())), preferred_element_type=jnp.float32
    )


def turn_pair(value, cosine, sine):
    half = value.shape[1] // 2
    first, second = value[:, :half], value[:, half:]
    return jnp.concatenate(
        [first * cosine - second * sine, second * cosine + first * sine], axis=1
    )


BF16, F32 = jnp.bfloat16, jnp.float32
TILE = 256


def load(copies, sems):
    started = [pltpu.make_async_copy(a, b, sems.at[i]) for i, (a, b) in enumerate(copies)]
    for copy in started:
        copy.start()
    return started


def whole_copies(seq, pieces, target):
    mask, own, near, far, last = pieces
    rows = own.shape[0]
    near = near.at[pl.ds(0, rows)]
    at = lambda m: target.at[pl.ds(pl.multiple_of((seq ^ m) * rows, 64), rows)]
    other = 3 - mask
    return [(own, at(0)), (near, at(mask)), (far, at(other)), (last, at(3))]


def half_copies(seq, pieces, target):
    own, low_near, high_near, low_far, high_far = pieces
    rows = own.shape[0]
    half = rows // 2
    last = pl.ds(low_near.shape[0] - half, half)
    low_near, high_near = low_near.at[last], high_near.at[last]
    at = lambda m, h: target.at[pl.ds(pl.multiple_of((seq ^ m) * rows + h * half, 32), half)]
    return [
        (own, target.at[pl.ds(pl.multiple_of(seq * rows, 64), rows)]),
        (low_near, at(2, 0)),
        (high_near, at(1, 1)),
        (low_far.at[0], at(1, 0)),
        (low_far.at[1], at(3, 0)),
        (high_far.at[0], at(2, 1)),
        (high_far.at[1], at(3, 1)),
    ]


SCALARS = pl.BlockSpec(memory_space=pltpu.SMEM)


def project_rows(place, tokens, pieces, feats, tables):
    rows, width = tokens.shape
    wide_columns = pieces[0].shape[1]

    def kernel(place_ref, x_ref, own, near_a, near_b, far_a, far_b, cq, sq, cp, sp, *refs):
        normed_ref, query_ref, pair_ref, gains_ref, w_ref, sems = refs

        @pl.when(pl.program_id(0) == 0)
        def _():
            copies = half_copies(place_ref[2], (own, near_a, near_b, far_a, far_b), w_ref)
            for copy in load(copies, sems):
                copy.wait()
            gains_ref[...] = w_ref[:, 2 * feats :].astype(F32).T[:8]

        x = x_ref[...].astype(F32)
        scale = lax.rsqrt(jnp.mean(x * x, axis=-1, keepdims=True) + epsilon)
        normed = (x * scale * gains_ref[0:1]).astype(BF16)
        normed_ref[...] = normed
        both = dot_nn(normed, w_ref[:, : 2 * feats])
        query_ref[...] = turn_pair(both[:, :feats], cq[...], sq[...]).astype(BF16)
        pair_ref[...] = turn_pair(both[:, feats:], cp[...], sp[...]).astype(BF16)

    half = feats // 2
    return call(
        kernel,
        rows // TILE,
        [SCALARS, tile(TILE, width)] + [ANYWHERE] * 5 + [tile(TILE, half)] * 4,
        [tile(TILE, width), tile(TILE, feats), tile(TILE, feats), whole(8, width)],
        [
            array(BF16, rows, width),
            array(BF16, rows, feats),
            array(BF16, rows, feats),
            array(F32, 8, width),
        ],
        4 * rows * width * feats,
        (place, tokens) + pieces + tables,
        [pltpu.VMEM((width, wide_columns), BF16), pltpu.SemaphoreType.DMA((7,))],
    )


def soft_rows(query, keys, place, places):
    bent = jnp.tanh(mul_nt(query, keys) * (HEAD_FEATURES ** (-0.5) / softcap))
    weight = jnp.where(places <= place, jnp.exp(softcap * bent), 0.0)
    return bent, weight / jnp.sum(weight, axis=-1, keepdims=True)


def attend_head(query, key, value, place, places, others):
    rows, feats = query.shape

    def kernel(q_ref, k_ref, v_ref, place_ref, places_ref, out_ref):
        _, probs = soft_rows(q_ref[...], k_ref[...], place_ref[...], places_ref[...])
        out_ref[...] = dot_nn(probs.astype(BF16), v_ref[...]).astype(BF16)

    return call(
        kernel,
        rows // TILE,
        [tile(TILE, feats), whole(rows, feats), whole(rows, feats), tile(TILE, 1), whole(1, rows)],
        [tile(TILE, feats)],
        [array(BF16, rows, feats)],
        4 * rows * rows * feats,
        (query, key, value, place, places),
        (),
        others,
    )[0]


def attend_head_back(place, query, key, value, mixed_grad, spot, spots, cosine, sine, others):
    rows, feats = query.shape
    score_scale = HEAD_FEATURES ** (-0.5)
    steps = rows // TILE

    def kernel(place_ref, q_ref, k_ref, v_ref, g_ref, spot_ref, spots_ref, c_ref, s_ref, *refs):
        dq, own_ref, send_ref, dk, dv = refs
        step = pl.program_id(0)

        @pl.when(step == 0)
        def _():
            dk[...] = jnp.zeros_like(dk)
            dv[...] = jnp.zeros_like(dv)

        query, keys, grad = q_ref[...], k_ref[...], g_ref[...]
        bent, probs = soft_rows(query, keys, spot_ref[...], spots_ref[...])
        prob_grad = mul_nt(grad, v_ref[...])
        delta = jnp.sum(probs * prob_grad, axis=-1, keepdims=True)
        raw = (probs * (prob_grad - delta) * (1.0 - bent * bent)).astype(BF16)
        total = dot_nn(raw, keys) * score_scale
        dq[...] = turn_pair(total, c_ref[...], -s_ref[...]).astype(BF16)
        dk[...] += mul_tn(raw, query) * score_scale
        dv[...] += mul_tn(probs.astype(BF16), grad)

        @pl.when(step == steps - 1)
        def _():
            first = place_ref[1] == 0
            own_ref[...] = jnp.where(first, dk[...], dv[...])
            send_ref[...] = jnp.where(first, dv[...], dk[...])

    return call(
        kernel,
        steps,
        [SCALARS, tile(TILE, feats), whole(rows, feats), whole(rows, feats), tile(TILE, feats)]
        + [tile(TILE, 1), whole(1, rows)]
        + [tile(TILE, feats // 2), tile(TILE, feats // 2)],
        [tile(TILE, feats), whole(rows, feats), whole(rows, feats)],
        [array(BF16, rows, feats), array(F32, rows, feats), array(F32, rows, feats)],
        10 * rows * rows * feats,
        (place, query, key, value, mixed_grad, spot, spots, cosine, sine),
        [pltpu.VMEM((rows, feats), F32)] * 2,
        others,
    )


OUT_ORDER = ((0, 0), (0, 2), (0, 1), (0, 3), (2, 0), (2, 2), (1, 1), (1, 3)) + (
    ((1, 0), (1, 2), (3, 0), (3, 2), (2, 1), (2, 3), (3, 1), (3, 3))
)


def branch_rows(place, mixed, own, other, tokens, gain_two, gain_three):
    heads, rows, feats = mixed.shape
    blocks, out_rows, width = own.shape
    per_head = feats // (CORES * out_rows)
    own_rows = TILE // CORES
    planes = 4

    def kernel(
        place_ref,
        m_ref,
        own_ref,
        other_ref,
        x_ref,
        two_ref,
        three_ref,
        out_ref,
        mine_ref,
        full_ref,
        w_ref,
        sems,
        full_sem,
    ):
        step = pl.program_id(0)
        plane, core, seq = place_ref[0], place_ref[1], place_ref[2]
        keep = pltpu.make_async_copy(w_ref, full_ref, full_sem)

        @pl.when(step == 0)
        def _():
            copies = []
            for i, (m, x) in enumerate(OUT_ORDER):
                at = (seq ^ m) * planes + (plane ^ x)
                copies.append((own_ref.at[i], w_ref.at[at, core]))
                copies.append((other_ref.at[i], w_ref.at[at, 1 - core]))
            for copy in load(copies, sems):
                copy.wait()
            keep.start()

        branch = 0.0
        for h in range(heads):
            head = w_ref[h * per_head : (h + 1) * per_head].reshape(feats, width)
            branch += dot_nn(m_ref[h], head)

        @pl.when(step == plane)
        def _():
            mine_ref[...] = jnp.where(core == 0, branch[:own_rows], branch[own_rows:])

        scale = lax.rsqrt(jnp.mean(branch * branch, axis=-1, keepdims=True) + epsilon)
        residual = x_ref[...].astype(F32) + branch * scale * two_ref[...]
        scale = lax.rsqrt(jnp.mean(residual * residual, axis=-1, keepdims=True) + epsilon)
        out_ref[...] = (residual * scale * three_ref[...]).astype(BF16)

        @pl.when(step == rows // TILE - 1)
        def _():
            keep.wait()

    return call(
        kernel,
        rows // TILE,
        [
            SCALARS,
            pl.BlockSpec((heads, TILE, feats), lambda i: (0, i, 0)),
            ANYWHERE,
            ANYWHERE,
            tile(TILE, width),
            whole(1, width),
            whole(1, width),
        ],
        [tile(TILE, width), whole(own_rows, width), ANYWHERE],
        [
            array(BF16, rows, width),
            array(F32, own_rows, width),
            array(BF16, blocks, CORES, out_rows, width),
        ],
        2 * heads * rows * feats * width,
        (place, mixed, own, other, tokens, gain_two, gain_three),
        [
            pltpu.VMEM((blocks, CORES, out_rows, width), BF16),
            pltpu.SemaphoreType.DMA((2 * blocks,)),
            pltpu.SemaphoreType.DMA,
        ],
    )


def feed_open(place, feed, gate_pieces, up_pieces):
    rows, width = feed.shape
    units = gate_pieces[0].shape[1]

    def kernel(place_ref, x_ref, *refs):
        gates, ups = refs[:4], refs[4:8]
        hidden_ref, gate_ref, up_ref, gw_ref, uw_ref, gate_sems, up_sems = refs[8:]
        seq = place_ref[2]
        gate_copies = whole_copies(seq, (1,) + gates, gw_ref)
        up_copies = whole_copies(seq, (2,) + ups, uw_ref)
        first = pl.program_id(0) == 0

        @pl.when(first)
        def _():
            started = load(gate_copies, gate_sems)
            load(up_copies, up_sems)
            for copy in started:
                copy.wait()

        x = x_ref[...]
        gate = dot_nn(x, gw_ref[...])

        @pl.when(first)
        def _():
            for i, (a, b) in enumerate(up_copies):
                pltpu.make_async_copy(a, b, up_sems.at[i]).wait()

        up = dot_nn(x, uw_ref[...])
        square = gate * gate
        bend = jnp.tanh(GELU_IN * (gate + GELU_CUBE * square * gate))
        half = 0.5 * (1.0 + bend)
        gelu = half * gate
        slope = half + 0.5 * gate * (1.0 - bend * bend) * (
            GELU_IN + 3.0 * GELU_IN * GELU_CUBE * square
        )
        hidden_ref[...] = (gelu * up).astype(BF16)
        gate_ref[...] = (up * slope).astype(BF16)
        up_ref[...] = gelu.astype(BF16)

    return call(
        kernel,
        rows // TILE,
        [SCALARS, tile(TILE, width)] + [ANYWHERE] * 8,
        [tile(TILE, units)] * 3,
        [array(BF16, rows, units)] * 3,
        4 * rows * width * units,
        (place, feed) + gate_pieces + up_pieces,
        [pltpu.VMEM((width, units), BF16)] * 2 + [pltpu.SemaphoreType.DMA((4,))] * 2,
    )


def feed_close(place, hidden, down_pieces):
    rows, units = hidden.shape
    width = down_pieces[0].shape[0] * 4

    def kernel(place_ref, x_ref, *refs):
        out_ref, dw_ref, sems = refs[5:]

        @pl.when(pl.program_id(0) == 0)
        def _():
            for copy in load(half_copies(place_ref[2], refs[:5], dw_ref), sems):
                copy.wait()

        out_ref[...] = mul_nt(x_ref[...], dw_ref[...]).astype(BF16)

    return call(
        kernel,
        rows // TILE,
        [SCALARS, tile(TILE, units)] + [ANYWHERE] * 5,
        [tile(TILE, width)],
        [array(BF16, rows, width)],
        2 * rows * width * units,
        (place, hidden) + down_pieces,
        [pltpu.VMEM((width, units), BF16), pltpu.SemaphoreType.DMA((7,))],
    )[0]


def mixed_back(branch, w_full):
    rows, width = branch.shape
    heads = QUERY_HEAD_COUNT
    feats = w_full.shape[0] // heads

    def kernel(b_ref, w_ref, out_ref):
        out_ref[0] = mul_nt(b_ref[...], w_ref[...]).astype(BF16)

    return call(
        kernel,
        heads,
        [whole(rows, width), tile(feats, width)],
        [pl.BlockSpec((1, rows, feats), lambda i: (i, 0, 0))],
        [array(BF16, heads, rows, feats)],
        2 * rows * width * heads * feats,
        (branch, w_full),
    )[0]


def feed_back(place, grad, gate_factor, up_factor, gate_pieces, up_pieces, down_pieces):
    rows, width = grad.shape
    units = gate_factor.shape[1]

    def kernel(place_ref, g_ref, gf_ref, uf_ref, *refs):
        gates, ups, downs = refs[:4], refs[4:8], refs[8:13]
        gate_ref, up_ref, out_ref, gw_ref, uw_ref, dw_ref, gate_sems, up_sems, down_sems = refs[13:]
        seq = place_ref[2]
        gate_copies = whole_copies(seq, (1,) + gates, gw_ref)
        up_copies = whole_copies(seq, (2,) + ups, uw_ref)
        first = pl.program_id(0) == 0

        @pl.when(first)
        def _():
            started = load(half_copies(seq, downs, dw_ref), down_sems)
            load(gate_copies, gate_sems)
            load(up_copies, up_sems)
            for copy in started:
                copy.wait()

        hidden_grad = dot_nn(g_ref[...], dw_ref[...])
        gate_low = (hidden_grad * gf_ref[...].astype(F32)).astype(BF16)
        up_low = (hidden_grad * uf_ref[...].astype(F32)).astype(BF16)
        gate_ref[...] = gate_low
        up_ref[...] = up_low

        @pl.when(first)
        def _():
            for copies, sems in ((gate_copies, gate_sems), (up_copies, up_sems)):
                for i, (a, b) in enumerate(copies):
                    pltpu.make_async_copy(a, b, sems.at[i]).wait()

        out_ref[...] = (mul_nt(gate_low, gw_ref[...]) + mul_nt(up_low, uw_ref[...])).astype(BF16)

    return call(
        kernel,
        rows // TILE,
        [SCALARS, tile(TILE, width), tile(TILE, units), tile(TILE, units)] + [ANYWHERE] * 13,
        [tile(TILE, units), tile(TILE, units), tile(TILE, width)],
        [array(BF16, rows, units), array(BF16, rows, units), array(BF16, rows, width)],
        6 * rows * width * units,
        (place, grad, gate_factor, up_factor) + gate_pieces + up_pieces + down_pieces,
        [pltpu.VMEM((width, units), BF16)] * 3
        + [pltpu.SemaphoreType.DMA((4,))] * 2
        + [pltpu.SemaphoreType.DMA((7,))],
    )


def normed_back(place, query_grad, own, other, cosine, sine, pieces):
    rows, feats = query_grad.shape
    width, wide_columns = pieces[0].shape[0] * 4, pieces[0].shape[1]

    def kernel(place_ref, q_ref, own_ref, other_ref, c_ref, s_ref, *refs):
        both_ref, out_ref, w_ref, sems = refs[5:]

        @pl.when(pl.program_id(0) == 0)
        def _():
            for copy in load(half_copies(place_ref[2], refs[:5], w_ref), sems):
                copy.wait()

        pair = turn_pair(own_ref[...] + other_ref[...], c_ref[...], -s_ref[...]).astype(BF16)
        both_ref[:, :feats] = q_ref[...]
        both_ref[:, feats:] = pair
        out_ref[...] = mul_nt(both_ref[...], w_ref[:, : 2 * feats]).astype(BF16)

    return call(
        kernel,
        rows // TILE,
        [SCALARS] + [tile(TILE, feats)] * 3 + [tile(TILE, feats // 2)] * 2 + [ANYWHERE] * 5,
        [tile(TILE, 2 * feats), tile(TILE, width)],
        [array(BF16, rows, 2 * feats), array(BF16, rows, width)],
        4 * rows * feats * width,
        (place, query_grad, own, other, cosine, sine) + pieces,
        [pltpu.VMEM((width, wide_columns), BF16), pltpu.SemaphoreType.DMA((7,))],
    )


def own_grads(place, own, other, weights, gain):
    line, rows, columns = own.shape
    feats = HEAD_FEATURES

    def kernel(place_ref, own_ref, other_ref, wq, wk, wv, g_ref, dq, dk, dv, gains_ref, first_ref):
        front = place_ref[1] == 0
        total, first = 0.0, 0.0
        for step in range(line):
            plane = (place_ref[0] + (line - step)) % line
            a, b = own_ref[step].astype(F32), other_ref[step].astype(F32)
            pair = jnp.where(front, a, b), jnp.where(front, b, a)
            total += a[:, 2 * feats :] + b[:, 2 * feats :]
            at = pl.ds(pl.multiple_of(plane * feats, feats), feats)
            for core, (out, w) in enumerate(((dk, wk), (dv, wv))):
                value = pair[core][:, feats : 2 * feats]
                out[:, at] = value
                first += jnp.sum(w[:, at].astype(F32) * value, axis=1, keepdims=True)
                spot = pl.ds(pl.multiple_of((plane * CORES + core) * feats, feats), feats)
                value = pair[core][:, :feats]
                dq[:, spot] = value
                first += jnp.sum(wq[:, spot].astype(F32) * value, axis=1, keepdims=True)
        gains_ref[...] = total
        first_ref[...] = first / g_ref[...].astype(F32)

    shapes = [w.shape for w in weights] + [(rows, columns - 2 * feats), (rows, 1)]
    return call(
        kernel,
        1,
        [SCALARS, whole(*own.shape), whole(*own.shape)] + [whole(*w.shape) for w in weights] + [whole(rows, 1)],
        [whole(*s) for s in shapes],
        [array(F32, *s) for s in shapes],
        0,
        (place, own, other) + weights + (gain,),
    )


def weight_grad(left, right, block, others, more=None):
    rows, width = left.shape
    columns = right.shape[1]
    total = columns + (0 if more is None else more.shape[1])

    def kernel(left_ref, right_ref, *refs):
        refs[-1][:, :columns] = mul_tn(left_ref[...], right_ref[...]).astype(BF16)
        if more is not None:
            refs[-1][:, columns:] = refs[0][...]

    extra = () if more is None else (more,)
    return call(
        kernel,
        width // block,
        [pl.BlockSpec((rows, block), lambda i: (0, i)), whole(rows, columns)]
        + [tile(block, v.shape[1]) for v in extra],
        [tile(block, total)],
        [array(BF16, width, total)],
        2 * rows * width * columns,
        (left, right) + extra,
        (),
        others,
    )[0]


def head_body(
    tokens,
    w_query,
    w_key,
    w_value,
    w_output,
    w_gate,
    w_up,
    w_down,
    first_gain,
    second_gain,
    third_gain,
    fourth_gain,
    block_pairs,
    cotangent,
    n_seq,
    n_ctx,
):
    moves = Moves(n_seq, n_ctx)
    order = Order()
    pin, hold = order.pin, order.hold
    line = moves.line
    core_zero = moves.core == 0
    rows, width = tokens.shape
    feat_rows = w_query.shape[0]
    out_rows = w_output.shape[0]
    feats = HEAD_FEATURES
    pad = 128
    gather = lambda v: lax.all_gather(v, "ctx", axis=0, tiled=True)
    scatter = lambda v: lax.psum_scatter(v, "ctx", scatter_dimension=0, tiled=True)

    place = jnp.stack([moves.plane, moves.core, moves.seq]).astype(jnp.int32)
    block = w_gate.shape[0]
    half = block // 2

    out_near = moves.plane_swap(w_output, 2)
    gains_in = jnp.stack([first_gain, second_gain, third_gain, fourth_gain], axis=1)
    gains_in = jnp.pad(gains_in, ((0, 0), (0, pad - 4)))
    by_head = jnp.concatenate(
        [
            w_query.reshape(feat_rows, line, CORES, feats),
            jnp.stack(
                [
                    w_key.reshape(feat_rows, line, feats),
                    w_value.reshape(feat_rows, line, feats),
                ],
                axis=2,
            ),
            jnp.broadcast_to(gains_in[:, None, None, :], (feat_rows, line, CORES, pad)),
        ],
        axis=3,
    ).transpose(2, 1, 0, 3)
    by_plane = moves.exchange_cores(by_head).transpose(1, 0, 2, 3)
    down_own = w_down.T
    near_x = moves.across(jnp.concatenate([w_gate, down_own[half:]]), 1)
    near_y = moves.across(jnp.concatenate([w_up, down_own[:half]]), 2)
    own_columns = moves.exchange_line(by_plane).reshape(n_ctx * feat_rows, 2 * feats + pad)
    own_columns = pin(own_columns, by_plane)
    tokens_in = hold(tokens)
    tokens_all = gather(tokens_in)
    columns_move = moves.gather_halves(own_columns[:half], own_columns[half:], pin)
    next(columns_move)
    near_x, near_y = pin(near_x), pin(near_y)
    out_two = pin(jnp.stack([w_output, pin(out_near)]))
    next(columns_move)

    block_size = rows // 2
    offsets = jnp.arange(block_size, dtype=jnp.int32)
    pos = (hold(block_pairs)[:, :, None] * block_size + offsets[None, None, :]).reshape(-1)
    spot, spots = pos[:, None], pos[None, :]
    frequency = theta ** (-2.0 * jnp.arange(feats // 2, dtype=jnp.float32) / feats)
    angles = wide(pos)[:, None] * frequency[None, :]
    cosine, sine = pin(jnp.cos(angles)), pin(jnp.sin(angles))
    pair_cosine = pin(jnp.where(core_zero, cosine, 1.0))
    pair_sine = pin(jnp.where(core_zero, sine, 0.0))
    tables = (cosine, sine, pair_cosine, pair_sine)

    columns = (own_columns,) + next(columns_move)
    gate_far = moves.across(hold(w_gate), 2)
    up_far = moves.across(hold(w_up), 1)
    tokens_all = pin(tokens_all, tokens_in)
    out_two = hold(out_two)
    out_far = moves.plane_swap(out_two, 1)

    normed, query, pair, gains = project_rows(place, tokens_all, columns, feats, tables)
    gain_one, gain_two, gain_three, gain_four = (gains[i : i + 1] for i in range(4))
    pair_other = moves.swap(pair)
    order.mark(pair)
    pair_other = pin(pair_other, pair)
    key = jnp.where(core_zero, pair, pair_other)
    value = jnp.where(core_zero, pair_other, pair)
    mixed = pin(attend_head(query, key, value, spot, spots, order.last))
    mixed_all = lax.all_gather(mixed, "ctx", axis=0)

    out_far = pin(out_far, out_two)
    out_move = moves.gather_halves(out_two, out_far, pin)
    next(out_move)
    next(out_move)
    gate_far, up_far = pin(gate_far), pin(up_far)
    low_near, high_near, low_far, high_far = next(out_move)
    gate_last = moves.across(hold(near_x[:block]), 2)
    up_last = moves.across(hold(near_y[:block]), 1)
    out_own = jnp.concatenate(
        [out_two, out_far, low_near, high_near, *(v.reshape(4, *v.shape[2:]) for v in (low_far, high_far))]
    )
    out_own = pin(out_own)
    out_other = moves.swap(out_own)
    low_two = pin(jnp.stack([down_own[:half], near_y[block:]]))
    high_two = pin(jnp.stack([down_own[half:], near_x[block:]]))
    out_other = pin(out_other, out_own)
    mixed_all = pin(mixed_all, mixed)
    feed_all, branch, w_full = branch_rows(
        place, mixed_all, out_own, out_other, tokens_all, gain_two, gain_three
    )
    order.mark(branch)
    gate_pieces = (w_gate, near_x, gate_far, pin(gate_last))
    up_pieces = (w_up, near_y, up_far, pin(up_last))
    down_low, down_high = moves.across(hold(low_two), 1), moves.across(hold(high_two), 2)
    hidden, gate_factor, up_factor = feed_open(place, feed_all, gate_pieces, up_pieces)
    order.mark(hidden)
    down_pieces = (down_own, near_y, near_x, pin(down_low), pin(down_high))
    feed_part = feed_close(place, hidden, down_pieces)
    order.mark(feed_part)
    feed_out = scatter(feed_part)

    scale_two, unit_two = rms_parts(hold(branch))
    residual = wide(tokens) + unit_two * gain_two
    scale_three, unit_three = rms_parts(residual)
    unit_two, unit_three, residual = pin(unit_two), pin(unit_three), pin(residual)

    upstream = wide(cotangent)
    feed_out = pin(feed_out, feed_part)
    scale_four, unit_four = rms_parts(wide(feed_out))
    layer_out = narrow(residual + unit_four * gain_four)
    feed_grad, fourth_term = rms_back(scale_four, unit_four, gain_four, upstream)
    feed_low = pin(narrow(feed_grad))
    grad_all = pin(gather(feed_low), feed_low)
    gate_low, up_low, input_part = feed_back(
        place, grad_all, gate_factor, up_factor, gate_pieces, up_pieces, down_pieces
    )
    order.mark(input_part)
    feed_input_grad = scatter(input_part)
    shape = (n_seq, block, gate_low.shape[1])
    down_term = weight_grad(grad_all, hidden, 384, order.last).reshape(shape)
    order.mark(down_term)
    down_move = moves.scatter_halves(down_term, pin)
    next(down_move)
    gate_term = weight_grad(feed_all, gate_low, 384, order.last).reshape(shape)
    order.mark(gate_term)
    gate_move = moves.scatter_whole(gate_term, 1, pin)
    next(gate_move)
    up_term = weight_grad(feed_all, up_low, 384, order.last).reshape(shape)
    order.mark(up_term)
    up_move = moves.scatter_whole(up_term, 2, pin)
    next(up_move)
    feed_input_grad = wide(pin(feed_input_grad, input_part))
    middle_grad, third_term = rms_back(scale_three, unit_three, gain_three, feed_input_grad)
    residual_grad = upstream + middle_grad
    branch_grad, second_term = rms_back(scale_two, unit_two, gain_two, residual_grad)
    branch_low = pin(narrow(branch_grad))
    branch_all = gather(branch_low)

    mixed_own = pin(mixed_back(branch_low, w_full.reshape(-1, width)))
    mixed_grad = lax.all_to_all(mixed_own, "ctx", split_axis=0, concat_axis=0, tiled=True)
    next(down_move)
    mixed_grad = pin(mixed_grad.reshape(-1, feats))
    query_grad, pair_own, pair_send = attend_head_back(
        place, query, key, value, mixed_grad, spot, spots, cosine, sine, order.last
    )
    order.mark(query_grad)
    pair_other = moves.swap(pair_send)
    pair_other = pin(pair_other)
    qkv_grad, normed_part = normed_back(
        place, query_grad, pair_own, pair_other, pair_cosine, pair_sine, columns
    )
    order.mark(normed_part)
    normed_grad = scatter(normed_part)

    terms = jnp.stack([second_term, third_term, fourth_term])
    terms = narrow(jnp.pad(terms, ((0, pad - 3), (0, 0))).T)
    qkv_term = weight_grad(normed, qkv_grad, 384, order.last, terms)
    order.mark(qkv_term)
    down_sum = next(down_move).T
    qkv_move = moves.scatter_halves(qkv_term.reshape(n_seq, width // n_seq, -1), pin)
    next(qkv_move)
    branch_all = pin(branch_all, branch_low)
    output_term = weight_grad(mixed, branch_all, feats, order.last)
    order.mark(output_term)
    out_term = output_term.reshape(CORES, CORES, out_rows, width).transpose(1, 0, 2, 3)
    out_term = moves.exchange_cores(out_term).reshape(line, out_rows, width)
    next(qkv_move)
    next(gate_move), next(up_move)
    out_move = moves.scatter_whole(pin(out_term), 2, pin)
    next(out_move)
    own_term = pin(narrow(next(qkv_move))).reshape(line, CORES, feat_rows, 2 * feats + pad)
    own_term = pin(moves.exchange_steps(own_term))
    own_other = moves.swap(lax.dynamic_index_in_dim(own_term, 1 - moves.core, 1, False))
    own_term = lax.dynamic_index_in_dim(own_term, moves.core, 1, False)
    next(out_move)
    normed_grad = pin(normed_grad)
    scale_one, unit_one = rms_parts(wide(tokens))
    input_grad, _ = rms_back(scale_one, unit_one, gain_one, wide(normed_grad))
    grad_tokens = pin(narrow(residual_grad + input_grad))
    grad_output = moves.transpose_chips(narrow(next(out_move)))
    gate_sum, up_sum = next(gate_move), next(up_move)
    grad_query, grad_key, grad_value, grad_gains, grad_first = own_grads(
        place, own_term, pin(own_other), (w_query, w_key, w_value), first_gain[:, None]
    )
    grad_output = wide(pin(grad_output))
    return (
        layer_out,
        grad_tokens,
        grad_query,
        grad_key,
        grad_value,
        grad_output,
        gate_sum,
        up_sum,
        down_sum,
        grad_first[:, 0],
        grad_gains[:, 0],
        grad_gains[:, 1],
        grad_gains[:, 2],
    )


def solution(mesh):
    placed = (
        P(("seq", "ctx"), None),
        P(("seq", "ctx"), None),
        P(("seq", "ctx"), None),
        P(("seq", "ctx"), None),
        P(("seq", "ctx"), None),
        P("seq", "ctx"),
        P("seq", "ctx"),
        P("ctx", "seq"),
        P(("seq", "ctx")),
        P(("seq", "ctx")),
        P(("seq", "ctx")),
        P(("seq", "ctx")),
        P(),
        P(("seq", "ctx"), None),
    )
    n_seq, n_ctx = mesh.shape["seq"], mesh.shape["ctx"]
    if n_ctx == QUERY_HEAD_COUNT and n_seq == 4:
        body = partial(head_body, n_seq=n_seq, n_ctx=n_ctx)
    else:
        body = context_body
    return jax.shard_map(
        body,
        mesh=mesh,
        in_specs=placed,
        out_specs=(
            P(("seq", "ctx"), None),
            P(("seq", "ctx"), None),
            P(("seq", "ctx"), None),
            P(("seq", "ctx"), None),
            P(("seq", "ctx"), None),
            P(("seq", "ctx"), None),
            P("seq", "ctx"),
            P("seq", "ctx"),
            P("ctx", "seq"),
            P(("seq", "ctx")),
            P(("seq", "ctx")),
            P(("seq", "ctx")),
            P(("seq", "ctx")),
        ),
        check_vma=False,
    )
```

```python
from functools import partial

import jax
import jax.numpy as jnp
from jax import lax
from jax.experimental import pallas as pl
from jax.experimental.pallas import tpu as pltpu
from jax.sharding import PartitionSpec as P

QUERY_HEAD_COUNT = 8
KV_HEADS = 4
HEAD_FEATURES = 256


epsilon = 1e-06
softcap = 50.0
theta = 10000.0
floor_value = -1e30


def rms_scale(signal, weight):
    return signal * lax.rsqrt(jnp.mean(signal * signal, axis=-1, keepdims=True) + epsilon) * weight


def norm_back(signal, weight, upstream):
    outcome, pullback = jax.vjp(rms_scale, signal, weight)
    return pullback(upstream)


def gate_mix(gate_pre, up_pre):
    return jax.nn.gelu(gate_pre, approximate=True) * up_pre


def rotate(signal, positions, head_width):
    row_count = signal.shape[0]
    head_count = signal.shape[1] // head_width
    half_width = head_width // 2
    frequency = theta ** (-2.0 * jnp.arange(half_width, dtype=jnp.float32) / head_width)
    angles = positions.astype(jnp.float32)[:, None] * frequency[None, :]
    cosine = jnp.cos(angles)[:, None, :]
    sine_wave = jnp.sin(angles)[:, None, :]
    shaped = signal.reshape(row_count, head_count, head_width)
    first_half = shaped[:, :, :half_width]
    second = shaped[:, :, half_width:]
    turned = jnp.concatenate(
        [first_half * cosine - second * sine_wave, second * cosine + first_half * sine_wave], axis=2
    )
    return turned.reshape(row_count, head_count * head_width)


def block_scores(head_queries, key_all, key_pos, query_pos, block_rows, score_scale):
    block_keys = key_all.reshape(block_rows, KV_HEADS, HEAD_FEATURES)
    allowed = key_pos[None, :] <= query_pos[:, None]
    unscaled_score = (
        jnp.einsum("fwvi,hwi->wvfh", head_queries, block_keys, preferred_element_type=jnp.float32)
        * score_scale
    )
    bent_score = jnp.tanh(unscaled_score / softcap)
    capped = jnp.where(allowed, softcap * bent_score, floor_value)
    return (block_keys, allowed, bent_score, capped)


def attend(head_queries, key_all, value_all, query_pos, key_pos, score_scale):
    length_total = key_all.shape[0]
    block_count = max(1, length_total // 2048)
    block_rows = length_total // block_count
    row_count = head_queries.shape[0]
    group_size = head_queries.shape[2]

    def total_step(block_index, carried):
        running_max, running_sum = carried
        block_keys, allowed, bent_score, capped = block_scores(
            head_queries, key_all, key_pos, query_pos, block_rows, score_scale
        )
        new_max = jnp.maximum(running_max, jnp.max(capped, axis=-1))
        added = jnp.sum(jnp.where(allowed, jnp.exp(capped - new_max[..., None]), 0.0), axis=-1)
        return (new_max, running_sum * jnp.exp(running_max - new_max) + added)

    start_max = jnp.full((KV_HEADS, group_size, row_count), floor_value, jnp.float32)
    start_sum = jnp.zeros((KV_HEADS, group_size, row_count), jnp.float32)
    running_max, running_sum = lax.fori_loop(0, block_count, total_step, (start_max, start_sum))
    log_total = running_max + jnp.log(running_sum)

    def mix_step(block_index, carried):
        accum, rest_acc = carried
        block_keys, allowed, bent_score, capped = block_scores(
            head_queries, key_all, key_pos, query_pos, block_rows, score_scale
        )
        block_values = value_all.reshape(block_rows, KV_HEADS, HEAD_FEATURES)
        prob_full = jnp.where(allowed, jnp.exp(capped - log_total[..., None]), 0.0)
        lowered_probs = prob_full.astype(jnp.bfloat16)
        remaining_probs = (prob_full - lowered_probs.astype(jnp.float32)).astype(jnp.bfloat16)
        accum = accum + jnp.einsum(
            "xmbe,exk->bxmk", lowered_probs, block_values, preferred_element_type=jnp.float32
        )
        rest_acc = rest_acc + jnp.einsum(
            "xmbe,exk->bxmk", remaining_probs, block_values, preferred_element_type=jnp.float32
        )
        return (accum, rest_acc)

    start_mix = jnp.zeros((row_count, KV_HEADS, group_size, HEAD_FEATURES), jnp.float32)
    full_mixture, rest_acc = lax.fori_loop(0, block_count, mix_step, (start_mix, start_mix))
    exact_mixture = full_mixture + rest_acc
    return (
        log_total,
        full_mixture.reshape(row_count, QUERY_HEAD_COUNT * HEAD_FEATURES),
        exact_mixture,
    )


def attend_back(
    head_queries,
    key_all,
    value_all,
    query_pos,
    key_pos,
    score_scale,
    log_total,
    exact_mixture,
    mixed_grad,
):
    length_total = key_all.shape[0]
    block_count = max(1, length_total // 2048)
    block_rows = length_total // block_count
    row_count = head_queries.shape[0]
    group_size = head_queries.shape[2]
    head_gradient = mixed_grad.reshape(row_count, KV_HEADS, group_size, HEAD_FEATURES)
    row_difference = jnp.einsum("ozlq,ozlq->zlo", head_gradient.astype(jnp.float32), exact_mixture)

    def grad_step(block_index, carried):
        query_acc, key_acc, value_acc = carried
        block_keys, allowed, bent_score, capped = block_scores(
            head_queries, key_all, key_pos, query_pos, block_rows, score_scale
        )
        block_values = value_all.reshape(block_rows, KV_HEADS, HEAD_FEATURES)
        prob_full = jnp.where(allowed, jnp.exp(capped - log_total[..., None]), 0.0)
        lowered_probs = prob_full.astype(jnp.bfloat16)
        value_part = jnp.einsum(
            "zwcv,czwy->vzy", lowered_probs, head_gradient, preferred_element_type=jnp.float32
        )
        prob_grad = jnp.einsum(
            "fwvi,hwi->wvfh", head_gradient, block_values, preferred_element_type=jnp.float32
        )
        lowered_logits = (
            prob_full * (prob_grad - row_difference[..., None]) * (1.0 - bent_score * bent_score)
        ).astype(jnp.bfloat16)
        query_acc = (
            query_acc
            + jnp.einsum(
                "xmbe,exk->bxmk", lowered_logits, block_keys, preferred_element_type=jnp.float32
            )
            * score_scale
        )
        key_part = (
            jnp.einsum(
                "zwcv,czwy->vzy", lowered_logits, head_queries, preferred_element_type=jnp.float32
            )
            * score_scale
        )
        key_acc = key_part.reshape(block_rows, KV_HEADS * HEAD_FEATURES)
        value_acc = value_part.reshape(block_rows, KV_HEADS * HEAD_FEATURES)
        return (query_acc, key_acc, value_acc)

    start = (
        jnp.zeros((row_count, KV_HEADS, group_size, HEAD_FEATURES), jnp.float32),
        jnp.zeros((length_total, KV_HEADS * HEAD_FEATURES), jnp.float32),
        jnp.zeros((length_total, KV_HEADS * HEAD_FEATURES), jnp.float32),
    )
    query_acc, key_acc, value_acc = lax.fori_loop(0, block_count, grad_step, start)
    return (query_acc.reshape(row_count, QUERY_HEAD_COUNT * HEAD_FEATURES), key_acc, value_acc)


def context_body(
    tokens,
    w_query,
    w_key,
    w_value,
    w_output,
    w_gate,
    w_up,
    w_down,
    first_gain,
    second_gain,
    third_gain,
    fourth_gain,
    block_pairs,
    cotangent,
):
    query_full, key_full, value_full, output_full, gain_one, gain_two, gain_three, gain_four = (
        lax.all_gather(w_query, ("seq", "ctx"), axis=0, tiled=True),
        lax.all_gather(w_key, ("seq", "ctx"), axis=0, tiled=True),
        lax.all_gather(w_value, ("seq", "ctx"), axis=0, tiled=True),
        lax.all_gather(w_output, ("seq", "ctx"), axis=0, tiled=True),
        lax.all_gather(first_gain, ("seq", "ctx"), axis=0, tiled=True),
        lax.all_gather(second_gain, ("seq", "ctx"), axis=0, tiled=True),
        lax.all_gather(third_gain, ("seq", "ctx"), axis=0, tiled=True),
        lax.all_gather(fourth_gain, ("seq", "ctx"), axis=0, tiled=True),
    )
    gain_one = gain_one.astype(jnp.float32)
    gain_two = gain_two.astype(jnp.float32)
    gain_three = gain_three.astype(jnp.float32)
    gain_four = gain_four.astype(jnp.float32)
    row_count = tokens.shape[0]
    block_size = row_count // 2
    group_size = QUERY_HEAD_COUNT // KV_HEADS
    score_scale = HEAD_FEATURES ** (-0.5)
    own_pair = lax.dynamic_index_in_dim(block_pairs, lax.axis_index("ctx"), 0, keepdims=False)
    offsets = jnp.arange(block_size, dtype=jnp.int32)
    query_pos = jnp.concatenate(
        [own_pair[0] * block_size + offsets, own_pair[1] * block_size + offsets]
    )
    key_pos = (block_pairs[:, :, None] * block_size + offsets[None, None, :]).reshape(-1)
    residual_in = tokens.astype(jnp.float32)
    normed = rms_scale(residual_in, gain_one).astype(jnp.bfloat16)
    query_proj = jnp.dot(normed, query_full, preferred_element_type=jnp.float32)
    key_proj = jnp.dot(normed, key_full, preferred_element_type=jnp.float32)
    value_proj = jnp.dot(normed, value_full, preferred_element_type=jnp.float32)
    query_low = rotate(query_proj, query_pos, HEAD_FEATURES).astype(jnp.bfloat16)
    key_low = rotate(key_proj, query_pos, HEAD_FEATURES).astype(jnp.bfloat16)
    lowered_values = value_proj.astype(jnp.bfloat16)
    key_all, value_all = (
        lax.all_gather(key_low, "ctx", axis=0, tiled=True),
        lax.all_gather(lowered_values, "ctx", axis=0, tiled=True),
    )
    head_queries = query_low.reshape(row_count, KV_HEADS, group_size, HEAD_FEATURES)
    log_total, full_mixture, exact_mixture = attend(
        head_queries, key_all, value_all, query_pos, key_pos, score_scale
    )
    mixed_low = full_mixture.astype(jnp.bfloat16)
    branch = jnp.dot(mixed_low, output_full, preferred_element_type=jnp.float32)
    residual = residual_in + rms_scale(branch, gain_two)
    feed_input = rms_scale(residual, gain_three).astype(jnp.bfloat16)
    part_gate, part_up, part_down = (
        lax.all_gather(w_gate, "seq", axis=0, tiled=True),
        lax.all_gather(w_up, "seq", axis=0, tiled=True),
        lax.all_gather(w_down, "seq", axis=1, tiled=True),
    )
    feed_all = lax.all_gather(feed_input, "ctx", axis=0, tiled=True)
    gate_pre = jnp.dot(feed_all, part_gate, preferred_element_type=jnp.float32)
    up_pre = jnp.dot(feed_all, part_up, preferred_element_type=jnp.float32)
    hidden = gate_mix(gate_pre, up_pre).astype(jnp.bfloat16)
    feed_out = lax.psum_scatter(
        jnp.dot(hidden, part_down, preferred_element_type=jnp.float32).astype(jnp.bfloat16),
        "ctx",
        scatter_dimension=0,
        tiled=True,
    ).astype(jnp.float32)
    layer_out = (residual + rms_scale(feed_out, gain_four)).astype(jnp.bfloat16)
    upstream = cotangent.astype(jnp.float32)
    feed_grad, fourth_term = norm_back(feed_out, gain_four, upstream)
    feed_low = feed_grad.astype(jnp.bfloat16)
    cotangent_all = lax.all_gather(feed_low, "ctx", axis=0, tiled=True)
    hidden_grad = jnp.einsum(
        "td,fd->tf", cotangent_all, part_down, preferred_element_type=jnp.float32
    )
    outcome, mix_pull = jax.vjp(gate_mix, gate_pre, up_pre)
    gate_grad, up_grad = mix_pull(hidden_grad)
    gate_low = gate_grad.astype(jnp.bfloat16)
    up_low = up_grad.astype(jnp.bfloat16)
    input_part = jnp.einsum(
        "tf,df->td", gate_low, part_gate, preferred_element_type=jnp.float32
    ) + jnp.einsum("tf,df->td", up_low, part_up, preferred_element_type=jnp.float32)
    feed_input_grad = lax.psum_scatter(
        input_part.astype(jnp.bfloat16), "ctx", scatter_dimension=0, tiled=True
    ).astype(jnp.float32)
    gate_term = jnp.einsum("tf,td->fd", gate_low, feed_all, preferred_element_type=jnp.float32)
    up_term = jnp.einsum("tf,td->fd", up_low, feed_all, preferred_element_type=jnp.float32)
    down_term = jnp.einsum("tf,td->fd", hidden, cotangent_all, preferred_element_type=jnp.float32)
    gate_sum, up_sum, down_sum = (
        lax.psum_scatter(
            gate_term.astype(jnp.bfloat16), "seq", scatter_dimension=1, tiled=True
        ).astype(jnp.float32),
        lax.psum_scatter(
            up_term.astype(jnp.bfloat16), "seq", scatter_dimension=1, tiled=True
        ).astype(jnp.float32),
        lax.psum_scatter(
            down_term.astype(jnp.bfloat16), "seq", scatter_dimension=1, tiled=True
        ).astype(jnp.float32),
    )
    middle_grad, third_term = norm_back(residual, gain_three, feed_input_grad)
    residual_grad = upstream + middle_grad
    branch_grad, second_term = norm_back(branch, gain_two, residual_grad)
    branch_low = branch_grad.astype(jnp.bfloat16)
    output_term = jnp.einsum("th,td->hd", mixed_low, branch_low, preferred_element_type=jnp.float32)
    mixed_grad = jnp.einsum(
        "td,hd->th", branch_low, output_full, preferred_element_type=jnp.float32
    ).astype(jnp.bfloat16)
    query_sum, key_acc, value_acc = attend_back(
        head_queries,
        key_all,
        value_all,
        query_pos,
        key_pos,
        score_scale,
        log_total,
        exact_mixture,
        mixed_grad,
    )
    key_own, value_own = (
        lax.psum_scatter(
            key_acc.astype(jnp.bfloat16), "ctx", scatter_dimension=0, tiled=True
        ).astype(jnp.float32),
        lax.psum_scatter(
            value_acc.astype(jnp.bfloat16), "ctx", scatter_dimension=0, tiled=True
        ).astype(jnp.float32),
    )
    query_grad = rotate(query_sum, -query_pos, HEAD_FEATURES).astype(jnp.bfloat16)
    key_grad = rotate(key_own, -query_pos, HEAD_FEATURES).astype(jnp.bfloat16)
    value_grad = value_own.astype(jnp.bfloat16)
    normed_grad = jnp.einsum(
        "th,dh->td", query_grad, query_full, preferred_element_type=jnp.float32
    )
    normed_grad = normed_grad + jnp.einsum(
        "th,dh->td", key_grad, key_full, preferred_element_type=jnp.float32
    )
    normed_grad = normed_grad + jnp.einsum(
        "th,dh->td", value_grad, value_full, preferred_element_type=jnp.float32
    )
    query_term = jnp.einsum("td,th->dh", normed, query_grad, preferred_element_type=jnp.float32)
    key_term = jnp.einsum("td,th->dh", normed, key_grad, preferred_element_type=jnp.float32)
    value_term = jnp.einsum("td,th->dh", normed, value_grad, preferred_element_type=jnp.float32)
    input_grad, first_term = norm_back(residual_in, gain_one, normed_grad)
    grad_tokens = (residual_grad + input_grad).astype(jnp.bfloat16)
    grad_sums = (
        lax.psum_scatter(query_term, ("seq", "ctx"), scatter_dimension=0, tiled=True),
        lax.psum_scatter(key_term, ("seq", "ctx"), scatter_dimension=0, tiled=True),
        lax.psum_scatter(value_term, ("seq", "ctx"), scatter_dimension=0, tiled=True),
        lax.psum_scatter(output_term, ("seq", "ctx"), scatter_dimension=0, tiled=True),
        lax.psum_scatter(first_term, ("seq", "ctx"), scatter_dimension=0, tiled=True),
        lax.psum_scatter(second_term, ("seq", "ctx"), scatter_dimension=0, tiled=True),
        lax.psum_scatter(third_term, ("seq", "ctx"), scatter_dimension=0, tiled=True),
        lax.psum_scatter(fourth_term, ("seq", "ctx"), scatter_dimension=0, tiled=True),
    )
    return (
        layer_out,
        grad_tokens,
        grad_sums[0],
        grad_sums[1],
        grad_sums[2],
        grad_sums[3],
        gate_sum.T,
        up_sum.T,
        down_sum,
        grad_sums[4],
        grad_sums[5],
        grad_sums[6],
        grad_sums[7],
    )


CORES = 2
GELU_IN = 0.7978845608
GELU_CUBE = 0.044715
VMEM_LIMIT = 56 * 2**20


def wide(value):
    return value.astype(jnp.float32)


def narrow(value):
    return value.astype(jnp.bfloat16)


def rms_parts(signal):
    scale = lax.rsqrt(jnp.mean(signal * signal, axis=-1, keepdims=True) + epsilon)
    return scale, signal * scale


def rms_back(scale, unit, weight, upstream):
    weighted = upstream * weight
    mean = jnp.mean(weighted * unit, axis=-1, keepdims=True)
    return scale * (weighted - unit * mean), jnp.sum(upstream * unit, axis=0)


def dot_nn(left, right):
    return jnp.dot(left, right, preferred_element_type=jnp.float32)


def dot_nt(left, right):
    return jnp.einsum("ab,cb->ac", left, right, preferred_element_type=jnp.float32)


def dot_tn(left, right):
    return jnp.einsum("ab,ac->bc", left, right, preferred_element_type=jnp.float32)


def after(value, *others):
    anywhere = pl.BlockSpec(memory_space=pl.ANY)
    return pl.pallas_call(
        lambda *refs: None,
        in_specs=[anywhere] * (1 + len(others)),
        out_specs=anywhere,
        out_shape=jax.ShapeDtypeStruct(value.shape, value.dtype),
        input_output_aliases={0: 0},
    )(value, *others)


def copied(value, rows, *others):
    columns = value.shape[1]
    part = pl.BlockSpec((rows // 4, columns), lambda i: (i, 0))

    def kernel(*refs):
        refs[-1][...] = refs[0][...]

    return pl.pallas_call(
        kernel,
        grid=(4,),
        in_specs=[part] + [pl.BlockSpec(memory_space=pl.ANY)] * len(others),
        out_specs=part,
        out_shape=jax.ShapeDtypeStruct((rows, columns), value.dtype),
    )(value, *others)


def fresh(shape, dtype, *others):
    anywhere = pl.BlockSpec(memory_space=pl.ANY)
    return pl.pallas_call(
        lambda *refs: None,
        in_specs=[anywhere] * len(others),
        out_specs=anywhere,
        out_shape=jax.ShapeDtypeStruct(shape, dtype),
    )(*others)


def lull(*others):
    anywhere = pl.BlockSpec(memory_space=pl.ANY)
    return pl.pallas_call(
        lambda *refs: None,
        in_specs=[anywhere] * len(others),
        out_specs=anywhere,
        out_shape=jax.ShapeDtypeStruct((8, 128), jnp.float32),
        cost_estimate=pl.CostEstimate(flops=10**12, bytes_accessed=0, transcendentals=0),
    )(*others)


class Order:
    def __init__(self):
        self.last = ()

    def pin(self, value, sent=None):
        extra = () if sent is None else (lull(sent),)
        value = after(value, *self.last, *extra)
        self.last = (value,)
        return value

    def mark(self, value):
        self.last = (value,)

    def late(self, value, rows):
        return copied(value, rows, *self.last)

    def hold(self, value):
        return after(value, *self.last)


class Moves:
    def __init__(self, n_seq, n_ctx):
        self.n_seq, self.n_ctx = n_seq, n_ctx
        self.line = n_ctx // CORES
        self.seq = lax.axis_index("seq")
        self.ctx = lax.axis_index("ctx")
        self.plane = self.ctx // CORES
        self.core = self.ctx % CORES

    def _send(self, value, move):
        pairs = []
        for s in range(self.n_seq):
            for c in range(self.n_ctx):
                t = move(s, c // CORES, c % CORES)
                pairs.append((s * self.n_ctx + c, t[0] * self.n_ctx + t[1] * CORES + t[2]))
        return lax.ppermute(value, ("seq", "ctx"), pairs)

    def across(self, value, mask):
        return self._send(value, lambda s, z, k: (s ^ mask, z, k))

    def along(self, value, step):
        return self._send(value, lambda s, z, k: (s, (z + step) % self.line, k))

    def plane_swap(self, value, mask):
        return self._send(value, lambda s, z, k: (s, z ^ mask, k))

    def swap(self, value):
        return self._send(value, lambda s, z, k: (s, z, k ^ 1))

    def gather_halves(self, low, high, gate):
        low_near = self.across(low, 2)
        high_near = self.across(high, 1)
        yield None
        low_near, high_near = gate(low_near, low), gate(high_near)
        low_two, high_two = jnp.stack([low, low_near]), jnp.stack([high, high_near])
        low_far = self.across(low_two, 1)
        high_far = self.across(high_two, 2)
        yield None
        yield low_near, high_near, gate(low_far, low_two), gate(high_far)

    def scatter_whole(self, terms, mask, gate, ready=lambda v: v):
        other = 3 - mask
        pick = lambda m: lax.dynamic_index_in_dim(terms, self.seq ^ m, 0, False)
        sent = ready(jnp.stack([pick(mask), pick(3)]))
        near = self.across(sent, mask)
        yield None
        near = gate(near, sent)
        onward = narrow(wide(pick(other)) + wide(near[1]))
        far = self.across(onward, other)
        yield None
        yield wide(pick(0)) + wide(near[0]) + wide(gate(far, onward))

    def scatter_halves(self, terms, gate, ready=lambda v: v):
        half = terms.shape[1] // 2
        low = self.scatter_whole(terms[:, :half], 1, gate, ready)
        high = self.scatter_whole(terms[:, half:], 2, gate, ready)
        for _ in range(2):
            next(low), next(high)
            yield None
        yield jnp.concatenate([next(low), next(high)], axis=0)

    def exchange_line(self, blocks):
        out = fresh(blocks.shape, blocks.dtype, blocks)
        own = lax.dynamic_index_in_dim(blocks, self.plane, 0, False)
        out = lax.dynamic_update_index_in_dim(out, own, self.plane, 0)
        for step in range(1, self.line):
            sent = lax.dynamic_index_in_dim(blocks, (self.plane + step) % self.line, 0, False)
            got = self.along(sent, step)
            out = lax.dynamic_update_index_in_dim(out, got, (self.plane - step) % self.line, 0)
        return out

    def transpose_chips(self, value):
        return self._send(value, lambda s, z, k: (z, s, k))

    def exchange_cores(self, blocks):
        own = lax.dynamic_index_in_dim(blocks, self.core, 0, False)
        got = self.swap(lax.dynamic_index_in_dim(blocks, 1 - self.core, 0, False))
        first = self.core == 0
        return jnp.stack([jnp.where(first, own, got), jnp.where(first, got, own)])


ANYWHERE = pl.BlockSpec(memory_space=pl.ANY)


def tile(rows, columns):
    return pl.BlockSpec((rows, columns), lambda i: (i, 0))


def whole(*shape):
    return pl.BlockSpec(shape, lambda i: (0,) * len(shape))


def call(kernel, steps, in_specs, out_specs, out_shape, flops, args, scratch=(), others=()):
    count = len(args)

    def body(*refs):
        kernel(*refs[:count], *refs[count + len(others) :])

    return pl.pallas_call(
        body,
        grid=(steps,),
        in_specs=in_specs + [ANYWHERE] * len(others),
        out_specs=out_specs,
        out_shape=out_shape,
        scratch_shapes=list(scratch),
        compiler_params=pltpu.CompilerParams(vmem_limit_bytes=VMEM_LIMIT),
        cost_estimate=pl.CostEstimate(flops=flops, bytes_accessed=0, transcendentals=0),
    )(*args, *others)


def array(dtype, *shape):
    return jax.ShapeDtypeStruct(shape, dtype)


def mul_nt(left, right):
    return lax.dot_general(
        left, right, (((1,), (1,)), ((), ())), preferred_element_type=jnp.float32
    )


def mul_tn(left, right):
    return lax.dot_general(
        left, right, (((0,), (0,)), ((), ())), preferred_element_type=jnp.float32
    )


def turn_pair(value, cosine, sine):
    half = value.shape[1] // 2
    first, second = value[:, :half], value[:, half:]
    return jnp.concatenate(
        [first * cosine - second * sine, second * cosine + first * sine], axis=1
    )


BF16, F32 = jnp.bfloat16, jnp.float32
TILE = 256


def load(copies, sems):
    started = [pltpu.make_async_copy(a, b, sems.at[i]) for i, (a, b) in enumerate(copies)]
    for copy in started:
        copy.start()
    return started


def whole_copies(seq, pieces, target, left):
    mask, own, near, far, last = pieces
    rows = own.shape[0]
    near = near.at[pl.ds(0, rows)]
    columns = pl.ds(left, own.shape[1])
    at = lambda m: target.at[pl.ds(pl.multiple_of((seq ^ m) * rows, 64), rows), columns]
    other = 3 - mask
    return [(own, at(0)), (near, at(mask)), (far, at(other)), (last, at(3))]


def half_copies(seq, pieces, target):
    own, low_near, high_near, low_far, high_far = pieces
    rows = own.shape[0]
    half = rows // 2
    last = pl.ds(low_near.shape[0] - half, half)
    low_near, high_near = low_near.at[last], high_near.at[last]
    at = lambda m, h: target.at[pl.ds(pl.multiple_of((seq ^ m) * rows + h * half, 32), half)]
    return [
        (own, target.at[pl.ds(pl.multiple_of(seq * rows, 64), rows)]),
        (low_near, at(2, 0)),
        (high_near, at(1, 1)),
        (low_far.at[0], at(1, 0)),
        (low_far.at[1], at(3, 0)),
        (high_far.at[0], at(2, 1)),
        (high_far.at[1], at(3, 1)),
    ]


SCALARS = pl.BlockSpec(memory_space=pltpu.SMEM)


def project_rows(place, tokens, pieces, feats, tables):
    rows, width = tokens.shape
    wide_columns = pieces[0].shape[1]

    def kernel(place_ref, x_ref, own, near_a, near_b, far_a, far_b, cq, sq, cp, sp, *refs):
        normed_ref, query_ref, pair_ref, gains_ref, w_ref, sems = refs

        @pl.when(pl.program_id(0) == 0)
        def _():
            copies = half_copies(place_ref[2], (own, near_a, near_b, far_a, far_b), w_ref)
            for copy in load(copies, sems):
                copy.wait()
            pad = wide_columns - 2 * feats
            rows8 = lax.broadcasted_iota(jnp.int32, (8, pad), 0)
            columns8 = lax.broadcasted_iota(jnp.int32, (8, pad), 1)
            picks = (rows8 == columns8).astype(BF16)
            gains_ref[...] = mul_nt(picks, w_ref[:, 2 * feats :])

        x = x_ref[...].astype(F32)
        scale = lax.rsqrt(jnp.mean(x * x, axis=-1, keepdims=True) + epsilon)
        normed = (x * scale * gains_ref[0:1]).astype(BF16)
        normed_ref[...] = normed
        both = dot_nn(normed, w_ref[:, : 2 * feats])
        query_ref[...] = turn_pair(both[:, :feats], cq[...], sq[...]).astype(BF16)
        pair_ref[...] = turn_pair(both[:, feats:], cp[...], sp[...]).astype(BF16)

    half = feats // 2
    return call(
        kernel,
        rows // TILE,
        [SCALARS, tile(TILE, width)] + [ANYWHERE] * 5 + [tile(TILE, half)] * 4,
        [tile(TILE, width), tile(TILE, feats), tile(TILE, feats), whole(8, width)],
        [
            array(BF16, rows, width),
            array(BF16, rows, feats),
            array(BF16, rows, feats),
            array(F32, 8, width),
        ],
        4 * rows * width * feats,
        (place, tokens) + pieces + tables,
        [pltpu.VMEM((width, wide_columns), BF16), pltpu.SemaphoreType.DMA((7,))],
    )


def soft_rows(query, keys, place, places):
    bent = jnp.tanh(mul_nt(query, keys) * (HEAD_FEATURES ** (-0.5) / softcap))
    weight = jnp.where(places <= place, jnp.exp(softcap * bent), 0.0)
    return bent, weight / jnp.sum(weight, axis=-1, keepdims=True)


def attend_head(query, key, value, place, places, others):
    rows, feats = query.shape

    def kernel(q_ref, k_ref, v_ref, place_ref, places_ref, out_ref):
        _, probs = soft_rows(q_ref[...], k_ref[...], place_ref[...], places_ref[...])
        out_ref[...] = dot_nn(probs.astype(BF16), v_ref[...]).astype(BF16)

    return call(
        kernel,
        rows // TILE,
        [tile(TILE, feats), whole(rows, feats), whole(rows, feats), tile(TILE, 1), whole(1, rows)],
        [tile(TILE, feats)],
        [array(BF16, rows, feats)],
        4 * rows * rows * feats,
        (query, key, value, place, places),
        (),
        others,
    )[0]


def attend_head_back(
    place, query, key, value, branch, w_out, spot, spots, cosine, sine, others
):
    rows, feats = query.shape
    width = branch.shape[1]
    score_scale = HEAD_FEATURES ** (-0.5)
    steps = rows // TILE

    def kernel(place_ref, q_ref, k_ref, v_ref, b_ref, w_ref, spot_ref, spots_ref, c_ref, s_ref, *refs):
        dq, own_ref, send_ref, dk, dv = refs
        step = pl.program_id(0)

        @pl.when(step == 0)
        def _():
            dk[...] = jnp.zeros_like(dk)
            dv[...] = jnp.zeros_like(dv)

        query, keys = q_ref[...], k_ref[...]
        grad = mul_nt(b_ref[...], w_ref[...]).astype(BF16)
        bent, probs = soft_rows(query, keys, spot_ref[...], spots_ref[...])
        prob_grad = mul_nt(grad, v_ref[...])
        delta = jnp.sum(probs * prob_grad, axis=-1, keepdims=True)
        raw = (probs * (prob_grad - delta) * (1.0 - bent * bent)).astype(BF16)
        total = dot_nn(raw, keys) * score_scale
        dq[...] = turn_pair(total, c_ref[...], -s_ref[...]).astype(BF16)
        dk[...] += mul_tn(raw, query) * score_scale
        dv[...] += mul_tn(probs.astype(BF16), grad)

        @pl.when(step == steps - 1)
        def _():
            first = place_ref[1] == 0
            own_ref[...] = jnp.where(first, dk[...], dv[...])
            send_ref[...] = jnp.where(first, dv[...], dk[...])

    return call(
        kernel,
        steps,
        [SCALARS, tile(TILE, feats), whole(rows, feats), whole(rows, feats), tile(TILE, width)]
        + [whole(feats, width), tile(TILE, 1), whole(1, rows)]
        + [tile(TILE, feats // 2), tile(TILE, feats // 2)],
        [tile(TILE, feats), whole(rows, feats), whole(rows, feats)],
        [array(BF16, rows, feats), array(F32, rows, feats), array(F32, rows, feats)],
        10 * rows * rows * feats + 2 * rows * width * feats,
        (place, query, key, value, branch, w_out, spot, spots, cosine, sine),
        [pltpu.VMEM((rows, feats), F32)] * 2,
        others,
    )


OUT_ORDER = ((0, 0), (0, 2), (0, 1), (0, 3), (2, 0), (2, 2), (1, 1), (1, 3)) + (
    ((1, 0), (1, 2), (3, 0), (3, 2), (2, 1), (2, 3), (3, 1), (3, 3))
)


def branch_rows(place, mixed, own, other, tokens, gain_two, gain_three):
    heads, rows, feats = mixed.shape
    blocks, out_rows, width = own.shape
    own_rows = TILE // CORES
    planes = 4

    def kernel(
        place_ref,
        m_ref,
        own_ref,
        other_ref,
        x_ref,
        two_ref,
        three_ref,
        out_ref,
        mine_ref,
        full_ref,
        w_ref,
        sems,
        full_sem,
    ):
        step = pl.program_id(0)
        plane, core, seq = place_ref[0], place_ref[1], place_ref[2]
        keep = pltpu.make_async_copy(w_ref, full_ref, full_sem)

        @pl.when(step == 0)
        def _():
            copies = []
            for i, (m, x) in enumerate(OUT_ORDER):
                at = (seq ^ m) * planes + (plane ^ x)
                copies.append((own_ref.at[i], w_ref.at[at, core]))
                copies.append((other_ref.at[i], w_ref.at[at, 1 - core]))
            for copy in load(copies, sems):
                copy.wait()
            keep.start()

        rows_in = jnp.concatenate([m_ref[h] for h in range(heads)], axis=1)
        branch = dot_nn(rows_in, w_ref[...].reshape(heads * feats, width))

        @pl.when(step == plane)
        def _():
            mine_ref[...] = jnp.where(core == 0, branch[:own_rows], branch[own_rows:])

        scale = lax.rsqrt(jnp.mean(branch * branch, axis=-1, keepdims=True) + epsilon)
        residual = x_ref[...].astype(F32) + branch * scale * two_ref[...]
        scale = lax.rsqrt(jnp.mean(residual * residual, axis=-1, keepdims=True) + epsilon)
        out_ref[...] = (residual * scale * three_ref[...]).astype(BF16)

        @pl.when(step == rows // TILE - 1)
        def _():
            keep.wait()

    return call(
        kernel,
        rows // TILE,
        [
            SCALARS,
            pl.BlockSpec((heads, TILE, feats), lambda i: (0, i, 0)),
            ANYWHERE,
            ANYWHERE,
            tile(TILE, width),
            whole(1, width),
            whole(1, width),
        ],
        [tile(TILE, width), whole(own_rows, width), ANYWHERE],
        [
            array(BF16, rows, width),
            array(F32, own_rows, width),
            array(BF16, blocks, CORES, out_rows, width),
        ],
        2 * heads * rows * feats * width,
        (place, mixed, own, other, tokens, gain_two, gain_three),
        [
            pltpu.VMEM((blocks, CORES, out_rows, width), BF16),
            pltpu.SemaphoreType.DMA((2 * blocks,)),
            pltpu.SemaphoreType.DMA,
        ],
    )


def feed_open(place, feed, gate_pieces, up_pieces):
    rows, width = feed.shape
    units = gate_pieces[0].shape[1]

    def kernel(place_ref, x_ref, *refs):
        gates, ups = refs[:4], refs[4:8]
        hidden_ref, gate_ref, up_ref, w_ref, sems = refs[8:]

        @pl.when(pl.program_id(0) == 0)
        def _():
            copies = whole_copies(place_ref[2], (1,) + gates, w_ref, 0)
            copies += whole_copies(place_ref[2], (2,) + ups, w_ref, units)
            for copy in load(copies, sems):
                copy.wait()

        both = dot_nn(x_ref[...], w_ref[...])
        gate, up = both[:, :units], both[:, units:]
        square = gate * gate
        bend = jnp.tanh(GELU_IN * (gate + GELU_CUBE * square * gate))
        half = 0.5 * (1.0 + bend)
        gelu = half * gate
        slope = half + 0.5 * gate * (1.0 - bend * bend) * (
            GELU_IN + 3.0 * GELU_IN * GELU_CUBE * square
        )
        hidden_ref[...] = (gelu * up).astype(BF16)
        gate_ref[...] = (up * slope).astype(BF16)
        up_ref[...] = gelu.astype(BF16)

    return call(
        kernel,
        rows // TILE,
        [SCALARS, tile(TILE, width)] + [ANYWHERE] * 8,
        [tile(TILE, units)] * 3,
        [array(BF16, rows, units)] * 3,
        4 * rows * width * units,
        (place, feed) + gate_pieces + up_pieces,
        [pltpu.VMEM((width, 2 * units), BF16), pltpu.SemaphoreType.DMA((8,))],
    )


def feed_close(place, hidden, down_pieces):
    rows, units = hidden.shape
    width = down_pieces[0].shape[0] * 4

    def kernel(place_ref, x_ref, *refs):
        out_ref, dw_ref, sems = refs[5:]

        @pl.when(pl.program_id(0) == 0)
        def _():
            for copy in load(half_copies(place_ref[2], refs[:5], dw_ref), sems):
                copy.wait()

        out_ref[...] = mul_nt(x_ref[...], dw_ref[...]).astype(BF16)

    return call(
        kernel,
        rows // TILE,
        [SCALARS, tile(TILE, units)] + [ANYWHERE] * 5,
        [tile(TILE, width)],
        [array(BF16, rows, width)],
        2 * rows * width * units,
        (place, hidden) + down_pieces,
        [pltpu.VMEM((width, units), BF16), pltpu.SemaphoreType.DMA((7,))],
    )[0]


def feed_back(
    place, grad, gate_factor, up_factor, gate_pieces, up_pieces, down_pieces, others
):
    rows, width = grad.shape
    units = gate_factor.shape[1]

    def kernel(place_ref, g_ref, gf_ref, uf_ref, *refs):
        gates, ups, downs = refs[:4], refs[4:8], refs[8:13]
        gate_ref, up_ref, out_ref, w_ref, dw_ref, both_ref, sems, down_sems = refs[13:]
        seq = place_ref[2]
        copies = whole_copies(seq, (1,) + gates, w_ref, 0)
        copies += whole_copies(seq, (2,) + ups, w_ref, units)
        first = pl.program_id(0) == 0

        @pl.when(first)
        def _():
            started = load(half_copies(seq, downs, dw_ref), down_sems)
            load(copies, sems)
            for copy in started:
                copy.wait()

        hidden_grad = dot_nn(g_ref[...], dw_ref[...])
        gate_low = (hidden_grad * gf_ref[...].astype(F32)).astype(BF16)
        up_low = (hidden_grad * uf_ref[...].astype(F32)).astype(BF16)
        gate_ref[...] = gate_low
        up_ref[...] = up_low
        both_ref[:, :units] = gate_low
        both_ref[:, units:] = up_low

        @pl.when(first)
        def _():
            for i, (a, b) in enumerate(copies):
                pltpu.make_async_copy(a, b, sems.at[i]).wait()

        out_ref[...] = mul_nt(both_ref[...], w_ref[...]).astype(BF16)

    return call(
        kernel,
        rows // TILE,
        [SCALARS, tile(TILE, width), tile(TILE, units), tile(TILE, units)] + [ANYWHERE] * 13,
        [tile(TILE, units), tile(TILE, units), tile(TILE, width)],
        [array(BF16, rows, units), array(BF16, rows, units), array(BF16, rows, width)],
        6 * rows * width * units,
        (place, grad, gate_factor, up_factor) + gate_pieces + up_pieces + down_pieces,
        [
            pltpu.VMEM((width, 2 * units), BF16),
            pltpu.VMEM((width, units), BF16),
            pltpu.VMEM((TILE, 2 * units), BF16),
            pltpu.SemaphoreType.DMA((8,)),
            pltpu.SemaphoreType.DMA((7,)),
        ],
        others,
    )


def qkv_back(normed, query_grad, own, other, cosine, sine, more, others):
    rows, feats = query_grad.shape
    width = normed.shape[1]
    block = 384
    both_columns = 2 * feats

    def kernel(n_ref, q_ref, own_ref, other_ref, c_ref, s_ref, more_ref, both_ref, out_ref):
        @pl.when(pl.program_id(0) == 0)
        def _():
            pair = turn_pair(own_ref[...] + other_ref[...], c_ref[...], -s_ref[...])
            both_ref[:, :feats] = q_ref[...]
            both_ref[:, feats:] = pair.astype(BF16)

        out_ref[:, :both_columns] = mul_tn(n_ref[...], both_ref[...]).astype(BF16)
        out_ref[:, both_columns:] = more_ref[...]

    total = both_columns + more.shape[1]
    return call(
        kernel,
        width // block,
        [pl.BlockSpec((rows, block), lambda i: (0, i))]
        + [whole(rows, feats)] * 3
        + [whole(rows, feats // 2)] * 2
        + [tile(block, more.shape[1])],
        [whole(rows, both_columns), tile(block, total)],
        [array(BF16, rows, both_columns), array(BF16, width, total)],
        2 * rows * width * both_columns,
        (normed, query_grad, own, other, cosine, sine, more),
        (),
        others,
    )


def normed_back(place, both, pieces, others):
    rows, both_columns = both.shape
    width, wide_columns = pieces[0].shape[0] * 4, pieces[0].shape[1]

    def kernel(place_ref, both_ref, *refs):
        out_ref, w_ref, sems = refs[5:]

        @pl.when(pl.program_id(0) == 0)
        def _():
            for copy in load(half_copies(place_ref[2], refs[:5], w_ref), sems):
                copy.wait()

        out_ref[...] = mul_nt(both_ref[...], w_ref[:, :both_columns]).astype(BF16)

    return call(
        kernel,
        rows // TILE,
        [SCALARS, tile(TILE, both_columns)] + [ANYWHERE] * 5,
        [tile(TILE, width)],
        [array(BF16, rows, width)],
        2 * rows * both_columns * width,
        (place, both) + pieces,
        [pltpu.VMEM((width, wide_columns), BF16), pltpu.SemaphoreType.DMA((7,))],
        others,
    )[0]


def weight_grad(left, right, block, others):
    rows, width = left.shape
    columns = right.shape[1]

    def kernel(left_ref, right_ref, out_ref):
        out_ref[...] = mul_tn(left_ref[...], right_ref[...]).astype(BF16)

    return call(
        kernel,
        width // block,
        [pl.BlockSpec((rows, block), lambda i: (0, i)), whole(rows, columns)],
        [tile(block, columns)],
        [array(BF16, width, columns)],
        2 * rows * width * columns,
        (left, right),
        (),
        others,
    )[0]


def own_grads(terms, weights, gain):
    heads, rows, columns = terms.shape
    feats = HEAD_FEATURES

    def kernel(terms_ref, wq, wk, wv, g_ref, dq, dk, dv, gains_ref, first_ref):
        total, first = 0.0, 0.0
        for h in range(heads):
            term = terms_ref[h].astype(F32)
            total += term[:, 2 * feats :]
            pair, w = ((dk, wk), (dv, wv))[h % CORES]
            group = h // CORES
            for out, weight, at, value in (
                (dq, wq, slice(h * feats, (h + 1) * feats), term[:, :feats]),
                (pair, w, slice(group * feats, (group + 1) * feats), term[:, feats : 2 * feats]),
            ):
                out[:, at] = value
                first += jnp.sum(weight[:, at].astype(F32) * value, axis=1, keepdims=True)
        gains_ref[...] = total
        first_ref[...] = first / g_ref[...].astype(F32)

    shapes = [w.shape for w in weights] + [(rows, columns - 2 * feats), (rows, 1)]
    return call(
        kernel,
        1,
        [whole(*terms.shape)] + [whole(*w.shape) for w in weights] + [whole(rows, 1)],
        [whole(*s) for s in shapes],
        [array(F32, *s) for s in shapes],
        0,
        (terms,) + weights + (gain,),
    )


def head_body(
    tokens,
    w_query,
    w_key,
    w_value,
    w_output,
    w_gate,
    w_up,
    w_down,
    first_gain,
    second_gain,
    third_gain,
    fourth_gain,
    block_pairs,
    cotangent,
    n_seq,
    n_ctx,
):
    moves = Moves(n_seq, n_ctx)
    order = Order()
    pin, hold = order.pin, order.hold
    line = moves.line
    core_zero = moves.core == 0
    rows, width = tokens.shape
    feat_rows = w_query.shape[0]
    out_rows = w_output.shape[0]
    feats = HEAD_FEATURES
    pad = 128
    gather = lambda v: lax.all_gather(v, "ctx", axis=0, tiled=True)
    to_all = lambda v: lax.all_to_all(v, "ctx", split_axis=0, concat_axis=0, tiled=True)
    scatter = lambda v: lax.psum_scatter(v, "ctx", scatter_dimension=0, tiled=True)

    place = jnp.stack([moves.plane, moves.core, moves.seq]).astype(jnp.int32)
    block = w_gate.shape[0]
    half = block // 2

    out_near = moves.plane_swap(w_output, 2)
    gains_in = jnp.stack([first_gain, second_gain, third_gain, fourth_gain], axis=1)
    gains_in = jnp.pad(gains_in, ((0, 0), (0, pad - 4)))
    by_head = jnp.concatenate(
        [
            w_query.reshape(feat_rows, line, CORES, feats),
            jnp.stack(
                [
                    w_key.reshape(feat_rows, line, feats),
                    w_value.reshape(feat_rows, line, feats),
                ],
                axis=2,
            ),
            jnp.broadcast_to(gains_in[:, None, None, :], (feat_rows, line, CORES, pad)),
        ],
        axis=3,
    ).transpose(2, 1, 0, 3)
    by_plane = moves.exchange_cores(by_head).transpose(1, 0, 2, 3)
    down_own = w_down.T
    near_x = moves.across(jnp.concatenate([w_gate, down_own[half:]]), 1)
    near_y = moves.across(jnp.concatenate([w_up, down_own[:half]]), 2)
    own_columns = moves.exchange_line(by_plane).reshape(n_ctx * feat_rows, 2 * feats + pad)
    own_columns = pin(own_columns, by_plane)
    tokens_in = hold(tokens)
    tokens_all = gather(tokens_in)
    columns_move = moves.gather_halves(own_columns[:half], own_columns[half:], pin)
    next(columns_move)
    near_x, near_y = pin(near_x), pin(near_y)
    out_two = pin(jnp.stack([w_output, pin(out_near)]))
    next(columns_move)

    block_size = rows // 2
    offsets = jnp.arange(block_size, dtype=jnp.int32)
    pos = (hold(block_pairs)[:, :, None] * block_size + offsets[None, None, :]).reshape(-1)
    spot, spots = pos[:, None], pos[None, :]
    frequency = theta ** (-2.0 * jnp.arange(feats // 2, dtype=jnp.float32) / feats)
    angles = wide(pos)[:, None] * frequency[None, :]
    cosine, sine = pin(jnp.cos(angles)), pin(jnp.sin(angles))
    pair_cosine = pin(jnp.where(core_zero, cosine, 1.0))
    pair_sine = pin(jnp.where(core_zero, sine, 0.0))
    tables = (cosine, sine, pair_cosine, pair_sine)

    columns = (own_columns,) + next(columns_move)
    gate_far = moves.across(hold(w_gate), 2)
    up_far = moves.across(hold(w_up), 1)
    tokens_all = pin(tokens_all, tokens_in)
    out_two = hold(out_two)
    out_far = moves.plane_swap(out_two, 1)

    normed, query, pair, gains = project_rows(place, tokens_all, columns, feats, tables)
    gain_one, gain_two, gain_three, gain_four = (gains[i : i + 1] for i in range(4))
    pair_other = moves.swap(pair)
    order.mark(pair)
    pair_other = pin(pair_other, pair)
    key = jnp.where(core_zero, pair, pair_other)
    value = jnp.where(core_zero, pair_other, pair)
    mixed = pin(attend_head(query, key, value, spot, spots, order.last))
    mixed_all = lax.all_gather(mixed, "ctx", axis=0)

    out_far = pin(out_far, out_two)
    out_move = moves.gather_halves(out_two, out_far, pin)
    next(out_move)
    next(out_move)
    gate_far, up_far = pin(gate_far), pin(up_far)
    gate_last, up_last = order.late(near_x, block), order.late(near_y, block)
    low_near, high_near, low_far, high_far = next(out_move)
    gate_last, up_last = moves.across(hold(gate_last), 2), moves.across(hold(up_last), 1)
    out_own = jnp.concatenate(
        [out_two, out_far, low_near, high_near, *(v.reshape(4, *v.shape[2:]) for v in (low_far, high_far))]
    )
    out_own = pin(out_own)
    out_other = moves.swap(out_own)
    low_two = pin(jnp.stack([down_own[:half], near_y[block:]]))
    high_two = pin(jnp.stack([down_own[half:], near_x[block:]]))
    out_other = pin(out_other, out_own)
    mixed_all = pin(mixed_all, mixed)
    feed_all, branch, w_full = branch_rows(
        place, mixed_all, out_own, out_other, tokens_all, gain_two, gain_three
    )
    order.mark(branch)
    gate_pieces = (w_gate, near_x, gate_far, pin(gate_last))
    up_pieces = (w_up, near_y, up_far, pin(up_last))
    down_low, down_high = moves.across(hold(low_two), 1), moves.across(hold(high_two), 2)
    hidden, gate_factor, up_factor = feed_open(place, feed_all, gate_pieces, up_pieces)
    order.mark(hidden)
    down_pieces = (down_own, near_y, near_x, pin(down_low), pin(down_high))
    feed_part = feed_close(place, hidden, down_pieces)
    order.mark(feed_part)
    feed_out = scatter(feed_part)

    scale_two, unit_two = rms_parts(hold(branch))
    residual = wide(tokens) + unit_two * gain_two
    scale_three, unit_three = rms_parts(residual)
    later = hold(place)
    w_out = lax.dynamic_slice_in_dim(
        w_full.reshape(-1, width), (later[0] * CORES + later[1]) * feats, feats, 0
    )
    w_out = pin(w_out)
    unit_two, unit_three, residual = pin(unit_two), pin(unit_three), pin(residual)

    upstream = wide(cotangent)
    feed_out = pin(feed_out, feed_part)
    scale_four, unit_four = rms_parts(wide(feed_out))
    layer_out = narrow(residual + unit_four * gain_four)
    feed_grad, fourth_term = rms_back(scale_four, unit_four, gain_four, upstream)
    feed_low = pin(narrow(feed_grad))
    grad_all = pin(gather(feed_low), feed_low)
    shape = (n_seq, block, hidden.shape[1])
    gate_low, up_low, input_part = feed_back(
        place, grad_all, gate_factor, up_factor, gate_pieces, up_pieces, down_pieces, order.last
    )
    order.mark(input_part)
    feed_input_grad = scatter(input_part)
    down_term = weight_grad(grad_all, hidden, 384, order.last).reshape(shape)
    order.mark(down_term)
    plain = lambda value, sent=None: pin(value)
    down_move = moves.scatter_halves(down_term, plain)
    next(down_move)
    gate_term = weight_grad(feed_all, gate_low, 384, order.last).reshape(shape)
    order.mark(gate_term)
    gate_move = moves.scatter_whole(gate_term, 1, plain)
    next(gate_move)
    up_term = weight_grad(feed_all, up_low, 384, order.last).reshape(shape)
    order.mark(up_term)
    up_move = moves.scatter_whole(up_term, 2, plain)
    next(up_move)
    next(down_move)
    feed_input_grad = wide(pin(feed_input_grad, input_part))
    middle_grad, third_term = rms_back(scale_three, unit_three, gain_three, feed_input_grad)
    residual_grad = upstream + middle_grad
    branch_grad, second_term = rms_back(scale_two, unit_two, gain_two, residual_grad)
    branch_low = pin(narrow(branch_grad))

    branch_all = gather(branch_low)
    next(gate_move), next(up_move)
    branch_all = pin(branch_all, branch_low)
    query_grad, pair_own, pair_send = attend_head_back(
        place, query, key, value, branch_all, w_out, spot, spots, cosine, sine, order.last
    )
    order.mark(query_grad)
    pair_other = moves.swap(pair_send)
    pair_other = pin(pair_other, pair_send)
    down_sum = next(down_move).T
    terms = jnp.stack([second_term, third_term, fourth_term])
    terms = narrow(jnp.pad(terms, ((0, pad - 3), (0, 0))).T)
    qkv_grad, qkv_term = qkv_back(
        normed, query_grad, pair_own, pair_other, pair_cosine, pair_sine, terms, order.last
    )
    order.mark(qkv_term)
    qkv_move = moves.scatter_halves(qkv_term.reshape(n_seq, width // n_seq, -1), pin)
    next(qkv_move)
    normed_part = normed_back(place, qkv_grad, columns, order.last)
    order.mark(normed_part)
    normed_grad = scatter(normed_part)

    output_term = weight_grad(mixed, branch_all, feats, order.last)
    order.mark(output_term)
    out_term = output_term.reshape(CORES, CORES, out_rows, width).transpose(1, 0, 2, 3)
    out_term = moves.exchange_cores(out_term).reshape(line, out_rows, width)
    next(qkv_move)
    gate_sum, up_sum = next(gate_move), next(up_move)
    out_move = moves.scatter_whole(pin(out_term), 2, pin)
    next(out_move)
    own_in = pin(narrow(next(qkv_move))).reshape(n_ctx, feat_rows, 2 * feats + pad)
    own_term = to_all(own_in)
    next(out_move)
    grad_output = moves.transpose_chips(pin(narrow(next(out_move))))
    own_term = pin(own_term, own_in)
    normed_grad = pin(normed_grad)
    scale_one, unit_one = rms_parts(wide(tokens))
    input_grad, _ = rms_back(scale_one, unit_one, gain_one, wide(normed_grad))
    grad_tokens = pin(narrow(residual_grad + input_grad))
    grad_query, grad_key, grad_value, grad_gains, grad_first = own_grads(
        own_term, (w_query, w_key, w_value), first_gain[:, None]
    )
    grad_output = wide(pin(grad_output))
    return (
        layer_out,
        grad_tokens,
        grad_query,
        grad_key,
        grad_value,
        grad_output,
        gate_sum,
        up_sum,
        down_sum,
        grad_first[:, 0],
        grad_gains[:, 0],
        grad_gains[:, 1],
        grad_gains[:, 2],
    )


def solution(mesh):
    placed = (
        P(("seq", "ctx"), None),
        P(("seq", "ctx"), None),
        P(("seq", "ctx"), None),
        P(("seq", "ctx"), None),
        P(("seq", "ctx"), None),
        P("seq", "ctx"),
        P("seq", "ctx"),
        P("ctx", "seq"),
        P(("seq", "ctx")),
        P(("seq", "ctx")),
        P(("seq", "ctx")),
        P(("seq", "ctx")),
        P(),
        P(("seq", "ctx"), None),
    )
    n_seq, n_ctx = mesh.shape["seq"], mesh.shape["ctx"]
    if n_ctx == QUERY_HEAD_COUNT and n_seq == 4:
        body = partial(head_body, n_seq=n_seq, n_ctx=n_ctx)
    else:
        body = context_body
    return jax.shard_map(
        body,
        mesh=mesh,
        in_specs=placed,
        out_specs=(
            P(("seq", "ctx"), None),
            P(("seq", "ctx"), None),
            P(("seq", "ctx"), None),
            P(("seq", "ctx"), None),
            P(("seq", "ctx"), None),
            P(("seq", "ctx"), None),
            P("seq", "ctx"),
            P("seq", "ctx"),
            P("ctx", "seq"),
            P(("seq", "ctx")),
            P(("seq", "ctx")),
            P(("seq", "ctx")),
            P(("seq", "ctx")),
        ),
        check_vma=False,
    )
```

```python
from functools import partial

import jax
import jax.numpy as jnp
from jax import lax
from jax.experimental import pallas as pl
from jax.experimental.pallas import tpu as pltpu
from jax.sharding import PartitionSpec as P

QUERY_HEAD_COUNT = 8
KV_HEADS = 4
HEAD_FEATURES = 256


epsilon = 1e-06
softcap = 50.0
theta = 10000.0
floor_value = -1e30


def rms_scale(signal, weight):
    return signal * lax.rsqrt(jnp.mean(signal * signal, axis=-1, keepdims=True) + epsilon) * weight


def norm_back(signal, weight, upstream):
    outcome, pullback = jax.vjp(rms_scale, signal, weight)
    return pullback(upstream)


def gate_mix(gate_pre, up_pre):
    return jax.nn.gelu(gate_pre, approximate=True) * up_pre


def rotate(signal, positions, head_width):
    row_count = signal.shape[0]
    head_count = signal.shape[1] // head_width
    half_width = head_width // 2
    frequency = theta ** (-2.0 * jnp.arange(half_width, dtype=jnp.float32) / head_width)
    angles = positions.astype(jnp.float32)[:, None] * frequency[None, :]
    cosine = jnp.cos(angles)[:, None, :]
    sine_wave = jnp.sin(angles)[:, None, :]
    shaped = signal.reshape(row_count, head_count, head_width)
    first_half = shaped[:, :, :half_width]
    second = shaped[:, :, half_width:]
    turned = jnp.concatenate(
        [first_half * cosine - second * sine_wave, second * cosine + first_half * sine_wave], axis=2
    )
    return turned.reshape(row_count, head_count * head_width)


def block_scores(head_queries, key_all, key_pos, query_pos, block_rows, score_scale):
    block_keys = key_all.reshape(block_rows, KV_HEADS, HEAD_FEATURES)
    allowed = key_pos[None, :] <= query_pos[:, None]
    unscaled_score = (
        jnp.einsum("fwvi,hwi->wvfh", head_queries, block_keys, preferred_element_type=jnp.float32)
        * score_scale
    )
    bent_score = jnp.tanh(unscaled_score / softcap)
    capped = jnp.where(allowed, softcap * bent_score, floor_value)
    return (block_keys, allowed, bent_score, capped)


def attend(head_queries, key_all, value_all, query_pos, key_pos, score_scale):
    length_total = key_all.shape[0]
    block_count = max(1, length_total // 2048)
    block_rows = length_total // block_count
    row_count = head_queries.shape[0]
    group_size = head_queries.shape[2]

    def total_step(block_index, carried):
        running_max, running_sum = carried
        block_keys, allowed, bent_score, capped = block_scores(
            head_queries, key_all, key_pos, query_pos, block_rows, score_scale
        )
        new_max = jnp.maximum(running_max, jnp.max(capped, axis=-1))
        added = jnp.sum(jnp.where(allowed, jnp.exp(capped - new_max[..., None]), 0.0), axis=-1)
        return (new_max, running_sum * jnp.exp(running_max - new_max) + added)

    start_max = jnp.full((KV_HEADS, group_size, row_count), floor_value, jnp.float32)
    start_sum = jnp.zeros((KV_HEADS, group_size, row_count), jnp.float32)
    running_max, running_sum = lax.fori_loop(0, block_count, total_step, (start_max, start_sum))
    log_total = running_max + jnp.log(running_sum)

    def mix_step(block_index, carried):
        accum, rest_acc = carried
        block_keys, allowed, bent_score, capped = block_scores(
            head_queries, key_all, key_pos, query_pos, block_rows, score_scale
        )
        block_values = value_all.reshape(block_rows, KV_HEADS, HEAD_FEATURES)
        prob_full = jnp.where(allowed, jnp.exp(capped - log_total[..., None]), 0.0)
        lowered_probs = prob_full.astype(jnp.bfloat16)
        remaining_probs = (prob_full - lowered_probs.astype(jnp.float32)).astype(jnp.bfloat16)
        accum = accum + jnp.einsum(
            "xmbe,exk->bxmk", lowered_probs, block_values, preferred_element_type=jnp.float32
        )
        rest_acc = rest_acc + jnp.einsum(
            "xmbe,exk->bxmk", remaining_probs, block_values, preferred_element_type=jnp.float32
        )
        return (accum, rest_acc)

    start_mix = jnp.zeros((row_count, KV_HEADS, group_size, HEAD_FEATURES), jnp.float32)
    full_mixture, rest_acc = lax.fori_loop(0, block_count, mix_step, (start_mix, start_mix))
    exact_mixture = full_mixture + rest_acc
    return (
        log_total,
        full_mixture.reshape(row_count, QUERY_HEAD_COUNT * HEAD_FEATURES),
        exact_mixture,
    )


def attend_back(
    head_queries,
    key_all,
    value_all,
    query_pos,
    key_pos,
    score_scale,
    log_total,
    exact_mixture,
    mixed_grad,
):
    length_total = key_all.shape[0]
    block_count = max(1, length_total // 2048)
    block_rows = length_total // block_count
    row_count = head_queries.shape[0]
    group_size = head_queries.shape[2]
    head_gradient = mixed_grad.reshape(row_count, KV_HEADS, group_size, HEAD_FEATURES)
    row_difference = jnp.einsum("ozlq,ozlq->zlo", head_gradient.astype(jnp.float32), exact_mixture)

    def grad_step(block_index, carried):
        query_acc, key_acc, value_acc = carried
        block_keys, allowed, bent_score, capped = block_scores(
            head_queries, key_all, key_pos, query_pos, block_rows, score_scale
        )
        block_values = value_all.reshape(block_rows, KV_HEADS, HEAD_FEATURES)
        prob_full = jnp.where(allowed, jnp.exp(capped - log_total[..., None]), 0.0)
        lowered_probs = prob_full.astype(jnp.bfloat16)
        value_part = jnp.einsum(
            "zwcv,czwy->vzy", lowered_probs, head_gradient, preferred_element_type=jnp.float32
        )
        prob_grad = jnp.einsum(
            "fwvi,hwi->wvfh", head_gradient, block_values, preferred_element_type=jnp.float32
        )
        lowered_logits = (
            prob_full * (prob_grad - row_difference[..., None]) * (1.0 - bent_score * bent_score)
        ).astype(jnp.bfloat16)
        query_acc = (
            query_acc
            + jnp.einsum(
                "xmbe,exk->bxmk", lowered_logits, block_keys, preferred_element_type=jnp.float32
            )
            * score_scale
        )
        key_part = (
            jnp.einsum(
                "zwcv,czwy->vzy", lowered_logits, head_queries, preferred_element_type=jnp.float32
            )
            * score_scale
        )
        key_acc = key_part.reshape(block_rows, KV_HEADS * HEAD_FEATURES)
        value_acc = value_part.reshape(block_rows, KV_HEADS * HEAD_FEATURES)
        return (query_acc, key_acc, value_acc)

    start = (
        jnp.zeros((row_count, KV_HEADS, group_size, HEAD_FEATURES), jnp.float32),
        jnp.zeros((length_total, KV_HEADS * HEAD_FEATURES), jnp.float32),
        jnp.zeros((length_total, KV_HEADS * HEAD_FEATURES), jnp.float32),
    )
    query_acc, key_acc, value_acc = lax.fori_loop(0, block_count, grad_step, start)
    return (query_acc.reshape(row_count, QUERY_HEAD_COUNT * HEAD_FEATURES), key_acc, value_acc)


def context_body(
    tokens,
    w_query,
    w_key,
    w_value,
    w_output,
    w_gate,
    w_up,
    w_down,
    first_gain,
    second_gain,
    third_gain,
    fourth_gain,
    block_pairs,
    cotangent,
):
    query_full, key_full, value_full, output_full, gain_one, gain_two, gain_three, gain_four = (
        lax.all_gather(w_query, ("seq", "ctx"), axis=0, tiled=True),
        lax.all_gather(w_key, ("seq", "ctx"), axis=0, tiled=True),
        lax.all_gather(w_value, ("seq", "ctx"), axis=0, tiled=True),
        lax.all_gather(w_output, ("seq", "ctx"), axis=0, tiled=True),
        lax.all_gather(first_gain, ("seq", "ctx"), axis=0, tiled=True),
        lax.all_gather(second_gain, ("seq", "ctx"), axis=0, tiled=True),
        lax.all_gather(third_gain, ("seq", "ctx"), axis=0, tiled=True),
        lax.all_gather(fourth_gain, ("seq", "ctx"), axis=0, tiled=True),
    )
    gain_one = gain_one.astype(jnp.float32)
    gain_two = gain_two.astype(jnp.float32)
    gain_three = gain_three.astype(jnp.float32)
    gain_four = gain_four.astype(jnp.float32)
    row_count = tokens.shape[0]
    block_size = row_count // 2
    group_size = QUERY_HEAD_COUNT // KV_HEADS
    score_scale = HEAD_FEATURES ** (-0.5)
    own_pair = lax.dynamic_index_in_dim(block_pairs, lax.axis_index("ctx"), 0, keepdims=False)
    offsets = jnp.arange(block_size, dtype=jnp.int32)
    query_pos = jnp.concatenate(
        [own_pair[0] * block_size + offsets, own_pair[1] * block_size + offsets]
    )
    key_pos = (block_pairs[:, :, None] * block_size + offsets[None, None, :]).reshape(-1)
    residual_in = tokens.astype(jnp.float32)
    normed = rms_scale(residual_in, gain_one).astype(jnp.bfloat16)
    query_proj = jnp.dot(normed, query_full, preferred_element_type=jnp.float32)
    key_proj = jnp.dot(normed, key_full, preferred_element_type=jnp.float32)
    value_proj = jnp.dot(normed, value_full, preferred_element_type=jnp.float32)
    query_low = rotate(query_proj, query_pos, HEAD_FEATURES).astype(jnp.bfloat16)
    key_low = rotate(key_proj, query_pos, HEAD_FEATURES).astype(jnp.bfloat16)
    lowered_values = value_proj.astype(jnp.bfloat16)
    key_all, value_all = (
        lax.all_gather(key_low, "ctx", axis=0, tiled=True),
        lax.all_gather(lowered_values, "ctx", axis=0, tiled=True),
    )
    head_queries = query_low.reshape(row_count, KV_HEADS, group_size, HEAD_FEATURES)
    log_total, full_mixture, exact_mixture = attend(
        head_queries, key_all, value_all, query_pos, key_pos, score_scale
    )
    mixed_low = full_mixture.astype(jnp.bfloat16)
    branch = jnp.dot(mixed_low, output_full, preferred_element_type=jnp.float32)
    residual = residual_in + rms_scale(branch, gain_two)
    feed_input = rms_scale(residual, gain_three).astype(jnp.bfloat16)
    part_gate, part_up, part_down = (
        lax.all_gather(w_gate, "seq", axis=0, tiled=True),
        lax.all_gather(w_up, "seq", axis=0, tiled=True),
        lax.all_gather(w_down, "seq", axis=1, tiled=True),
    )
    feed_all = lax.all_gather(feed_input, "ctx", axis=0, tiled=True)
    gate_pre = jnp.dot(feed_all, part_gate, preferred_element_type=jnp.float32)
    up_pre = jnp.dot(feed_all, part_up, preferred_element_type=jnp.float32)
    hidden = gate_mix(gate_pre, up_pre).astype(jnp.bfloat16)
    feed_out = lax.psum_scatter(
        jnp.dot(hidden, part_down, preferred_element_type=jnp.float32).astype(jnp.bfloat16),
        "ctx",
        scatter_dimension=0,
        tiled=True,
    ).astype(jnp.float32)
    layer_out = (residual + rms_scale(feed_out, gain_four)).astype(jnp.bfloat16)
    upstream = cotangent.astype(jnp.float32)
    feed_grad, fourth_term = norm_back(feed_out, gain_four, upstream)
    feed_low = feed_grad.astype(jnp.bfloat16)
    cotangent_all = lax.all_gather(feed_low, "ctx", axis=0, tiled=True)
    hidden_grad = jnp.einsum(
        "td,fd->tf", cotangent_all, part_down, preferred_element_type=jnp.float32
    )
    outcome, mix_pull = jax.vjp(gate_mix, gate_pre, up_pre)
    gate_grad, up_grad = mix_pull(hidden_grad)
    gate_low = gate_grad.astype(jnp.bfloat16)
    up_low = up_grad.astype(jnp.bfloat16)
    input_part = jnp.einsum(
        "tf,df->td", gate_low, part_gate, preferred_element_type=jnp.float32
    ) + jnp.einsum("tf,df->td", up_low, part_up, preferred_element_type=jnp.float32)
    feed_input_grad = lax.psum_scatter(
        input_part.astype(jnp.bfloat16), "ctx", scatter_dimension=0, tiled=True
    ).astype(jnp.float32)
    gate_term = jnp.einsum("tf,td->fd", gate_low, feed_all, preferred_element_type=jnp.float32)
    up_term = jnp.einsum("tf,td->fd", up_low, feed_all, preferred_element_type=jnp.float32)
    down_term = jnp.einsum("tf,td->fd", hidden, cotangent_all, preferred_element_type=jnp.float32)
    gate_sum, up_sum, down_sum = (
        lax.psum_scatter(
            gate_term.astype(jnp.bfloat16), "seq", scatter_dimension=1, tiled=True
        ).astype(jnp.float32),
        lax.psum_scatter(
            up_term.astype(jnp.bfloat16), "seq", scatter_dimension=1, tiled=True
        ).astype(jnp.float32),
        lax.psum_scatter(
            down_term.astype(jnp.bfloat16), "seq", scatter_dimension=1, tiled=True
        ).astype(jnp.float32),
    )
    middle_grad, third_term = norm_back(residual, gain_three, feed_input_grad)
    residual_grad = upstream + middle_grad
    branch_grad, second_term = norm_back(branch, gain_two, residual_grad)
    branch_low = branch_grad.astype(jnp.bfloat16)
    output_term = jnp.einsum("th,td->hd", mixed_low, branch_low, preferred_element_type=jnp.float32)
    mixed_grad = jnp.einsum(
        "td,hd->th", branch_low, output_full, preferred_element_type=jnp.float32
    ).astype(jnp.bfloat16)
    query_sum, key_acc, value_acc = attend_back(
        head_queries,
        key_all,
        value_all,
        query_pos,
        key_pos,
        score_scale,
        log_total,
        exact_mixture,
        mixed_grad,
    )
    key_own, value_own = (
        lax.psum_scatter(
            key_acc.astype(jnp.bfloat16), "ctx", scatter_dimension=0, tiled=True
        ).astype(jnp.float32),
        lax.psum_scatter(
            value_acc.astype(jnp.bfloat16), "ctx", scatter_dimension=0, tiled=True
        ).astype(jnp.float32),
    )
    query_grad = rotate(query_sum, -query_pos, HEAD_FEATURES).astype(jnp.bfloat16)
    key_grad = rotate(key_own, -query_pos, HEAD_FEATURES).astype(jnp.bfloat16)
    value_grad = value_own.astype(jnp.bfloat16)
    normed_grad = jnp.einsum(
        "th,dh->td", query_grad, query_full, preferred_element_type=jnp.float32
    )
    normed_grad = normed_grad + jnp.einsum(
        "th,dh->td", key_grad, key_full, preferred_element_type=jnp.float32
    )
    normed_grad = normed_grad + jnp.einsum(
        "th,dh->td", value_grad, value_full, preferred_element_type=jnp.float32
    )
    query_term = jnp.einsum("td,th->dh", normed, query_grad, preferred_element_type=jnp.float32)
    key_term = jnp.einsum("td,th->dh", normed, key_grad, preferred_element_type=jnp.float32)
    value_term = jnp.einsum("td,th->dh", normed, value_grad, preferred_element_type=jnp.float32)
    input_grad, first_term = norm_back(residual_in, gain_one, normed_grad)
    grad_tokens = (residual_grad + input_grad).astype(jnp.bfloat16)
    grad_sums = (
        lax.psum_scatter(query_term, ("seq", "ctx"), scatter_dimension=0, tiled=True),
        lax.psum_scatter(key_term, ("seq", "ctx"), scatter_dimension=0, tiled=True),
        lax.psum_scatter(value_term, ("seq", "ctx"), scatter_dimension=0, tiled=True),
        lax.psum_scatter(output_term, ("seq", "ctx"), scatter_dimension=0, tiled=True),
        lax.psum_scatter(first_term, ("seq", "ctx"), scatter_dimension=0, tiled=True),
        lax.psum_scatter(second_term, ("seq", "ctx"), scatter_dimension=0, tiled=True),
        lax.psum_scatter(third_term, ("seq", "ctx"), scatter_dimension=0, tiled=True),
        lax.psum_scatter(fourth_term, ("seq", "ctx"), scatter_dimension=0, tiled=True),
    )
    return (
        layer_out,
        grad_tokens,
        grad_sums[0],
        grad_sums[1],
        grad_sums[2],
        grad_sums[3],
        gate_sum.T,
        up_sum.T,
        down_sum,
        grad_sums[4],
        grad_sums[5],
        grad_sums[6],
        grad_sums[7],
    )


CORES = 2
GELU_IN = 0.7978845608
GELU_CUBE = 0.044715
VMEM_LIMIT = 56 * 2**20


def wide(value):
    return value.astype(jnp.float32)


def narrow(value):
    return value.astype(jnp.bfloat16)


def rms_parts(signal):
    scale = lax.rsqrt(jnp.mean(signal * signal, axis=-1, keepdims=True) + epsilon)
    return scale, signal * scale


def rms_back(scale, unit, weight, upstream):
    weighted = upstream * weight
    mean = jnp.mean(weighted * unit, axis=-1, keepdims=True)
    return scale * (weighted - unit * mean), jnp.sum(upstream * unit, axis=0)


def dot_nn(left, right):
    return jnp.dot(left, right, preferred_element_type=jnp.float32)


def dot_nt(left, right):
    return jnp.einsum("ab,cb->ac", left, right, preferred_element_type=jnp.float32)


def dot_tn(left, right):
    return jnp.einsum("ab,ac->bc", left, right, preferred_element_type=jnp.float32)


def after(value, *others):
    anywhere = pl.BlockSpec(memory_space=pl.ANY)
    return pl.pallas_call(
        lambda *refs: None,
        in_specs=[anywhere] * (1 + len(others)),
        out_specs=anywhere,
        out_shape=jax.ShapeDtypeStruct(value.shape, value.dtype),
        input_output_aliases={0: 0},
    )(value, *others)


def copied(value, rows, *others):
    columns = value.shape[1]
    part = pl.BlockSpec((rows // 4, columns), lambda i: (i, 0))

    def kernel(*refs):
        refs[-1][...] = refs[0][...]

    return pl.pallas_call(
        kernel,
        grid=(4,),
        in_specs=[part] + [pl.BlockSpec(memory_space=pl.ANY)] * len(others),
        out_specs=part,
        out_shape=jax.ShapeDtypeStruct((rows, columns), value.dtype),
    )(value, *others)


def fresh(shape, dtype, *others):
    anywhere = pl.BlockSpec(memory_space=pl.ANY)
    return pl.pallas_call(
        lambda *refs: None,
        in_specs=[anywhere] * len(others),
        out_specs=anywhere,
        out_shape=jax.ShapeDtypeStruct(shape, dtype),
    )(*others)


def lull(*others):
    anywhere = pl.BlockSpec(memory_space=pl.ANY)
    return pl.pallas_call(
        lambda *refs: None,
        in_specs=[anywhere] * len(others),
        out_specs=anywhere,
        out_shape=jax.ShapeDtypeStruct((8, 128), jnp.float32),
        cost_estimate=pl.CostEstimate(flops=10**12, bytes_accessed=0, transcendentals=0),
    )(*others)


class Order:
    def __init__(self):
        self.last = ()

    def pin(self, value, sent=None):
        extra = () if sent is None else (lull(sent),)
        value = after(value, *self.last, *extra)
        self.last = (value,)
        return value

    def mark(self, value):
        self.last = (value,)

    def late(self, value, rows):
        return copied(value, rows, *self.last)

    def hold(self, value):
        return after(value, *self.last)


class Moves:
    def __init__(self, n_seq, n_ctx):
        self.n_seq, self.n_ctx = n_seq, n_ctx
        self.line = n_ctx // CORES
        self.seq = lax.axis_index("seq")
        self.ctx = lax.axis_index("ctx")
        self.plane = self.ctx // CORES
        self.core = self.ctx % CORES

    def _send(self, value, move):
        pairs = []
        for s in range(self.n_seq):
            for c in range(self.n_ctx):
                t = move(s, c // CORES, c % CORES)
                pairs.append((s * self.n_ctx + c, t[0] * self.n_ctx + t[1] * CORES + t[2]))
        return lax.ppermute(value, ("seq", "ctx"), pairs)

    def across(self, value, mask):
        return self._send(value, lambda s, z, k: (s ^ mask, z, k))

    def along(self, value, step):
        return self._send(value, lambda s, z, k: (s, (z + step) % self.line, k))

    def plane_swap(self, value, mask):
        return self._send(value, lambda s, z, k: (s, z ^ mask, k))

    def swap(self, value):
        return self._send(value, lambda s, z, k: (s, z, k ^ 1))

    def gather_halves(self, low, high, gate):
        low_near = self.across(low, 2)
        high_near = self.across(high, 1)
        yield None
        low_near, high_near = gate(low_near, low), gate(high_near)
        low_two, high_two = jnp.stack([low, low_near]), jnp.stack([high, high_near])
        low_far = self.across(low_two, 1)
        high_far = self.across(high_two, 2)
        yield None
        yield low_near, high_near, gate(low_far, low_two), gate(high_far)

    def scatter_whole(self, terms, mask, gate, ready=lambda v: v):
        other = 3 - mask
        pick = lambda m: lax.dynamic_index_in_dim(terms, self.seq ^ m, 0, False)
        sent = ready(jnp.stack([pick(mask), pick(3)]))
        near = self.across(sent, mask)
        yield None
        near = gate(near, sent)
        onward = narrow(wide(pick(other)) + wide(near[1]))
        far = self.across(onward, other)
        yield None
        yield wide(pick(0)) + wide(near[0]) + wide(gate(far, onward))

    def scatter_halves(self, terms, gate, ready=lambda v: v):
        half = terms.shape[1] // 2
        low = self.scatter_whole(terms[:, :half], 1, gate, ready)
        high = self.scatter_whole(terms[:, half:], 2, gate, ready)
        for _ in range(2):
            next(low), next(high)
            yield None
        yield jnp.concatenate([next(low), next(high)], axis=0)

    def exchange_line(self, blocks):
        out = fresh(blocks.shape, blocks.dtype, blocks)
        own = lax.dynamic_index_in_dim(blocks, self.plane, 0, False)
        out = lax.dynamic_update_index_in_dim(out, own, self.plane, 0)
        for step in range(1, self.line):
            sent = lax.dynamic_index_in_dim(blocks, (self.plane + step) % self.line, 0, False)
            got = self.along(sent, step)
            out = lax.dynamic_update_index_in_dim(out, got, (self.plane - step) % self.line, 0)
        return out

    def transpose_chips(self, value):
        return self._send(value, lambda s, z, k: (z, s, k))

    def exchange_cores(self, blocks):
        own = lax.dynamic_index_in_dim(blocks, self.core, 0, False)
        got = self.swap(lax.dynamic_index_in_dim(blocks, 1 - self.core, 0, False))
        first = self.core == 0
        return jnp.stack([jnp.where(first, own, got), jnp.where(first, got, own)])


ANYWHERE = pl.BlockSpec(memory_space=pl.ANY)


def tile(rows, columns):
    return pl.BlockSpec((rows, columns), lambda i: (i, 0))


def whole(*shape):
    return pl.BlockSpec(shape, lambda i: (0,) * len(shape))


def call(kernel, steps, in_specs, out_specs, out_shape, flops, args, scratch=(), others=()):
    count = len(args)

    def body(*refs):
        kernel(*refs[:count], *refs[count + len(others) :])

    return pl.pallas_call(
        body,
        grid=(steps,),
        in_specs=in_specs + [ANYWHERE] * len(others),
        out_specs=out_specs,
        out_shape=out_shape,
        scratch_shapes=list(scratch),
        compiler_params=pltpu.CompilerParams(vmem_limit_bytes=VMEM_LIMIT),
        cost_estimate=pl.CostEstimate(flops=flops, bytes_accessed=0, transcendentals=0),
    )(*args, *others)


def array(dtype, *shape):
    return jax.ShapeDtypeStruct(shape, dtype)


def mul_nt(left, right):
    return lax.dot_general(
        left, right, (((1,), (1,)), ((), ())), preferred_element_type=jnp.float32
    )


def mul_tn(left, right):
    return lax.dot_general(
        left, right, (((0,), (0,)), ((), ())), preferred_element_type=jnp.float32
    )


def turn_pair(value, cosine, sine):
    half = value.shape[1] // 2
    first, second = value[:, :half], value[:, half:]
    return jnp.concatenate(
        [first * cosine - second * sine, second * cosine + first * sine], axis=1
    )


BF16, F32 = jnp.bfloat16, jnp.float32
TILE = 256


def load(copies, sems):
    started = [pltpu.make_async_copy(a, b, sems.at[i]) for i, (a, b) in enumerate(copies)]
    for copy in started:
        copy.start()
    return started


def whole_copies(seq, pieces, target, left):
    mask, own, near, far, last = pieces
    rows = own.shape[0]
    near = near.at[pl.ds(0, rows)]
    columns = pl.ds(left, own.shape[1])
    at = lambda m: target.at[pl.ds(pl.multiple_of((seq ^ m) * rows, 64), rows), columns]
    other = 3 - mask
    return [(own, at(0)), (near, at(mask)), (far, at(other)), (last, at(3))]


def half_copies(seq, pieces, target):
    own, low_near, high_near, low_far, high_far = pieces
    rows = own.shape[0]
    half = rows // 2
    last = pl.ds(low_near.shape[0] - half, half)
    low_near, high_near = low_near.at[last], high_near.at[last]
    at = lambda m, h: target.at[pl.ds(pl.multiple_of((seq ^ m) * rows + h * half, 32), half)]
    return [
        (own, target.at[pl.ds(pl.multiple_of(seq * rows, 64), rows)]),
        (low_near, at(2, 0)),
        (high_near, at(1, 1)),
        (low_far.at[0], at(1, 0)),
        (low_far.at[1], at(3, 0)),
        (high_far.at[0], at(2, 1)),
        (high_far.at[1], at(3, 1)),
    ]


SCALARS = pl.BlockSpec(memory_space=pltpu.SMEM)


def project_rows(place, tokens, pieces, feats, tables):
    rows, width = tokens.shape
    wide_columns = pieces[0].shape[1]

    def kernel(place_ref, x_ref, own, near_a, near_b, far_a, far_b, cq, sq, cp, sp, *refs):
        normed_ref, query_ref, pair_ref, gains_ref, w_ref, sems = refs

        @pl.when(pl.program_id(0) == 0)
        def _():
            copies = half_copies(place_ref[2], (own, near_a, near_b, far_a, far_b), w_ref)
            for copy in load(copies, sems):
                copy.wait()
            pad = wide_columns - 2 * feats
            rows8 = lax.broadcasted_iota(jnp.int32, (8, pad), 0)
            columns8 = lax.broadcasted_iota(jnp.int32, (8, pad), 1)
            picks = (rows8 == columns8).astype(BF16)
            gains_ref[...] = mul_nt(picks, w_ref[:, 2 * feats :])

        x = x_ref[...].astype(F32)
        scale = lax.rsqrt(jnp.mean(x * x, axis=-1, keepdims=True) + epsilon)
        normed = (x * scale * gains_ref[0:1]).astype(BF16)
        normed_ref[...] = normed
        both = dot_nn(normed, w_ref[:, : 2 * feats])
        query_ref[...] = turn_pair(both[:, :feats], cq[...], sq[...]).astype(BF16)
        pair_ref[...] = turn_pair(both[:, feats:], cp[...], sp[...]).astype(BF16)

    half = feats // 2
    return call(
        kernel,
        rows // TILE,
        [SCALARS, tile(TILE, width)] + [ANYWHERE] * 5 + [tile(TILE, half)] * 4,
        [tile(TILE, width), tile(TILE, feats), tile(TILE, feats), whole(8, width)],
        [
            array(BF16, rows, width),
            array(BF16, rows, feats),
            array(BF16, rows, feats),
            array(F32, 8, width),
        ],
        4 * rows * width * feats,
        (place, tokens) + pieces + tables,
        [pltpu.VMEM((width, wide_columns), BF16), pltpu.SemaphoreType.DMA((7,))],
    )


def soft_rows(query, keys, place, places):
    bent = jnp.tanh(mul_nt(query, keys) * (HEAD_FEATURES ** (-0.5) / softcap))
    weight = jnp.where(places <= place, jnp.exp(softcap * bent), 0.0)
    return bent, weight / jnp.sum(weight, axis=-1, keepdims=True)


def attend_head(query, key, value, place, places, others):
    rows, feats = query.shape

    def kernel(q_ref, k_ref, v_ref, place_ref, places_ref, out_ref):
        _, probs = soft_rows(q_ref[...], k_ref[...], place_ref[...], places_ref[...])
        out_ref[...] = dot_nn(probs.astype(BF16), v_ref[...]).astype(BF16)

    return call(
        kernel,
        rows // TILE,
        [tile(TILE, feats), whole(rows, feats), whole(rows, feats), tile(TILE, 1), whole(1, rows)],
        [tile(TILE, feats)],
        [array(BF16, rows, feats)],
        4 * rows * rows * feats,
        (query, key, value, place, places),
        (),
        others,
    )[0]


def attend_head_back(
    place, query, key, value, branch, w_out, spot, spots, cosine, sine, others
):
    rows, feats = query.shape
    width = branch.shape[1]
    score_scale = HEAD_FEATURES ** (-0.5)
    steps = rows // TILE

    def kernel(place_ref, q_ref, k_ref, v_ref, b_ref, w_ref, spot_ref, spots_ref, c_ref, s_ref, *refs):
        dq, own_ref, send_ref, dk, dv = refs
        step = pl.program_id(0)

        @pl.when(step == 0)
        def _():
            dk[...] = jnp.zeros_like(dk)
            dv[...] = jnp.zeros_like(dv)

        query, keys = q_ref[...], k_ref[...]
        grad = mul_nt(b_ref[...], w_ref[...]).astype(BF16)
        bent, probs = soft_rows(query, keys, spot_ref[...], spots_ref[...])
        prob_grad = mul_nt(grad, v_ref[...])
        delta = jnp.sum(probs * prob_grad, axis=-1, keepdims=True)
        raw = (probs * (prob_grad - delta) * (1.0 - bent * bent)).astype(BF16)
        total = dot_nn(raw, keys) * score_scale
        dq[...] = turn_pair(total, c_ref[...], -s_ref[...]).astype(BF16)
        dk[...] += mul_tn(raw, query) * score_scale
        dv[...] += mul_tn(probs.astype(BF16), grad)

        @pl.when(step == steps - 1)
        def _():
            first = place_ref[1] == 0
            own_ref[...] = jnp.where(first, dk[...], dv[...])
            send_ref[...] = jnp.where(first, dv[...], dk[...])

    return call(
        kernel,
        steps,
        [SCALARS, tile(TILE, feats), whole(rows, feats), whole(rows, feats), tile(TILE, width)]
        + [whole(feats, width), tile(TILE, 1), whole(1, rows)]
        + [tile(TILE, feats // 2), tile(TILE, feats // 2)],
        [tile(TILE, feats), whole(rows, feats), whole(rows, feats)],
        [array(BF16, rows, feats), array(F32, rows, feats), array(F32, rows, feats)],
        10 * rows * rows * feats + 2 * rows * width * feats,
        (place, query, key, value, branch, w_out, spot, spots, cosine, sine),
        [pltpu.VMEM((rows, feats), F32)] * 2,
        others,
    )


OUT_ORDER = ((0, 0), (0, 2), (0, 1), (0, 3), (2, 0), (2, 2), (1, 1), (1, 3)) + (
    ((1, 0), (1, 2), (3, 0), (3, 2), (2, 1), (2, 3), (3, 1), (3, 3))
)


def branch_rows(place, mixed, own, other, tokens, gain_two, gain_three):
    heads, rows, feats = mixed.shape
    blocks, out_rows, width = own.shape
    own_rows = TILE // CORES
    planes = 4

    def kernel(
        place_ref,
        m_ref,
        own_ref,
        other_ref,
        x_ref,
        two_ref,
        three_ref,
        out_ref,
        mine_ref,
        full_ref,
        w_ref,
        sems,
        full_sem,
    ):
        step = pl.program_id(0)
        plane, core, seq = place_ref[0], place_ref[1], place_ref[2]
        keep = pltpu.make_async_copy(w_ref, full_ref, full_sem)

        @pl.when(step == 0)
        def _():
            copies = []
            for i, (m, x) in enumerate(OUT_ORDER):
                at = (seq ^ m) * planes + (plane ^ x)
                copies.append((own_ref.at[i], w_ref.at[at, core]))
                copies.append((other_ref.at[i], w_ref.at[at, 1 - core]))
            for copy in load(copies, sems):
                copy.wait()
            keep.start()

        rows_in = jnp.concatenate([m_ref[h] for h in range(heads)], axis=1)
        branch = dot_nn(rows_in, w_ref[...].reshape(heads * feats, width))

        @pl.when(step == plane)
        def _():
            mine_ref[...] = jnp.where(core == 0, branch[:own_rows], branch[own_rows:])

        scale = lax.rsqrt(jnp.mean(branch * branch, axis=-1, keepdims=True) + epsilon)
        residual = x_ref[...].astype(F32) + branch * scale * two_ref[...]
        scale = lax.rsqrt(jnp.mean(residual * residual, axis=-1, keepdims=True) + epsilon)
        out_ref[...] = (residual * scale * three_ref[...]).astype(BF16)

        @pl.when(step == rows // TILE - 1)
        def _():
            keep.wait()

    return call(
        kernel,
        rows // TILE,
        [
            SCALARS,
            pl.BlockSpec((heads, TILE, feats), lambda i: (0, i, 0)),
            ANYWHERE,
            ANYWHERE,
            tile(TILE, width),
            whole(1, width),
            whole(1, width),
        ],
        [tile(TILE, width), whole(own_rows, width), ANYWHERE],
        [
            array(BF16, rows, width),
            array(F32, own_rows, width),
            array(BF16, blocks, CORES, out_rows, width),
        ],
        2 * heads * rows * feats * width,
        (place, mixed, own, other, tokens, gain_two, gain_three),
        [
            pltpu.VMEM((blocks, CORES, out_rows, width), BF16),
            pltpu.SemaphoreType.DMA((2 * blocks,)),
            pltpu.SemaphoreType.DMA,
        ],
    )


def feed_open(place, feed, gate_pieces, up_pieces):
    rows, width = feed.shape
    units = gate_pieces[0].shape[1]

    def kernel(place_ref, x_ref, *refs):
        gates, ups = refs[:4], refs[4:8]
        hidden_ref, gate_ref, up_ref, w_ref, sems = refs[8:]

        @pl.when(pl.program_id(0) == 0)
        def _():
            copies = whole_copies(place_ref[2], (1,) + gates, w_ref, 0)
            copies += whole_copies(place_ref[2], (2,) + ups, w_ref, units)
            for copy in load(copies, sems):
                copy.wait()

        both = dot_nn(x_ref[...], w_ref[...])
        gate, up = both[:, :units], both[:, units:]
        square = gate * gate
        bend = jnp.tanh(GELU_IN * (gate + GELU_CUBE * square * gate))
        half = 0.5 * (1.0 + bend)
        gelu = half * gate
        slope = half + 0.5 * gate * (1.0 - bend * bend) * (
            GELU_IN + 3.0 * GELU_IN * GELU_CUBE * square
        )
        hidden_ref[...] = (gelu * up).astype(BF16)
        gate_ref[...] = (up * slope).astype(BF16)
        up_ref[...] = gelu.astype(BF16)

    return call(
        kernel,
        rows // TILE,
        [SCALARS, tile(TILE, width)] + [ANYWHERE] * 8,
        [tile(TILE, units)] * 3,
        [array(BF16, rows, units)] * 3,
        4 * rows * width * units,
        (place, feed) + gate_pieces + up_pieces,
        [pltpu.VMEM((width, 2 * units), BF16), pltpu.SemaphoreType.DMA((8,))],
    )


def feed_close(place, hidden, down_pieces):
    rows, units = hidden.shape
    width = down_pieces[0].shape[0] * 4

    def kernel(place_ref, x_ref, *refs):
        out_ref, dw_ref, sems = refs[5:]

        @pl.when(pl.program_id(0) == 0)
        def _():
            for copy in load(half_copies(place_ref[2], refs[:5], dw_ref), sems):
                copy.wait()

        out_ref[...] = mul_nt(x_ref[...], dw_ref[...]).astype(BF16)

    return call(
        kernel,
        rows // TILE,
        [SCALARS, tile(TILE, units)] + [ANYWHERE] * 5,
        [tile(TILE, width)],
        [array(BF16, rows, width)],
        2 * rows * width * units,
        (place, hidden) + down_pieces,
        [pltpu.VMEM((width, units), BF16), pltpu.SemaphoreType.DMA((7,))],
    )[0]


def feed_back(
    place, grad, gate_factor, up_factor, gate_pieces, up_pieces, down_pieces, others
):
    rows, width = grad.shape
    units = gate_factor.shape[1]

    def kernel(place_ref, g_ref, gf_ref, uf_ref, *refs):
        gates, ups, downs = refs[:4], refs[4:8], refs[8:13]
        gate_ref, up_ref, out_ref, w_ref, dw_ref, both_ref, sems, down_sems = refs[13:]
        seq = place_ref[2]
        copies = whole_copies(seq, (1,) + gates, w_ref, 0)
        copies += whole_copies(seq, (2,) + ups, w_ref, units)
        first = pl.program_id(0) == 0

        @pl.when(first)
        def _():
            started = load(half_copies(seq, downs, dw_ref), down_sems)
            load(copies, sems)
            for copy in started:
                copy.wait()

        hidden_grad = dot_nn(g_ref[...], dw_ref[...])
        gate_low = (hidden_grad * gf_ref[...].astype(F32)).astype(BF16)
        up_low = (hidden_grad * uf_ref[...].astype(F32)).astype(BF16)
        gate_ref[...] = gate_low
        up_ref[...] = up_low
        both_ref[:, :units] = gate_low
        both_ref[:, units:] = up_low

        @pl.when(first)
        def _():
            for i, (a, b) in enumerate(copies):
                pltpu.make_async_copy(a, b, sems.at[i]).wait()

        out_ref[...] = mul_nt(both_ref[...], w_ref[...]).astype(BF16)

    return call(
        kernel,
        rows // TILE,
        [SCALARS, tile(TILE, width), tile(TILE, units), tile(TILE, units)] + [ANYWHERE] * 13,
        [tile(TILE, units), tile(TILE, units), tile(TILE, width)],
        [array(BF16, rows, units), array(BF16, rows, units), array(BF16, rows, width)],
        6 * rows * width * units,
        (place, grad, gate_factor, up_factor) + gate_pieces + up_pieces + down_pieces,
        [
            pltpu.VMEM((width, 2 * units), BF16),
            pltpu.VMEM((width, units), BF16),
            pltpu.VMEM((TILE, 2 * units), BF16),
            pltpu.SemaphoreType.DMA((8,)),
            pltpu.SemaphoreType.DMA((7,)),
        ],
        others,
    )


def qkv_back(normed, query_grad, own, other, cosine, sine, more, others):
    rows, feats = query_grad.shape
    width = normed.shape[1]
    block = 384
    both_columns = 2 * feats

    def kernel(n_ref, q_ref, own_ref, other_ref, c_ref, s_ref, more_ref, both_ref, out_ref):
        @pl.when(pl.program_id(0) == 0)
        def _():
            pair = turn_pair(own_ref[...] + other_ref[...], c_ref[...], -s_ref[...])
            both_ref[:, :feats] = q_ref[...]
            both_ref[:, feats:] = pair.astype(BF16)

        out_ref[:, :both_columns] = mul_tn(n_ref[...], both_ref[...]).astype(BF16)
        out_ref[:, both_columns:] = more_ref[...]

    total = both_columns + more.shape[1]
    return call(
        kernel,
        width // block,
        [pl.BlockSpec((rows, block), lambda i: (0, i))]
        + [whole(rows, feats)] * 3
        + [whole(rows, feats // 2)] * 2
        + [tile(block, more.shape[1])],
        [whole(rows, both_columns), tile(block, total)],
        [array(BF16, rows, both_columns), array(BF16, width, total)],
        2 * rows * width * both_columns,
        (normed, query_grad, own, other, cosine, sine, more),
        (),
        others,
    )


def normed_back(place, both, pieces, others):
    rows, both_columns = both.shape
    width, wide_columns = pieces[0].shape[0] * 4, pieces[0].shape[1]

    def kernel(place_ref, both_ref, *refs):
        out_ref, w_ref, sems = refs[5:]

        @pl.when(pl.program_id(0) == 0)
        def _():
            for copy in load(half_copies(place_ref[2], refs[:5], w_ref), sems):
                copy.wait()

        out_ref[...] = mul_nt(both_ref[...], w_ref[:, :both_columns]).astype(BF16)

    return call(
        kernel,
        rows // TILE,
        [SCALARS, tile(TILE, both_columns)] + [ANYWHERE] * 5,
        [tile(TILE, width)],
        [array(BF16, rows, width)],
        2 * rows * both_columns * width,
        (place, both) + pieces,
        [pltpu.VMEM((width, wide_columns), BF16), pltpu.SemaphoreType.DMA((7,))],
        others,
    )[0]


def weight_grad(left, right, block, others):
    rows, width = left.shape
    columns = right.shape[1]

    def kernel(left_ref, right_ref, out_ref):
        out_ref[...] = mul_tn(left_ref[...], right_ref[...]).astype(BF16)

    return call(
        kernel,
        width // block,
        [pl.BlockSpec((rows, block), lambda i: (0, i)), whole(rows, columns)],
        [tile(block, columns)],
        [array(BF16, width, columns)],
        2 * rows * width * columns,
        (left, right),
        (),
        others,
    )[0]


def own_grads(terms, weights, gain):
    heads, rows, columns = terms.shape
    feats = HEAD_FEATURES

    def kernel(terms_ref, wq, wk, wv, g_ref, dq, dk, dv, gains_ref, first_ref):
        total, first = 0.0, 0.0
        for h in range(heads):
            term = terms_ref[h].astype(F32)
            total += term[:, 2 * feats :]
            pair, w = ((dk, wk), (dv, wv))[h % CORES]
            group = h // CORES
            for out, weight, at, value in (
                (dq, wq, slice(h * feats, (h + 1) * feats), term[:, :feats]),
                (pair, w, slice(group * feats, (group + 1) * feats), term[:, feats : 2 * feats]),
            ):
                out[:, at] = value
                first += jnp.sum(weight[:, at].astype(F32) * value, axis=1, keepdims=True)
        gains_ref[...] = total
        first_ref[...] = first / g_ref[...].astype(F32)

    shapes = [w.shape for w in weights] + [(rows, columns - 2 * feats), (rows, 1)]
    return call(
        kernel,
        1,
        [whole(*terms.shape)] + [whole(*w.shape) for w in weights] + [whole(rows, 1)],
        [whole(*s) for s in shapes],
        [array(F32, *s) for s in shapes],
        0,
        (terms,) + weights + (gain,),
    )


def head_body(
    tokens,
    w_query,
    w_key,
    w_value,
    w_output,
    w_gate,
    w_up,
    w_down,
    first_gain,
    second_gain,
    third_gain,
    fourth_gain,
    block_pairs,
    cotangent,
    n_seq,
    n_ctx,
):
    moves = Moves(n_seq, n_ctx)
    order = Order()
    pin, hold = order.pin, order.hold
    line = moves.line
    core_zero = moves.core == 0
    rows, width = tokens.shape
    feat_rows = w_query.shape[0]
    out_rows = w_output.shape[0]
    feats = HEAD_FEATURES
    pad = 128
    gather = lambda v: lax.all_gather(v, "ctx", axis=0, tiled=True)
    to_all = lambda v: lax.all_to_all(v, "ctx", split_axis=0, concat_axis=0, tiled=True)
    scatter = lambda v: lax.psum_scatter(v, "ctx", scatter_dimension=0, tiled=True)

    place = jnp.stack([moves.plane, moves.core, moves.seq]).astype(jnp.int32)
    block = w_gate.shape[0]
    half = block // 2

    out_near = moves.plane_swap(w_output, 2)
    gains_in = jnp.stack([first_gain, second_gain, third_gain, fourth_gain], axis=1)
    gains_in = jnp.pad(gains_in, ((0, 0), (0, pad - 4)))
    by_head = jnp.concatenate(
        [
            w_query.reshape(feat_rows, line, CORES, feats),
            jnp.stack(
                [
                    w_key.reshape(feat_rows, line, feats),
                    w_value.reshape(feat_rows, line, feats),
                ],
                axis=2,
            ),
            jnp.broadcast_to(gains_in[:, None, None, :], (feat_rows, line, CORES, pad)),
        ],
        axis=3,
    ).transpose(2, 1, 0, 3)
    by_plane = moves.exchange_cores(by_head).transpose(1, 0, 2, 3)
    down_own = w_down.T
    near_x = moves.across(jnp.concatenate([w_gate, down_own[half:]]), 1)
    near_y = moves.across(jnp.concatenate([w_up, down_own[:half]]), 2)
    own_columns = moves.exchange_line(by_plane).reshape(n_ctx * feat_rows, 2 * feats + pad)
    own_columns = pin(own_columns, by_plane)
    tokens_in = hold(tokens)
    tokens_all = gather(tokens_in)
    columns_move = moves.gather_halves(own_columns[:half], own_columns[half:], pin)
    next(columns_move)
    near_x, near_y = pin(near_x), pin(near_y)
    out_two = pin(jnp.stack([w_output, pin(out_near)]))
    next(columns_move)
    gate_far = moves.across(hold(w_gate), 2)
    up_far = moves.across(hold(w_up), 1)

    block_size = rows // 2
    offsets = jnp.arange(block_size, dtype=jnp.int32)
    pos = (hold(block_pairs)[:, :, None] * block_size + offsets[None, None, :]).reshape(-1)
    spot, spots = pos[:, None], pos[None, :]
    frequency = theta ** (-2.0 * jnp.arange(feats // 2, dtype=jnp.float32) / feats)
    angles = wide(pos)[:, None] * frequency[None, :]
    cosine, sine = pin(jnp.cos(angles)), pin(jnp.sin(angles))
    pair_cosine = pin(jnp.where(core_zero, cosine, 1.0))
    pair_sine = pin(jnp.where(core_zero, sine, 0.0))
    tables = (cosine, sine, pair_cosine, pair_sine)

    columns = (own_columns,) + next(columns_move)
    out_two = hold(out_two)
    out_far = moves.plane_swap(out_two, 1)
    tokens_all = pin(tokens_all, tokens_in)

    normed, query, pair, gains = project_rows(place, tokens_all, columns, feats, tables)
    gain_one, gain_two, gain_three, gain_four = (gains[i : i + 1] for i in range(4))
    pair_other = moves.swap(pair)
    order.mark(pair)
    pair_other = pin(pair_other, pair)
    key = jnp.where(core_zero, pair, pair_other)
    value = jnp.where(core_zero, pair_other, pair)
    out_far = pin(out_far, out_two)
    mixed = pin(attend_head(query, key, value, spot, spots, order.last))
    mixed_all = lax.all_gather(mixed, "ctx", axis=0)

    out_move = moves.gather_halves(out_two, out_far, pin)
    next(out_move)
    next(out_move)
    gate_far, up_far = pin(gate_far), pin(up_far)
    gate_last, up_last = order.late(near_x, block), order.late(near_y, block)
    low_near, high_near, low_far, high_far = next(out_move)
    gate_last, up_last = moves.across(hold(gate_last), 2), moves.across(hold(up_last), 1)
    out_own = jnp.concatenate(
        [out_two, out_far, low_near, high_near, *(v.reshape(4, *v.shape[2:]) for v in (low_far, high_far))]
    )
    out_own = pin(out_own)
    out_other = moves.swap(out_own)
    low_two = pin(jnp.stack([down_own[:half], near_y[block:]]))
    high_two = pin(jnp.stack([down_own[half:], near_x[block:]]))
    out_other = pin(out_other, out_own)
    mixed_all = pin(mixed_all, mixed)
    feed_all, branch, w_full = branch_rows(
        place, mixed_all, out_own, out_other, tokens_all, gain_two, gain_three
    )
    order.mark(branch)
    gate_pieces = (w_gate, near_x, gate_far, pin(gate_last))
    up_pieces = (w_up, near_y, up_far, pin(up_last))
    down_low, down_high = moves.across(hold(low_two), 1), moves.across(hold(high_two), 2)
    hidden, gate_factor, up_factor = feed_open(place, feed_all, gate_pieces, up_pieces)
    order.mark(hidden)
    down_pieces = (down_own, near_y, near_x, pin(down_low), pin(down_high))
    feed_part = feed_close(place, hidden, down_pieces)
    order.mark(feed_part)
    feed_out = scatter(feed_part)

    scale_two, unit_two = rms_parts(hold(branch))
    residual = wide(tokens) + unit_two * gain_two
    scale_three, unit_three = rms_parts(residual)
    later = hold(place)
    w_out = lax.dynamic_slice_in_dim(
        w_full.reshape(-1, width), (later[0] * CORES + later[1]) * feats, feats, 0
    )
    w_out = pin(w_out)
    unit_two, unit_three, residual = pin(unit_two), pin(unit_three), pin(residual)

    upstream = wide(cotangent)
    feed_out = pin(feed_out, feed_part)
    scale_four, unit_four = rms_parts(wide(feed_out))
    layer_out = narrow(residual + unit_four * gain_four)
    feed_grad, fourth_term = rms_back(scale_four, unit_four, gain_four, upstream)
    feed_low = pin(narrow(feed_grad))
    grad_all = pin(gather(feed_low), feed_low)
    shape = (n_seq, block, hidden.shape[1])
    gate_low, up_low, input_part = feed_back(
        place, grad_all, gate_factor, up_factor, gate_pieces, up_pieces, down_pieces, order.last
    )
    order.mark(input_part)
    feed_input_grad = scatter(input_part)
    down_term = weight_grad(grad_all, hidden, 384, order.last).reshape(shape)
    order.mark(down_term)
    plain = lambda value, sent=None: pin(value)
    down_move = moves.scatter_halves(down_term, plain)
    next(down_move)
    gate_term = weight_grad(feed_all, gate_low, 384, order.last).reshape(shape)
    order.mark(gate_term)
    gate_move = moves.scatter_whole(gate_term, 1, plain)
    next(gate_move)
    up_term = weight_grad(feed_all, up_low, 384, order.last).reshape(shape)
    order.mark(up_term)
    up_move = moves.scatter_whole(up_term, 2, plain)
    next(up_move)
    next(down_move)
    feed_input_grad = wide(pin(feed_input_grad, input_part))
    middle_grad, third_term = rms_back(scale_three, unit_three, gain_three, feed_input_grad)
    residual_grad = upstream + middle_grad
    branch_grad, second_term = rms_back(scale_two, unit_two, gain_two, residual_grad)
    branch_low = pin(narrow(branch_grad))

    branch_all = gather(branch_low)
    next(gate_move), next(up_move)
    branch_all = pin(branch_all, branch_low)
    query_grad, pair_own, pair_send = attend_head_back(
        place, query, key, value, branch_all, w_out, spot, spots, cosine, sine, order.last
    )
    order.mark(query_grad)
    pair_other = moves.swap(pair_send)
    pair_other = pin(pair_other, pair_send)
    down_sum = next(down_move).T
    terms = jnp.stack([second_term, third_term, fourth_term])
    terms = narrow(jnp.pad(terms, ((0, pad - 3), (0, 0))).T)
    qkv_grad, qkv_term = qkv_back(
        normed, query_grad, pair_own, pair_other, pair_cosine, pair_sine, terms, order.last
    )
    order.mark(qkv_term)
    qkv_move = moves.scatter_halves(qkv_term.reshape(n_seq, width // n_seq, -1), pin)
    next(qkv_move)
    normed_part = normed_back(place, qkv_grad, columns, order.last)
    order.mark(normed_part)
    normed_grad = scatter(normed_part)

    output_term = weight_grad(mixed, branch_all, feats, order.last)
    order.mark(output_term)
    out_term = output_term.reshape(CORES, CORES, out_rows, width).transpose(1, 0, 2, 3)
    out_term = moves.exchange_cores(out_term).reshape(line, out_rows, width)
    next(qkv_move)
    gate_sum, up_sum = next(gate_move), next(up_move)
    out_move = moves.scatter_whole(pin(out_term), 2, pin)
    next(out_move)
    own_in = pin(narrow(next(qkv_move))).reshape(n_ctx, feat_rows, 2 * feats + pad)
    own_term = to_all(own_in)
    next(out_move)
    grad_output = moves.transpose_chips(pin(narrow(next(out_move))))
    normed_grad = pin(normed_grad)
    scale_one, unit_one = rms_parts(wide(tokens))
    input_grad, _ = rms_back(scale_one, unit_one, gain_one, wide(normed_grad))
    grad_tokens = pin(narrow(residual_grad + input_grad))
    own_term = pin(own_term, own_in)
    grad_query, grad_key, grad_value, grad_gains, grad_first = own_grads(
        own_term, (w_query, w_key, w_value), first_gain[:, None]
    )
    grad_output = wide(pin(grad_output))
    return (
        layer_out,
        grad_tokens,
        grad_query,
        grad_key,
        grad_value,
        grad_output,
        gate_sum,
        up_sum,
        down_sum,
        grad_first[:, 0],
        grad_gains[:, 0],
        grad_gains[:, 1],
        grad_gains[:, 2],
    )


def solution(mesh):
    placed = (
        P(("seq", "ctx"), None),
        P(("seq", "ctx"), None),
        P(("seq", "ctx"), None),
        P(("seq", "ctx"), None),
        P(("seq", "ctx"), None),
        P("seq", "ctx"),
        P("seq", "ctx"),
        P("ctx", "seq"),
        P(("seq", "ctx")),
        P(("seq", "ctx")),
        P(("seq", "ctx")),
        P(("seq", "ctx")),
        P(),
        P(("seq", "ctx"), None),
    )
    n_seq, n_ctx = mesh.shape["seq"], mesh.shape["ctx"]
    if n_ctx == QUERY_HEAD_COUNT and n_seq == 4:
        body = partial(head_body, n_seq=n_seq, n_ctx=n_ctx)
    else:
        body = context_body
    return jax.shard_map(
        body,
        mesh=mesh,
        in_specs=placed,
        out_specs=(
            P(("seq", "ctx"), None),
            P(("seq", "ctx"), None),
            P(("seq", "ctx"), None),
            P(("seq", "ctx"), None),
            P(("seq", "ctx"), None),
            P(("seq", "ctx"), None),
            P("seq", "ctx"),
            P("seq", "ctx"),
            P("ctx", "seq"),
            P(("seq", "ctx")),
            P(("seq", "ctx")),
            P(("seq", "ctx")),
            P(("seq", "ctx")),
        ),
        check_vma=False,
    )
```
